32 devices in a mesh: pipe: 2 (over core), dp: 16 (over z, y, x).
Axes of the slice: x: 2, y: 2, z: 4, core: 2. Of those that a mesh axis runs over, the one named last changes fastest.
Arguments:
- clips_in: bfloat16 [3, 6272, 2048], P(None, 'dp'), may hold values from -6 to 6
- cotangent: bfloat16 [3, 6272, 2048], P(None, 'dp'), may hold values from -6 to 6
- segment_ids: int32 [3, 16, 8], P(None, 'dp'), may hold values from 0 to 1, as said below
- w_in: float32 [2, 2048, 512], P('pipe', None, 'dp'), may hold values from -0.125 to 0.125
- w_squeeze: float32 [2, 512, 128], P('pipe', 'dp'), may hold values from -0.25 to 0.25
- w_near: float32 [2, 1152, 512], P('pipe', None, 'dp'), may hold values from -0.1875 to 0.1875
- w_far: float32 [2, 1152, 512], P('pipe', None, 'dp'), may hold values from -0.1875 to 0.1875
- w_mid: float32 [2, 4608, 512], P('pipe', None, 'dp'), may hold values from -0.09375 to 0.09375
- w_out: float32 [2, 512, 2048], P('pipe', None, 'dp'), may hold values from -0.25 to 0.25
- gain_mid: float32 [2, 2, 512], P('pipe', None, 'dp'), may hold values from 0.5 to 1.5
- bias_mid: float32 [2, 2, 512], P('pipe', None, 'dp'), may hold values from -0.5 to 0.5
- gain_out: float32 [2, 2048], P('pipe', 'dp'), may hold values from 0.5 to 1.5
- bias_out: float32 [2, 2048], P('pipe', 'dp'), may hold values from -0.5 to 0.5
Outputs:
- activations: bfloat16 [2, 3, 6272, 2048], P('pipe', None, 'dp')
- input_grads: bfloat16 [2, 3, 6272, 2048], P('pipe', None, 'dp')
- grad_w_in: float32 [2, 2048, 512], P('pipe', None, 'dp')
- grad_w_squeeze: float32 [2, 512, 128], P('pipe', 'dp')
- grad_w_near: float32 [2, 1152, 512], P('pipe', None, 'dp')
- grad_w_far: float32 [2, 1152, 512], P('pipe', None, 'dp')
- grad_w_mid: float32 [2, 4608, 512], P('pipe', None, 'dp')
- grad_w_out: float32 [2, 512, 2048], P('pipe', None, 'dp')
- grad_gain_mid: float32 [2, 2, 512], P('pipe', None, 'dp')
- grad_bias_mid: float32 [2, 2, 512], P('pipe', None, 'dp')
- grad_gain_out: float32 [2, 2048], P('pipe', 'dp')
- grad_bias_out: float32 [2, 2048], P('pipe', 'dp')
The draws below stay inside these ranges and needn't reach their ends.
Inputs may be any that keep to these rules, and one draw needn't show every extreme that they name: `segment_ids`: in every clip slot the ids are 0 on the first video's segments and 1 on the second's; each video has one segment or more.
All inputs are finite; a program needn't handle non-finite values.
Results may differ from the reference program's by a relative error of at most 0.023.
Values may be sent and summed in bfloat16 or wider, within the bound.
No kernel may reach another device: no remote copies, remote signals or barrier semaphores. Data moves between devices by JAX's collectives and lax.ppermute only.
A program may use at most 256 MiB of HBM per device.

```python
import jax
import jax.numpy as jnp
from jax import lax

C = 2048
MID = 512
RED = 128
SEG = 8
SIDE = 7
MB = 3
CLIPS = 16
ROWS = 6272
N_PIPE = 2


def draw_segment_ids(key, part):
    key = jax.random.fold_in(key, 11)
    split_at = jax.random.randint(key, (MB, CLIPS, 1), 1, SEG)
    return (jnp.arange(SEG)[None, None, :] >= split_at).astype(jnp.int32)


def block_levels(stream_key, shape, shards, low, high):
    factor_of, own = 1.0, jax.random.fold_in(stream_key, 6)
    for axis_at, parts in shards:
        steps = jnp.exp(jax.random.uniform(jax.random.fold_in(own, axis_at), (parts,), jnp.float32, low / len(shards), high / len(shards)))
        factor_of = factor_of * jnp.repeat(steps, shape[axis_at] // parts).reshape([-1 if axis == axis_at else 1 for axis in range(len(shape))])
    return factor_of


def scatter_about(key, dims, deviation, limit, cuts=(), dtype=jnp.bfloat16):
    array = jax.random.normal(key, dims, jnp.float32) * deviation
    if len(cuts) > 0:
        array = block_levels(key, dims, cuts, -0.22, 0.18) * array
    return jnp.clip(array, min=-limit, max=limit).astype(dtype)


def setup_inputs(seed: int = 0) -> dict:
    key_of = jax.random.split(jax.random.key(seed), 14)
    clips_in = scatter_about(key_of[0], (MB, ROWS, C), 1.0, 6.0, ((1, 16),))
    cotangent = scatter_about(key_of[1], (MB, ROWS, C), 1.0, 6.0, ((1, 16),))
    segment_ids = draw_segment_ids(jax.random.fold_in(key_of[13], 71), 0)
    w_in = scatter_about(key_of[3], (N_PIPE, C, MID), C ** -0.5, 0.125, ((0, 2), (2, 16)), jnp.float32)
    w_squeeze = scatter_about(key_of[4], (N_PIPE, MID, RED), MID ** -0.5, 0.25, ((0, 2), (1, 16)), jnp.float32)
    w_near = scatter_about(key_of[5], (N_PIPE, 9 * RED, MID), (9 * RED) ** -0.5, 0.1875, ((0, 2), (2, 16)), jnp.float32)
    w_far = scatter_about(key_of[6], (N_PIPE, 9 * RED, MID), (9 * RED) ** -0.5, 0.1875, ((0, 2), (2, 16)), jnp.float32)
    w_mid = scatter_about(key_of[7], (N_PIPE, 9 * MID, MID), (9 * MID) ** -0.5, 0.09375, ((0, 2), (2, 16)), jnp.float32)
    w_out = scatter_about(key_of[8], (N_PIPE, MID, C), MID ** -0.5, 0.25, ((0, 2), (2, 16)), jnp.float32)
    gain_mid = jnp.clip(0.5 + 1.0 * jax.random.uniform(key_of[9], (N_PIPE, 2, MID), jnp.float32) ** block_levels(key_of[9], (N_PIPE, 2, MID), ((0, 2), (2, 16)), -0.2, 0.2), 0.5, 1.5)
    bias_mid = jnp.clip(jax.random.uniform(key_of[10], (N_PIPE, 2, MID), jnp.float32, -0.5, 0.5) * block_levels(key_of[10], (N_PIPE, 2, MID), ((0, 2), (2, 16)), -0.4, 0.0), -0.5, 0.5)
    gain_out = jnp.clip(0.5 + 1.0 * jax.random.uniform(key_of[11], (N_PIPE, C), jnp.float32) ** block_levels(key_of[11], (N_PIPE, C), ((0, 2), (1, 16)), -0.2, 0.2), 0.5, 1.5)
    bias_out = jnp.clip(jax.random.uniform(key_of[12], (N_PIPE, C), jnp.float32, -0.5, 0.5) * block_levels(key_of[12], (N_PIPE, C), ((0, 2), (1, 16)), -0.4, 0.0), -0.5, 0.5)
    return dict(clips_in=clips_in, cotangent=cotangent, segment_ids=segment_ids, w_in=w_in, w_squeeze=w_squeeze, w_near=w_near, w_far=w_far, w_mid=w_mid, w_out=w_out, gain_mid=gain_mid, bias_mid=bias_mid, gain_out=gain_out, bias_out=bias_out)


epsilon = 1e-05

@jax.custom_vjp
def low(v):
    return lax.optimization_barrier(v.astype(jnp.bfloat16)).astype(jnp.float32)

@jax.custom_vjp
def low_back(v):
    return v

def low_keep(v):
    return (low(v), None)

def low_pass(kept, grad):
    return (grad,)

def back_keep(v):
    return (v, None)

def back_low(kept, grad):
    return (low(grad),)
low.defvjp(low_keep, low_pass)
low_back.defvjp(back_keep, back_low)

def matmul(left_side, right_side):
    return jnp.dot(left_side, right_side, precision=lax.Precision.HIGHEST, preferred_element_type=jnp.float32)

def patches(field_in, spread):
    channels = field_in.shape[-1]
    frames = field_in.reshape(-1, SIDE, SIDE, channels)
    padded = jnp.pad(frames, ((0, 0), (spread, spread), (spread, spread), (0, 0)))
    pieces = []
    for row_tap in range(3):
        for col_tap in range(3):
            pieces.append(padded[:, row_tap * spread:row_tap * spread + SIDE, col_tap * spread:col_tap * spread + SIDE, :])
    return jnp.concatenate(pieces, axis=-1).reshape(field_in.shape[0], 9 * channels)

def boundary(segment_ids):
    same_video = (segment_ids[..., 1:] == segment_ids[..., :-1]).astype(jnp.float32)
    closing = jnp.zeros(segment_ids.shape[:-1] + (1,), jnp.float32)
    return jnp.concatenate([same_video, closing], axis=-1)

def difference(field_in, row_mask):
    frames = field_in.reshape(row_mask.shape[0], SEG, SIDE * SIDE, field_in.shape[-1])
    shifted = jnp.concatenate([frames[:, 1:], jnp.zeros_like(frames[:, :1])], axis=1)
    return (row_mask[:, :, None, None] * (shifted - frames)).reshape(field_in.shape)

def normalize(values, gain_vec, bias_vec):
    centre = values - lax.optimization_barrier(jnp.mean(values, axis=0))
    spread = lax.optimization_barrier(jnp.mean(centre * centre, axis=0))
    return centre * lax.rsqrt(spread + epsilon) * gain_vec + bias_vec

def tdm_block(inputs, row_mask, params):
    w_in, w_squeeze, w_near, w_far, w_mid, w_out, gain_mid, bias_mid, gain_out, bias_out = params
    carried = low_back(inputs)
    first_act = low_back(matmul(low(carried), low(w_in)))
    hidden = jax.nn.silu(normalize(first_act, low(gain_mid[0]), low(bias_mid[0])))
    squeezed = low(low_back(matmul(low(difference(hidden, row_mask)), low(w_squeeze))))
    logits = low_back(matmul(patches(squeezed, 1), low(w_near)) + matmul(patches(squeezed, 2), low(w_far)))
    mixed_act = hidden * (0.5 + jax.nn.sigmoid(logits))
    second_act = low_back(matmul(patches(low(mixed_act), 1), low(w_mid)))
    middle = jax.nn.silu(normalize(second_act, low(gain_mid[1]), low(bias_mid[1])))
    third_act = low_back(matmul(low(middle), low(w_out)))
    return low(jax.nn.silu(carried + normalize(third_act, low(gain_out), low(bias_out))))

def reference(clips_in, cotangent, segment_ids, w_in, w_squeeze, w_near, w_far, w_mid, w_out, gain_mid, bias_mid, gain_out, bias_out):
    masters = (w_in, w_squeeze, w_near, w_far, w_mid, w_out, gain_mid, bias_mid, gain_out, bias_out)
    early_params = tuple((master[0] for master in masters))
    late_params = tuple((master[1] for master in masters))
    early_totals = tuple((jnp.zeros_like(master[0]) for master in masters))
    late_totals = tuple((jnp.zeros_like(master[1]) for master in masters))
    early_outs, late_outs, early_grads, late_grads = ([], [], [], [])
    for micro_batch in range(MB):
        row_mask = boundary(segment_ids[micro_batch])

        def section_fn(inputs, params):
            return tdm_block(inputs, row_mask, params)
        early_out, early_pull = jax.vjp(section_fn, clips_in[micro_batch].astype(jnp.float32), early_params)
        late_out, late_pull = jax.vjp(section_fn, early_out, late_params)
        grad_between, late_terms = late_pull(cotangent[micro_batch].astype(jnp.float32))
        grad_source, early_terms = early_pull(grad_between)
        early_totals = jax.tree.map(jnp.add, early_totals, early_terms)
        late_totals = jax.tree.map(jnp.add, late_totals, late_terms)
        early_outs.append(early_out)
        late_outs.append(late_out)
        early_grads.append(grad_source)
        late_grads.append(grad_between)
    activations = jnp.stack([jnp.stack(early_outs), jnp.stack(late_outs)]).astype(jnp.bfloat16)
    input_grads = jnp.stack([jnp.stack(early_grads), jnp.stack(late_grads)]).astype(jnp.bfloat16)
    stacked = tuple((jnp.stack([early_sum, late_sum]) for early_sum, late_sum in zip(early_totals, late_totals)))
    return (activations, input_grads, stacked[0], stacked[1], stacked[2], stacked[3], stacked[4], stacked[5], stacked[6], stacked[7], stacked[8], stacked[9])
```

```python
import functools

import jax
import jax.numpy as jnp
from jax import lax
from jax.experimental import pallas as pl
from jax.experimental.pallas import tpu as pltpu
from jax.sharding import PartitionSpec as P

SEG = 8
SIDE = 7
PIX = SIDE * SIDE
HALF = SEG // 2
STRIDE = HALF + 1
LINE = 16
ROWS = PIX * LINE
EPS = 1e-05
F32 = jnp.float32
BF16 = jnp.bfloat16
VMEM_BYTES = 40 * 1024 * 1024


def dot(left, right):
    return lax.dot_general(left, right, (((1,), (0,)), ((), ())), preferred_element_type=F32)


def dot_nt(left, right):
    return lax.dot_general(left, right, (((1,), (1,)), ((), ())), preferred_element_type=F32)


def dot_tn(left, right):
    return lax.dot_general(left, right, (((0,), (0,)), ((), ())), preferred_element_type=F32)


def sigmoid(v):
    return 0.5 * jnp.tanh(0.5 * v) + 0.5


def line_of(width):
    return lax.broadcasted_iota(jnp.int32, (LINE, width), 0)


def own_lines(width):
    r = line_of(width)
    inside = (r < 4) | ((r >= 5) & (r < 9)) | ((r >= 10) & (r < 14))
    return inside.astype(F32)


def per_line(values):
    width = values.shape[1]
    r = line_of(width)
    return jnp.where(r < 5, values[0:1], jnp.where(r < 10, values[1:2], values[2:3]))


def per_batch(lines, count):
    r = line_of(lines.shape[1])
    pieces = []
    for b in range(3):
        keep = (r >= 5 * b) & (r < 5 * b + count)
        pieces.append(jnp.sum(jnp.where(keep, lines, 0.0), axis=0, keepdims=True))
    return pieces


def flat(v):
    return v.reshape(-1, v.shape[-1])


def chunks(body, init=0):
    return lax.fori_loop(0, SIDE, body, init)


def ref_stats(a_ref, first, width):
    lanes = pl.ds(first, width)

    def add(i, s):
        return s + jnp.sum(a_ref[pl.ds(i * SIDE, SIDE), :, lanes], axis=0)

    sums = per_batch(chunks(add, jnp.zeros((LINE, width), F32)), HALF)
    means = [s / (HALF * PIX) for s in sums]
    mean_lines = per_line(jnp.concatenate(means, axis=0))

    def add_sq(i, s):
        d = a_ref[pl.ds(i * SIDE, SIDE), :, lanes] - mean_lines[None]
        return s + jnp.sum(d * d, axis=0)

    sq = per_batch(chunks(add_sq, jnp.zeros((LINE, width), F32)), HALF)
    zero = jnp.zeros((1, width), F32)
    return jnp.concatenate(means + [zero] + sq + [zero], axis=0)


def pack(st):
    cut = st.shape[1] * 3 // 4
    rest = [
        jnp.concatenate([st[r : r + 1, cut:] for r in rows], axis=1)
        for rows in ((0, 1, 2), (4, 5, 6))
    ]
    return jnp.concatenate([st[0:3, :cut], st[4:7, :cut]] + rest, axis=0)


def unpack(p, group):
    third = p.shape[1] // 3
    row = p[6 + group : 7 + group]
    rest = jnp.concatenate([row[:, third * k : third * (k + 1)] for k in range(3)], axis=0)
    return jnp.concatenate([p[3 * group : 3 * group + 3], rest], axis=1)


def spread(st, out_ref):
    packed = pack(st)
    for k in range(out_ref.shape[0]):
        out_ref[k] = packed


def merge_norm(gs, rows_each):
    count = sum(g.shape[0] for g in gs)
    total = sum(jnp.sum(g[...], axis=0) for g in gs)
    mean = total / count
    off = 0.0
    for g in gs:
        d = g[...] - mean[None]
        off = off + jnp.sum(d * d, axis=0)
    var = (unpack(total, 1) + rows_each * unpack(off, 0)) / (rows_each * count)
    return eight(unpack(mean, 0), var)


def merge_sums(gs, rows_each):
    total = sum(jnp.sum(g[...], axis=0) for g in gs)
    return eight(unpack(total, 0), unpack(total, 1))


def eight(first, second):
    zero = jnp.zeros((1, first.shape[1]), F32)
    return jnp.concatenate([first, zero, second, zero], axis=0)


def merge_wide(merge, place, g, g_other, out_ref):
    core = place[0]
    rows_each = float(2 * HALF * PIX)
    half = out_ref.shape[1] // 2
    out_ref[:, pl.ds(pl.multiple_of(core * half, half), half)] = merge([g], rows_each)
    out_ref[:, pl.ds(pl.multiple_of((1 - core) * half, half), half)] = merge([g_other], rows_each)


def split_wide(place, st, keep_ref, send_ref):
    core = place[0]
    half = st.shape[1] // 2
    keep_ref[...] = st[:, pl.ds(pl.multiple_of(core * half, half), half)]
    send_ref[...] = st[:, pl.ds(pl.multiple_of((1 - core) * half, half), half)]


def pair_kernel(norm, keep, recv, out_ref):
    a, b = keep[...], recv[...]
    if norm:
        d = a[0:3] - b[0:3]
        mean = 0.5 * (a[0:3] + b[0:3])
        st = eight(mean, a[4:7] + b[4:7] + (HALF * PIX / 2.0) * d * d)
    else:
        st = a + b
    spread(st, out_ref)


OWN_ROWS = float(HALF * PIX)


def gains_kernel(wt, place, *rest):
    refs, (gb_ref, gbo_ref, buf, sems) = rest[: wt.count], rest[wt.count :]
    wait_all(wt.copies("gain", place, refs, buf, sems))
    i = lax.broadcasted_iota(jnp.int32, (128, 512), 0)
    j = lax.broadcasted_iota(jnp.int32, (128, 512), 1)
    mid = jnp.zeros((16, 512), F32)
    for k in range(16):
        g = buf[k // 4, k // 2 % 2, k % 2, 0]
        hot = jnp.where((i < 32) & (j == 32 * k + i), 1.0, 0.0).astype(BF16)
        mid = mid + dot(g, hot)
        gbo_ref[:, 128 * k : 128 * k + 128] = g[4:12].astype(F32)
    gb_ref[...] = mid[0:8]


def wait_all(copies):
    for c in copies:
        c.wait()


class Weights:
    def __init__(self, kind, segments):
        self.kind, self.segments = kind, segments

    @property
    def count(self):
        return 2 if self.kind == "whole" else 8

    def sems(self, name):
        return len(self.segments[name]) * (2 if self.kind == "whole" else 4)

    def copies(self, name, place, refs, buf, sems):
        core, y, x = place[0], place[1], place[2]
        found = []
        for part, start, at, width in self.segments[name]:
            for side in range(2):
                c = core if side == 0 else 1 - core
                if self.kind == "whole":
                    pairs = [(refs[side], (ALL, ALL, ALL))]
                elif part == "P":
                    pairs = [(refs[4 * side], (ALL, y, ALL)), (refs[4 * side + 1], (ALL, 1 - y, ALL))]
                else:
                    pairs = [(refs[4 * side + 2], (ALL, ALL, x)), (refs[4 * side + 3], (ALL, ALL, 1 - x))]
                for ref, where in pairs:
                    source = ref.at[..., pl.ds(start, width)]
                    if isinstance(at, tuple):
                        target = buf.at[where + (c, at[0])]
                    else:
                        target = buf.at[where + (c, ALL, pl.ds(at, width))]
                    found.append(pltpu.make_async_copy(source, target, sems.at[len(found)]))
        for copy in found:
            copy.start()
        return found


ALL = slice(None)


def first_matmul(x_ref, w_buf, a_ref, stb_ref):
    for j in range(2):
        w = w_buf[2 * j : 2 * j + 2].reshape(256, 2048)
        a_ref[:, :, pl.ds(256 * j, 256)] = dot_nt(flat(x_ref[...]), w).reshape(PIX, LINE, 256)
    spread(ref_stats(a_ref, 0, 512), stb_ref)


def permute_kernel(core_ref, x_ref, out_ref):
    core = core_ref[0]
    i = lax.broadcasted_iota(jnp.int32, (ROWS, SEG * PIX), 0)
    j = lax.broadcasted_iota(jnp.int32, (ROWS, SEG * PIX), 1)
    pixel, line = i >> 4, i & 15
    hots = []
    for b in range(3):
        t = line - 5 * b
        target = (HALF * core + t) * PIX + pixel
        hots.append(jnp.where((t >= 0) & (t < HALF) & (j == target), 1.0, 0.0).astype(BF16))
    for k in range(4):
        lanes = pl.ds(512 * k, 512)
        total = dot(hots[0], x_ref[0, :, lanes])
        total = total + dot(hots[1], x_ref[1, :, lanes])
        total = total + dot(hots[2], x_ref[2, :, lanes])
        out_ref[:, :, lanes] = total.astype(BF16).reshape(PIX, LINE, 512)


def restore_kernel(place, early_ref, late_ref, early_in, late_in, out_ref, buf, sems):
    core = place[0]

    def fetch(mine, received):
        copies = [
            pltpu.make_async_copy(mine, buf.at[core], sems.at[0]),
            pltpu.make_async_copy(received, buf.at[1 - core], sems.at[1]),
        ]
        for c in copies:
            c.start()
        for c in copies:
            c.wait()

    @pl.when(core == 0)
    def _():
        fetch(early_ref, early_in)

    @pl.when(core == 1)
    def _():
        fetch(late_ref, late_in)

    def hot(first, count, side, b):
        j = lax.broadcasted_iota(jnp.int32, (count, ROWS), 0) + first
        i = lax.broadcasted_iota(jnp.int32, (count, ROWS), 1)
        seg = jnp.zeros_like(j)
        for k in range(1, SEG):
            seg = seg + jnp.where(j >= PIX * k, 1, 0)
        t = seg - HALF * side
        target = (j - PIX * seg) * LINE + 5 * b + t
        return jnp.where((t >= 0) & (t < HALF) & (i == target), 1.0, 0.0).astype(BF16)

    for b in range(3):
        lower, upper = hot(0, 208, 0, b), hot(192, 200, 1, b)
        for k in range(4):
            lanes = pl.ds(512 * k, 512)
            low = dot(lower, flat(buf[0, :, :, lanes])).astype(BF16)
            high = dot(upper, flat(buf[1, :, :, lanes])).astype(BF16)
            out_ref[b, 0:192, lanes] = low[:192]
            out_ref[b, 192:208, lanes] = low[192:] + high[:16]
            out_ref[b, 208:392, lanes] = high[16:]


def first_kernel(wt, place, x_ref, *rest):
    refs, (a_ref, st_ref, w_buf, sems) = rest[: wt.count], rest[wt.count :]
    copies = wt.copies("in", place, refs, w_buf, sems)
    wait_all(copies)
    first_matmul(x_ref, w_buf, a_ref, st_ref)


def tap_ranges(shift):
    return max(0, -shift), min(SIDE, SIDE - shift)


def build_patches(sq, patch):
    patch[...] = jnp.zeros(patch.shape, BF16)
    sq4 = sq.reshape(SIDE, SIDE, LINE, 128)
    for k in (1, 2):
        for tap in range(9):
            dy, dx = k * (tap // 3 - 1), k * (tap % 3 - 1)
            (y0, y1), (x0, x1) = tap_ranges(dy), tap_ranges(dx)
            col = ((k - 1) * 9 + tap) * 128
            patch[y0:y1, x0:x1, :, col : col + 128] = sq4[y0 + dy : y1 + dy, x0 + dx : x1 + dx]


def clear_border(pad):
    zero_row = jnp.zeros((9, LINE, 512), BF16)
    pad[0] = zero_row
    pad[8] = zero_row
    for y in range(1, 8):
        pad[y, 0] = jnp.zeros((LINE, 512), BF16)
        pad[y, 8] = jnp.zeros((LINE, 512), BF16)


def middle_kernel(wt, place, a_in, a_other, g, g_other, gb_ref, msk_ref, *rest):
    refs = rest[: wt.count]
    (
        a_ref, diff_ref, sq_ref, op_ref, mix_ref, second_ref, st_ref, mv_ref,
        sq_buf, nf_buf, mid_buf, hid, patch, sq_sems, nf_sems, mid_sems,
    ) = rest[wt.count :]
    core = place[0]
    sq_copies = wt.copies("sq", place, refs, sq_buf, sq_sems)
    nf_copies = wt.copies("nf", place, refs, nf_buf, nf_sems)
    mid_copies = wt.copies("mid", place, refs, mid_buf, mid_sems)
    clear_border(mix_ref)
    mv_ref[...] = merge_norm([g, g_other], OWN_ROWS)
    r = line_of(512)
    halo = ((r == 4) | (r == 9) | (r == 14)) & (core == 0)
    mean = per_line(mv_ref[0:3])
    scale = lax.rsqrt(per_line(mv_ref[4:7]) + EPS) * gb_ref[0:1]
    shift = gb_ref[1:2]
    m = msk_ref[:, 0:1]

    def hidden_chunk(i, _):
        rows = pl.ds(i * SIDE, SIDE)
        a = jnp.where(halo[None], pltpu.roll(a_other[rows], 4, 1), a_in[rows])
        a_ref[rows] = a
        n1 = (a - mean[None]) * scale[None] + shift[None]
        h = n1 * sigmoid(n1)
        hid[rows] = h
        diff_ref[rows] = (m[None] * (pltpu.roll(h, LINE - 1, 1) - h)).astype(BF16)
        return 0

    chunks(hidden_chunk)
    wait_all(sq_copies)
    sq = dot(flat(diff_ref[...]), sq_buf[...].reshape(512, 128)).astype(BF16)
    sq_ref[...] = sq.reshape(PIX, LINE, 128)
    build_patches(sq, patch)
    wait_all(nf_copies)
    for j in range(2):
        lanes = pl.ds(256 * j, 256)
        w = nf_buf[2 * j : 2 * j + 2].reshape(256, 2304)
        logits = dot_nt(patch[...].reshape(ROWS, 2304), w).reshape(PIX, LINE, 256)
        opening = sigmoid(logits)
        op_ref[:, :, lanes] = opening.astype(BF16)
        mixed = (hid[:, :, lanes] * (0.5 + opening)).astype(BF16)
        mix_ref[1:8, 1:8, :, lanes] = mixed.reshape(SIDE, SIDE, LINE, 256)
    wait_all(mid_copies)

    second_ref[...] = jnp.zeros(second_ref.shape, F32)

    def tap_step(tap, _):
        ty, tx = tap // 3, tap % 3
        v = mix_ref[pl.ds(ty, SIDE), pl.ds(tx, SIDE)].reshape(ROWS, 512)
        w = mid_buf[..., pl.ds(pl.multiple_of(tap * 512, 512), 512)].reshape(512, 512)
        second_ref[...] += dot_nt(v, w).reshape(PIX, LINE, 512)
        return 0

    lax.fori_loop(0, 9, tap_step, 0)
    spread(ref_stats(second_ref, 0, 512), st_ref)


def wide_kernel(wt, place, second, g, g_other, gb_ref, *rest):
    refs = rest[: wt.count]
    mid_ref, third_ref, keep_ref, send_ref, mv_ref, buf, st_ref, sems = rest[wt.count :]
    copies = wt.copies("out", place, refs, buf, sems)
    mv_ref[...] = merge_norm([g, g_other], OWN_ROWS)
    mean = per_line(mv_ref[0:3])
    scale = lax.rsqrt(per_line(mv_ref[4:7]) + EPS) * gb_ref[2:3]
    shift = gb_ref[3:4]

    def chunk(i, _):
        rows = pl.ds(i * SIDE, SIDE)
        n2 = (second[rows] - mean[None]) * scale[None] + shift[None]
        mid_ref[rows] = (n2 * sigmoid(n2)).astype(BF16)
        return 0

    chunks(chunk)
    wait_all(copies)

    def tile(j, _):
        w = buf[j].reshape(512, 512)
        lanes = pl.ds(pl.multiple_of(512 * j, 512), 512)
        third_ref[:, :, lanes] = dot_nt(flat(mid_ref[...]), w).reshape(PIX, LINE, 512)
        st_ref[:, lanes] = ref_stats(third_ref, pl.multiple_of(512 * j, 512), 512)
        return 0

    lax.fori_loop(0, 4, tile, 0)
    split_wide(place, st_ref, keep_ref, send_ref)


def finish(third, x_ref, mv_ref, gb_ref, each):
    own = own_lines(512)

    def tile(j, _):
        lanes = pl.ds(pl.multiple_of(512 * j, 512), 512)
        mean = per_line(mv_ref[0:3, lanes])
        inv = lax.rsqrt(per_line(mv_ref[4:7, lanes]) + EPS)
        gain, bias = gb_ref[0:1, lanes], gb_ref[1:2, lanes]

        def chunk(i, carry):
            rows = pl.ds(i * SIDE, SIDE)
            xhat = (third[rows, :, lanes] - mean[None]) * inv[None]
            z = x_ref[rows, :, lanes].astype(F32) + xhat * gain[None] + bias[None]
            sg = sigmoid(z)
            return each(rows, lanes, xhat, z, sg, own, carry)

        zero = jnp.zeros((LINE, 512), F32)
        s1, s2 = chunks(chunk, (zero, zero))
        each(None, lanes, None, None, None, None, (s1, s2))
        return 0

    lax.fori_loop(0, 4, tile, 0)


def sums_of(dh, dg):
    zero = jnp.zeros((1, dh.shape[1]), F32)
    return jnp.concatenate(per_batch(dh, STRIDE) + [zero] + per_batch(dg, STRIDE) + [zero], axis=0)


def turn_kernel(wt, place, third, x_ref, g, g_other, gb_ref, *rest):
    refs = rest[: wt.count]
    act_ref, xhat_ref, slope_ref, a_ref, st_ref, mv_ref, w_buf, sems = rest[wt.count :]
    copies = wt.copies("in", place, refs, w_buf, sems)
    merge_wide(merge_norm, place, g, g_other, mv_ref)

    def each(rows, lanes, xhat, z, sg, own, carry):
        if rows is None:
            return carry
        act_ref[rows, :, lanes] = (z * sg * own[None]).astype(BF16)
        xhat_ref[rows, :, lanes] = xhat.astype(BF16)
        slope_ref[rows, :, lanes] = (sg * (1.0 + z * (1.0 - sg)) * own[None]).astype(BF16)
        return carry

    finish(third, x_ref, mv_ref, gb_ref, each)
    wait_all(copies)
    first_matmul(act_ref, w_buf, a_ref, st_ref)


def top_kernel(
    place, third, x_ref, g, g_other, gb_ref, dy_ref,
    act_ref, xhat_ref, dz_ref, keep_ref, send_ref, mv_ref, sums_ref,
):
    merge_wide(merge_norm, place, g, g_other, mv_ref)

    def each(rows, lanes, xhat, z, sg, own, carry):
        if rows is None:
            sums_ref[:, lanes] = sums_of(*carry)
            return carry
        act_ref[rows, :, lanes] = (z * sg * own[None]).astype(BF16)
        xhat_ref[rows, :, lanes] = xhat.astype(BF16)
        dz = dy_ref[rows, :, lanes].astype(F32) * (sg * (1.0 + z * (1.0 - sg)) * own[None])
        dz_ref[rows, :, lanes] = dz.astype(BF16)
        return carry[0] + jnp.sum(dz, axis=0), carry[1] + jnp.sum(dz * xhat, axis=0)

    finish(third, x_ref, mv_ref, gb_ref, each)
    split_wide(place, sums_ref, keep_ref, send_ref)


class Shares:
    def __init__(self, kind, parts):
        self.kind, self.parts = kind, parts

    @property
    def count(self):
        return 2 if self.kind == "whole" else 4 * sum(1 for width in self.parts if width)

    def outs(self):
        if self.kind == "whole":
            width = sum(self.parts)
            return [((4, 2, 2, 16, width), BF16)] * 2
        return [((4, 2, 16, width), BF16) for width in self.parts if width for _ in range(4)]

    def store(self, place, refs, first, result, zs=ALL):
        core, y, x = place[0], place[1], place[2]
        width = result.shape[1]
        parts = result.astype(BF16).reshape(-1, 2, 2, 2, 16, width)
        lower, upper = parts[:, :, :, 0], parts[:, :, :, 1]
        sides = [jnp.where(core == 0, lower, upper), jnp.where(core == 0, upper, lower)]
        if self.kind == "whole":
            for ref, v in zip(refs, sides):
                ref[zs, :, :, :, pl.ds(first, width)] = v
            return
        is_p = first < self.parts[0]
        start = first if is_p else first - self.parts[0]
        lanes = pl.ds(start, width)
        refs = refs[:4] if is_p else refs[-4:]
        for k, v in enumerate(sides):
            if is_p:
                two, at = (v[:, 0], v[:, 1]), y
            else:
                two, at = (v[:, :, 0], v[:, :, 1]), x
            refs[2 * k][zs, :, :, lanes] = jnp.where(at == 0, two[0], two[1])
            refs[2 * k + 1][zs, :, :, lanes] = jnp.where(at == 0, two[1], two[0])


def wide_back_kernel(
    rows_total, wt, place, dz, xhat, mv3_ref, g, g_other, gbo_ref, second, mv2_ref, gb_ref, *rest
):
    refs, (dn2_ref, stb_ref, d3, s3_ref, buf, sems) = rest[: wt.count], rest[wt.count :]
    copies = wt.copies("out", place, refs, buf, sems)
    merge_wide(merge_sums, place, g, g_other, s3_ref)
    own = own_lines(512)

    def tile(j, _):
        lanes = pl.ds(pl.multiple_of(512 * j, 512), 512)
        k = lax.rsqrt(per_line(mv3_ref[4:7, lanes]) + EPS) * gbo_ref[0:1, lanes] * own
        dh = per_line(s3_ref[0:3, lanes]) / rows_total
        dg = per_line(s3_ref[4:7, lanes]) / rows_total

        def chunk(i, c):
            rows = pl.ds(i * SIDE, SIDE)
            v = dz[rows, :, lanes].astype(F32) - dh[None] - xhat[rows, :, lanes].astype(F32) * dg[None]
            d3[rows, :, lanes] = (k[None] * v).astype(BF16)
            return c

        return chunks(chunk, 0)

    lax.fori_loop(0, 4, tile, 0)
    wait_all(copies)
    dn2_ref[...] = jnp.zeros(dn2_ref.shape, F32)

    def product(j, _):
        lanes = pl.ds(pl.multiple_of(512 * j, 512), 512)
        w = buf[j].reshape(512, 512)
        dn2_ref[...] += dot(flat(d3[:, :, lanes]), w).reshape(PIX, LINE, 512)
        return 0

    lax.fori_loop(0, 4, product, 0)
    mean = per_line(mv2_ref[0:3])
    inv = lax.rsqrt(per_line(mv2_ref[4:7]) + EPS)
    gain, bias = gb_ref[2:3], gb_ref[3:4]

    def chunk(i, carry):
        rows = pl.ds(i * SIDE, SIDE)
        xh = (second[rows] - mean[None]) * inv[None]
        n2 = xh * gain[None] + bias[None]
        sg = sigmoid(n2)
        dn = dn2_ref[rows] * (sg * (1.0 + n2 * (1.0 - sg)))
        dn2_ref[rows] = dn
        return carry[0] + jnp.sum(dn, axis=0), carry[1] + jnp.sum(dn * xh, axis=0)

    zero = jnp.zeros((LINE, 512), F32)
    spread(sums_of(*chunks(chunk, (zero, zero))), stb_ref)


def wide_grad(sh, place, refs, start, d3, mid):
    for j in range(4):
        v = flat(d3[:, :, pl.ds(512 * j, 512)])
        res = dot_tn(v, flat(mid[...])).reshape(2, 2, 2, 4, 16, 512)
        for g in range(4):
            sh.store(place, refs, start + 512 * g, res[:, :, :, g].reshape(128, 512), slice(j, j + 1))


def middle_grad(sh, place, refs, start, d2, mixp):
    for tap in range(9):
        mixed = mixp[tap // 3 : tap // 3 + SIDE, tap % 3 : tap % 3 + SIDE].reshape(ROWS, 512)
        sh.store(place, refs, start + 512 * tap, dot_tn(flat(d2[...]), mixed))


def branch_grad(sh, place, refs, start, dlog, sq_ref, diff, dsq, patch):
    build_patches(flat(sq_ref[...]), patch)
    for j in range(3):
        pv = patch[:, :, :, pl.ds(768 * j, 768)].reshape(ROWS, 768)
        sh.store(place, refs, start + 128 + 768 * j, dot_tn(flat(dlog[...]), pv))
    sh.store(place, refs, start, dot_tn(flat(diff[...]), flat(dsq[...])))


def wide_grad_kernel(sh, place, d3, mid, *refs):
    wide_grad(sh, place, refs, 0, d3, mid)


def branch_grad_kernel(sh, place, dlog, sq_ref, diff, dsq, *rest):
    branch_grad(sh, place, rest[: sh.count], 0, dlog, sq_ref, diff, dsq, rest[sh.count])


def all_grad_kernel(sh, place, d3, mid, d2, mixp, dlog, sq_ref, diff, dsq, *rest):
    refs = rest[: sh.count]
    branch_grad(sh, place, refs, 0, dlog, sq_ref, diff, dsq, rest[sh.count])
    middle_grad(sh, place, refs, 2432, d2, mixp)
    wide_grad(sh, place, refs, 7040, d3, mid)


def second_back_kernel(rows_total, sh, place, dn2, second, mv2_ref, g, g_other, gb_ref, *rest):
    if sh is not None:
        mixp, refs, (d2, s2_ref) = rest[0], rest[1 : 1 + sh.count], rest[1 + sh.count :]
    else:
        d2, s2_ref = rest
    s2_ref[...] = merge_sums([g, g_other], OWN_ROWS)
    own = own_lines(512)
    mean2 = per_line(mv2_ref[0:3])
    inv2 = lax.rsqrt(per_line(mv2_ref[4:7]) + EPS)
    k2 = inv2 * gb_ref[2:3] * own
    dh2 = per_line(s2_ref[0:3]) / rows_total
    dg2 = per_line(s2_ref[4:7]) / rows_total

    def chunk(i, c):
        rows = pl.ds(i * SIDE, SIDE)
        xh = (second[rows] - mean2[None]) * inv2[None]
        d2[rows] = (k2[None] * (dn2[rows] - dh2[None] - xh * dg2[None])).astype(BF16)
        return c

    chunks(chunk)
    if sh is not None:
        middle_grad(sh, place, refs, 0, d2, mixp)


def middle_back_kernel(wt, place, d2, a_ref, mv1_ref, gb_ref, msk_ref, op_ref, *rest):
    refs = rest[: wt.count]
    (
        dn1_ref, stb_ref, dlog, dsq_ref,
        sq_buf, nf_buf, mid_buf, d2p, dmix, dsq, sq_sems, nf_sems, mid_sems,
    ) = rest[wt.count :]
    mid_copies = wt.copies("mid", place, refs, mid_buf, mid_sems)
    nf_copies = wt.copies("nf", place, refs, nf_buf, nf_sems)
    sq_copies = wt.copies("sq", place, refs, sq_buf, sq_sems)
    clear_border(d2p)
    for y in range(SIDE):
        d2p[y + 1, 1:8] = d2[SIDE * y : SIDE * y + SIDE]
    wait_all(mid_copies)
    dmix[...] = jnp.zeros(dmix.shape, F32)

    def tap_step(tap, _):
        ty, tx = tap // 3, tap % 3
        v = d2p[pl.ds(2 - ty, SIDE), pl.ds(2 - tx, SIDE)].reshape(ROWS, 512)
        w = mid_buf[..., pl.ds(pl.multiple_of(tap * 512, 512), 512)].reshape(512, 512)
        dmix[...] += dot(v, w).reshape(PIX, LINE, 512)
        return 0

    lax.fori_loop(0, 9, tap_step, 0)
    mean1 = per_line(mv1_ref[0:3])
    inv1 = lax.rsqrt(per_line(mv1_ref[4:7]) + EPS)
    gain1, bias1 = gb_ref[0:1], gb_ref[1:2]

    def log_chunk(i, c):
        rows = pl.ds(i * SIDE, SIDE)
        n1 = (a_ref[rows] - mean1[None]) * inv1[None] * gain1[None] + bias1[None]
        h = n1 * sigmoid(n1)
        op = op_ref[rows].astype(F32)
        dlog[rows] = (dmix[rows] * h * op * (1.0 - op)).astype(BF16)
        return c

    chunks(log_chunk)
    wait_all(nf_copies)
    dsq[...] = jnp.zeros(dsq.shape, F32)
    for k in (1, 2):
        for ty in range(3):
            w = nf_buf[..., pl.ds(((k - 1) * 9 + ty * 3) * 128, 384)].reshape(512, 384)
            res = dot(flat(dlog[...]), w).reshape(SIDE, SIDE, LINE, 384)
            for tx in range(3):
                dy, dx = k * (ty - 1), k * (tx - 1)
                (y0, y1), (x0, x1) = tap_ranges(dy), tap_ranges(dx)
                dsq[y0 + dy : y1 + dy, x0 + dx : x1 + dx] += res[
                    y0:y1, x0:x1, :, 128 * tx : 128 * tx + 128
                ]
    dsq_low = dsq[...].astype(BF16).reshape(ROWS, 128)
    dsq_ref[...] = dsq_low.reshape(PIX, LINE, 128)
    wait_all(sq_copies)
    dn1_ref[...] = dot_nt(dsq_low, sq_buf[...].reshape(512, 128)).reshape(PIX, LINE, 512)
    m = msk_ref[:, 0:1]

    def last_chunk(i, carry):
        rows = pl.ds(i * SIDE, SIDE)
        xh = (a_ref[rows] - mean1[None]) * inv1[None]
        n1 = xh * gain1[None] + bias1[None]
        sg = sigmoid(n1)
        e = dn1_ref[rows] * m[None]
        op = op_ref[rows].astype(F32)
        dhid = dmix[rows] * (0.5 + op) - e + pltpu.roll(e, 1, 1)
        dn = dhid * (sg * (1.0 + n1 * (1.0 - sg)))
        dn1_ref[rows] = dn
        return carry[0] + jnp.sum(dn, axis=0), carry[1] + jnp.sum(dn * xh, axis=0)

    zero = jnp.zeros((LINE, 512), F32)
    spread(sums_of(*chunks(last_chunk, (zero, zero))), stb_ref)


def first_d1(rows_total, place, dn1, dn1_other, a_ref, mv1_ref, s1_ref, gb_ref, d1):
    own = own_lines(512)
    r = line_of(512)
    first = ((r == 0) | (r == 5) | (r == 10)) & (place[0] == 1)
    mean = per_line(mv1_ref[0:3])
    inv = lax.rsqrt(per_line(mv1_ref[4:7]) + EPS)
    k = inv * gb_ref[0:1] * own
    dh = per_line(s1_ref[0:3]) / rows_total
    dg = per_line(s1_ref[4:7]) / rows_total

    def chunk(i, c):
        rows = pl.ds(i * SIDE, SIDE)
        xh = (a_ref[rows] - mean[None]) * inv[None]
        dn = dn1[rows] + jnp.where(first[None], pltpu.roll(dn1_other[rows], LINE - 4, 1), 0.0)
        d1[rows] = (k[None] * (dn - dh[None] - xh * dg[None])).astype(BF16)
        return c

    chunks(chunk)


def first_back_kernel(
    rows_total, wt, place, dn1, dn1_other, a_ref, mv1_ref, g, g_other, gb_ref, dz, slope, xhat, *rest
):
    refs, rest = rest[: wt.count], rest[wt.count :]
    dx_ref, d1, s1_ref, dz_ref, keep_ref, send_ref, w_buf, sums_ref, sems = rest
    copies = wt.copies("in", place, refs, w_buf, sems)
    s1_ref[...] = merge_sums([g, g_other], OWN_ROWS)
    first_d1(rows_total, place, dn1, dn1_other, a_ref, mv1_ref, s1_ref, gb_ref, d1)
    wait_all(copies)

    def tile(j, _):
        lanes = pl.ds(pl.multiple_of(512 * j, 512), 512)
        w = w_buf[..., lanes].reshape(512, 512)
        dx = dot(flat(d1[...]), w).reshape(PIX, LINE, 512) + dz[:, :, lanes].astype(F32)
        dx_low = dx.astype(BF16)
        dx_ref[:, :, lanes] = dx_low
        d = dx_low.astype(F32) * slope[:, :, lanes].astype(F32)
        dz_ref[:, :, lanes] = d.astype(BF16)
        sums_ref[:, lanes] = sums_of(
            jnp.sum(d, axis=0), jnp.sum(d * xhat[:, :, lanes].astype(F32), axis=0)
        )
        return 0

    lax.fori_loop(0, 4, tile, 0)
    split_wide(place, sums_ref, keep_ref, send_ref)


def first_grad(sh, place, refs, d1, x_ref):
    for j in range(4):
        x = flat(x_ref[:, :, pl.ds(512 * j, 512)])
        sh.store(place, refs, 512 * j, dot_tn(flat(d1[...]), x))


def first_grad_kernel(sh, place, d1, x_ref, *refs):
    first_grad(sh, place, refs, d1, x_ref)


def last_grad_kernel(
    rows_total, sh, place, dn1, dn1_other, a_ref, mv1_ref, g, g_other, gb_ref, x_ref, *rest
):
    refs, (d1, s1_ref) = rest[: sh.count], rest[sh.count :]
    s1_ref[...] = merge_sums([g, g_other], OWN_ROWS)
    first_d1(rows_total, place, dn1, dn1_other, a_ref, mv1_ref, s1_ref, gb_ref, d1)
    first_grad(sh, place, refs, d1, x_ref)


def last_back_kernel(wt, place, d1, dz, *rest):
    refs, (dx_ref, w_buf, sems) = rest[: wt.count], rest[wt.count :]
    wait_all(wt.copies("in", place, refs, w_buf, sems))

    def tile(j, _):
        lanes = pl.ds(pl.multiple_of(512 * j, 512), 512)
        w = w_buf[..., lanes].reshape(512, 512)
        dx = dot(flat(d1[...]), w).reshape(PIX, LINE, 512) + dz[:, :, lanes].astype(F32)
        dx_ref[:, :, lanes] = dx.astype(BF16)
        return 0

    lax.fori_loop(0, 4, tile, 0)


VM = pl.BlockSpec(memory_space=pltpu.VMEM)
HB = pl.BlockSpec(memory_space=pltpu.HBM)
SM = pl.BlockSpec(memory_space=pltpu.SMEM)


def call(kernel, specs, outs, scratch=(), us=5):
    return pl.pallas_call(
        kernel,
        in_specs=specs,
        out_specs=tuple(VM for _ in outs),
        out_shape=tuple(jax.ShapeDtypeStruct(s, d) for s, d in outs),
        scratch_shapes=list(scratch),
        compiler_params=pltpu.CompilerParams(vmem_limit_bytes=VMEM_BYTES),
        cost_estimate=pl.CostEstimate(flops=us * 10**9, bytes_accessed=us * 3 * 10**6, transcendentals=0),
    )


def pm(width, dtype):
    return ((PIX, LINE, width), dtype)


def wbuf(width):
    return pltpu.VMEM((4, 2, 2, 2, 16, width), BF16)


STAT = ((8, 512), F32)
WIDE_STAT = ((8, 2048), F32)
PAIR = [(0, 1), (1, 0)]


class Links:
    def __init__(self, dp, core):
        self.dp, self.core = dp, core
        self.at = lax.axis_index("dp")

    def bit(self, k):
        return (self.at // k) % 2

    def place(self):
        y, x = (self.bit(2), self.bit(1)) if self.split else (0, 0)
        return jnp.stack([self.core, jnp.int32(y), jnp.int32(x)]).astype(jnp.int32)

    split = True

    def swap(self, v):
        return lax.ppermute(v, "pipe", PAIR)

    def across(self, v, k):
        return lax.ppermute(v, "dp", [(i, i ^ k) for i in range(self.dp)])

    def to_all(self, spread, *meanwhile):
        g = lax.all_to_all(spread, "dp", 0, 0)
        if meanwhile:
            g = after(g, *meanwhile)
        return g, self.swap(g)

    def by_core(self, own, other):
        first = self.core == 0
        return jnp.where(first, own, other), jnp.where(first, other, own)

    def in_order(self, which, own, other, axis):
        pair = jnp.where(which == 0, jnp.stack([own, other], axis), jnp.stack([other, own], axis))
        return pair

    def halves(self, piece):
        two = piece.reshape(2, 16, piece.shape[1])
        keep = lax.dynamic_index_in_dim(two, self.core, 0, keepdims=False)
        recv = self.swap(lax.dynamic_index_in_dim(two, 1 - self.core, 0, keepdims=False))
        return self.by_core(keep, recv)

    def gather_z(self, own):
        v = self.in_order(self.bit(8), own, self.across(own, 8), 0)
        v = self.in_order(self.bit(4), v, self.across(v, 4), 1)
        return v.reshape(4, 16, -1)

    def gather_xy(self, v, cut, *then):
        p, q = v[..., :cut], v[..., cut:]
        p_other, q_other = self.across(p, 1), self.across(q, 2)
        if then:
            p_other, q_other = after((p_other, q_other), *then)
        p = self.in_order(self.bit(1), p, p_other, 1)
        q = self.in_order(self.bit(2), q, q_other, 1)
        mine = (p, self.across(p, 2), q, self.across(q, 1))
        return mine + tuple(self.swap(v) for v in mine)

    def gather_split(self, own, cut):
        return self.gather_xy(self.gather_z(own), cut)

    def gather_whole(self, own):
        return lax.all_gather(own, "dp").reshape(4, 2, 2, 16, -1)

    def gather_blocks(self, gains, inner, rest, wide):
        rows = jnp.concatenate([jnp.pad(v, ((0, 0), (0, 128 - v.shape[1]))) for v in gains], axis=0)
        tail = jnp.pad(rows, ((0, 32 - rows.shape[0]), (0, 0)))
        a = self.halves(jnp.concatenate([inner, tail], axis=1))
        b, c = self.halves(rest), self.halves(self.narrow_rows(wide))
        b0 = self.gather_whole(b[0])
        a0 = self.gather_split(a[0], 1024)
        ca = self.gather_z(after(jnp.concatenate([c[0], a[1]], axis=1), a0))
        block_0 = {
            "A": (Weights("split", SPLIT_A), a0),
        }
        return block_0, (ca, b0, jnp.concatenate([c[1], b[1]], axis=1))

    def gather_middle(self, blocks, then):
        block_0, (ca, b0, bc) = blocks
        b0 = after(b0, then)
        block_0["B"] = (Weights("whole", middle_at(0)), (b0, self.swap(b0)))
        return block_0, (ca, self.gather_whole(after(bc, b0)))

    def gather_next(self, blocks, second):
        block_0, (ca, bc) = blocks
        ca = self.gather_xy(ca, 2048, second)
        block_0["C"] = (Weights("split", SPLIT_C), ca)
        return block_0, (ca, bc)

    def gather_last(self, blocks, third):
        block_0, (ca, bc) = blocks
        bc = after(bc, third)
        bc = (bc, self.swap(bc))
        return block_0, {
            "A": (Weights("split", SPLIT_A1), ca),
            "B": (Weights("whole", middle_at(2048)), bc),
            "C": (Weights("whole", wide_at(0)), bc),
        }

    def gains_of(self, group, place):
        wt, refs = group
        return call(
            functools.partial(gains_kernel, wt), [SM] + [HB] * len(refs), [STAT, WIDE_STAT],
            [wbuf(128), pltpu.SemaphoreType.DMA((wt.sems("gain"),))],
        )(place, *refs)

    def add(self, a, b):
        return (a.astype(F32) + b.astype(F32)).astype(BF16)

    def halve(self, v, axis, k, then=None):
        which = self.bit(k)
        keep = lax.dynamic_index_in_dim(v, which, axis, keepdims=False)
        send = lax.dynamic_index_in_dim(v, 1 - which, axis, keepdims=False)
        moved = self.across(send, k)
        if then is not None:
            moved = after(moved, then)
        return self.add(keep, moved)

    def scatter_split(self, g, then=(None,) * 4):
        done = []
        for own, other, send_own, send_other, k in ((*g[:4], 2), (*g[4:], 1)):
            other = self.add(other, self.swap(send_other))
            moved = self.across(other, k)
            if then[0] is not None:
                moved = after(moved, then[0])
            v = self.add(self.add(own, self.swap(send_own)), moved)
            done.append(self.halve(v, 1, 3 - k, then[1]))
        v = jnp.concatenate(done, axis=-1)
        v = self.halve(v.reshape(2, 2, 16, -1), 1, 4, then[2])
        return self.halve(v, 0, 8, then[3])

    def half_sums(self, keep, send):
        return self.add(keep, self.swap(send)).reshape(16, 16, -1)

    def scatter_whole(self, v):
        return lax.psum_scatter(v, "dp", scatter_dimension=0, tiled=True)[0]

    def to_owner(self, early, late):
        early_other = lax.ppermute(early, "pipe", [(1, 0)])
        late_other = lax.ppermute(late, "pipe", [(0, 1)])
        at_0 = jnp.concatenate([early, early_other], axis=0)
        at_1 = jnp.concatenate([late_other, late], axis=0)
        return jnp.where(self.core == 0, at_0, at_1).astype(F32)

    def wide_rows(self, v):
        return v.reshape(2, 16, 4, -1).transpose(0, 2, 1, 3).reshape(128, -1)

    def narrow_rows(self, v):
        return v.reshape(2, 4, 16, -1).transpose(0, 2, 1, 3).reshape(32, -1)


class AnyLinks(Links):
    split = False

    def gather_blocks(self, gains, inner, rest, wide):
        full = [lax.all_gather(v, "dp", tiled=True) for v in (inner, wide, rest)]
        full[1] = jnp.stack([self.narrow_rows(f) for f in full[1].reshape(16, 128, -1)]).reshape(512, -1)
        own = jnp.concatenate(full, axis=1)
        vectors = [lax.all_gather(v, "dp", axis=1, tiled=True).astype(F32) for v in gains]
        mid = jnp.pad(jnp.concatenate(vectors[:4]), ((0, 4), (0, 0)))
        out = jnp.pad(jnp.concatenate(vectors[4:]), ((0, 6), (0, 0)))
        mids, outs = self.by_core(mid, self.swap(mid)), self.by_core(out, self.swap(out))
        blocks = []
        for s, full in enumerate(self.by_core(own, self.swap(own))):
            parts = full.reshape(16, 2, 16, -1)
            mine = lax.dynamic_index_in_dim(parts, self.core, 1, keepdims=False)
            theirs = lax.dynamic_index_in_dim(parts, 1 - self.core, 1, keepdims=False)
            refs = tuple(v.reshape(4, 2, 2, 16, -1) for v in (mine, theirs))
            groups = (("A", {"in": [("W", 0, 0, 2048)]}), ("B", middle_at(4096)), ("C", wide_at(2048)))
            blocks.append({k: (Weights("whole", v), refs) for k, v in groups})
            blocks[s]["gains"] = (mids[s], outs[s])
        return blocks

    def gather_middle(self, blocks, then):
        return blocks

    def gather_next(self, blocks, second):
        return blocks

    def gather_last(self, blocks, third):
        return blocks

    def gains_of(self, group, place):
        return group

    def scatter_pairs(self, early, late, wide):
        full = []
        for keep, send in (early, late):
            half = self.add(keep, self.swap(send)).reshape(16, 16, -1)
            full.append(jnp.stack(self.by_core(half, self.swap(half)), axis=1))
        total = jnp.where(self.core == 0, full[0], full[1])
        if wide:
            total = jnp.stack([self.wide_rows(v.reshape(32, -1)) for v in total])
        total = total.reshape(-1, total.shape[-1])
        return lax.psum_scatter(total, "dp", scatter_dimension=0, tiled=True).astype(F32)


def after(v, *others):
    return lax.optimization_barrier((v, others))[0]


SPLIT_A = {"in": [("P", 0, 0, 1024), ("Q", 0, 1024, 1024)], "gain": [("Q", 1024, 0, 128)]}
SPLIT_C = {"out": [("P", 512 * g, (g,), 512) for g in range(4)]}
SPLIT_A1 = {"in": [("Q", 0, 0, 2048)], "gain": [("Q", 2048, 0, 128)]}


def middle_at(first):
    return {
        "sq": [("W", first, 0, 128)],
        "nf": [("W", first + 128, 0, 2304)],
        "mid": [("W", first + 2432, 0, 4608)],
    }


def wide_at(first):
    return {"out": [("W", first + 512 * g, (g,), 512) for g in range(4)]}


def local(
    clips_in, cotangent, segment_ids, w_in, w_squeeze, w_near, w_far, w_mid, w_out,
    gain_mid, bias_mid, gain_out, bias_out,
):
    dp = lax.axis_size("dp")
    core = lax.axis_index("pipe")
    links = (Links if dp == 16 else AnyLinks)(dp, core)
    place = links.place()
    rows_total = float(clips_in.shape[1] * dp)

    def low(v):
        return v[0].astype(BF16)

    n = w_in.shape[2]
    gain_rows = [low(gain_mid)[0:1], low(bias_mid)[0:1], low(gain_mid)[1:2], low(bias_mid)[1:2]]
    gathered = links.gather_blocks(
        gain_rows + [low(gain_out)[None], low(bias_out)[None]],
        low(w_in).T,
        jnp.concatenate([low(w_squeeze), low(w_near).T, low(w_far).T, low(w_mid).T], axis=1),
        low(w_out).T,
    )

    def gains_of(s):
        return links.gains_of(gathered[s]["A" if links.split else "gains"], place)

    gains = [gains_of(0)]

    same = (segment_ids[:, 0, 1:] == segment_ids[:, 0, :-1]).astype(F32)
    same = jnp.concatenate([same, jnp.zeros((3, 1), F32)], axis=1)
    mine_seg = lax.dynamic_slice_in_dim(same, core * HALF, HALF, 1)
    msk = jnp.concatenate([mine_seg, jnp.zeros((3, 1), F32)], axis=1).reshape(15)
    msk = jnp.broadcast_to(jnp.concatenate([msk, jnp.zeros((1,), F32)])[:, None], (LINE, 128))

    permute = call(permute_kernel, [SM, VM], [pm(2048, BF16)])
    x0 = permute(place, clips_in)[0]
    dy = permute(place, cotangent)[0]

    dma = pltpu.SemaphoreType.DMA
    wide_buf = pltpu.VMEM((4, 2, 2, 2, 4, 16, 512), BF16)

    stb = ((dp, 8, 384), F32)
    half_stat = ((8, 1024), F32)
    buffers = {"in": wbuf(2048), "sq": wbuf(128), "nf": wbuf(2304), "mid": wbuf(4608), "out": wide_buf}
    groups = {"A": ("in",), "B": ("sq", "nf", "mid"), "C": ("out",)}

    def kernel(body, group, values, outs, scratch, *static):
        wt, refs = group[1]
        names = groups[group[0]]
        return call(
            functools.partial(body, *static, wt),
            [SM] + [VM] * len(values) + [HB] * len(refs),
            outs,
            [buffers[k] for k in names] + scratch + [dma((wt.sems(k),)) for k in names],
        )(place, *values, *refs)

    def group(s, k):
        return k, gathered[s][k]

    def first(s, x):
        return kernel(first_kernel, group(s, "A"), [x], [pm(512, F32), stb], [])

    def middle(s, *values):
        outs = [pm(512, F32), pm(512, BF16), pm(128, BF16), pm(512, BF16),
                ((9, 9, LINE, 512), BF16), pm(512, F32), stb, STAT]
        scratch = [pltpu.VMEM((PIX, LINE, 512), F32), pltpu.VMEM((SIDE, SIDE, LINE, 2304), BF16)]
        return kernel(middle_kernel, group(s, "B"), list(values), outs, scratch)

    def widen(s, *values):
        outs = [pm(512, BF16), pm(2048, F32), half_stat, half_stat, STAT]
        return kernel(wide_kernel, group(s, "C"), list(values), outs, [pltpu.VMEM((8, 2048), F32)])

    def turn(*values):
        outs = [pm(2048, BF16)] * 3 + [pm(512, F32), stb, WIDE_STAT]
        return kernel(turn_kernel, group(1, "A"), list(values), outs, [])

    top = call(
        top_kernel, [SM] + [VM] * 6, [pm(2048, BF16)] * 3 + [half_stat, half_stat, WIDE_STAT],
        [pltpu.VMEM((8, 2048), F32)],
    )

    def pairs(norm, keep, send, *meanwhile):
        recv = links.swap(send)
        v = call(functools.partial(pair_kernel, norm), [VM, VM], [((dp, 8, 768), F32)])(keep, recv)
        return links.to_all(v[0], *meanwhile)

    def wide_back(s, *values):
        outs = [pm(512, F32), stb, pm(2048, BF16), WIDE_STAT]
        return kernel(wide_back_kernel, group(s, "C"), list(values), outs, [], rows_total)

    def second_back(sh, *values):
        outs = [pm(512, BF16), STAT]
        return call(
            functools.partial(second_back_kernel, rows_total, sh), [SM] + [VM] * len(values),
            (sh.outs() if sh else []) + outs,
        )(place, *values)

    def middle_back(s, *values):
        outs = [pm(512, F32), stb, pm(512, BF16), pm(128, BF16)]
        scratch = [pltpu.VMEM((9, 9, LINE, 512), BF16), pltpu.VMEM((PIX, LINE, 512), F32),
                   pltpu.VMEM((SIDE, SIDE, LINE, 128), F32)]
        return kernel(middle_back_kernel, group(s, "B"), list(values), outs, scratch)

    def first_back(*values):
        outs = [pm(2048, BF16), pm(512, BF16), STAT, pm(2048, BF16), half_stat, half_stat]
        scratch = [pltpu.VMEM((8, 2048), F32)]
        return kernel(first_back_kernel, group(1, "A"), list(values), outs, scratch, rows_total)

    def last_grad(sh, *values):
        return call(
            functools.partial(last_grad_kernel, rows_total, sh), [SM] + [VM] * len(values),
            sh.outs() + [pm(512, BF16), STAT],
        )(place, *values)

    def last_back(*values):
        return kernel(last_back_kernel, group(0, "A"), list(values), [pm(2048, BF16)], [])[0]

    def shares_of(kind, *parts):
        return Shares(kind if links.split else "whole", parts)

    def grad(body, sh, values, scratch=()):
        return call(
            functools.partial(body, sh), [SM] + [VM] * len(values), sh.outs(), scratch
        )(place, *values)

    restore = call(
        restore_kernel, [SM, HB, HB, HB, HB], [((3, SEG * PIX, 2048), BF16)],
        [pltpu.VMEM((2, PIX, LINE, 2048), BF16), dma((2,))],
    )
    patch = [pltpu.VMEM((SIDE, SIDE, LINE, 2304), BF16)]

    def crossed(early, late):
        return lax.ppermute(early, "pipe", [(1, 0)]), lax.ppermute(late, "pipe", [(0, 1)])

    kept = []
    x = x0
    a, st = first(0, x)
    for s in range(2):
        gb, gbo = gains[s]
        sums = links.to_all(st, *([dy] if s == 0 else []))
        if s == 0:
            gathered = links.gather_middle(gathered, sums[0])
        a, diff, sq, op, mix, second, st, mv1 = middle(s, a, links.swap(a), *sums, gb, msk)
        if s == 0:
            gathered = links.gather_next(gathered, second)
        mid, third, keep, send, mv2 = widen(s, second, *links.to_all(st), gb)
        stats = pairs(True, keep, send)
        if s == 0:
            if links.split:
                gathered = (gathered[0], {"A": (Weights("split", SPLIT_A1), gathered[1][0])}, gathered[1])
                gains.append(gains_of(1))
            act0, xhat, slope0, a_next, st, mv3 = turn(third, x, *stats, gbo)
            if links.split:
                gathered = links.gather_last((gathered[0], gathered[2]), a_next)
            else:
                gains.append(gains_of(1))
        else:
            act1, xhat, dz, keep, send, mv3 = top(place, third, x, *stats, gbo, dy)
        kept.append((x, a, mv1, diff, sq, op, mix, second, mv2, mid, xhat, mv3))
        if s == 0:
            x, a = act0, a_next

    gb, gbo = gains[1]
    x, a, mv1, diff, sq, op, mix, second, mv2, mid, xhat, mv3 = kept[1]
    activations = restore(place, act0, act1, *crossed(act0, act1))[0]
    dn2, st, d3, s3 = wide_back(
        1, dz, xhat, mv3, *pairs(False, keep, send, activations), gbo, second, mv2, gb
    )
    d2, s2 = second_back(None, dn2, second, mv2, *links.to_all(st), gb)
    dn1, st, dlog, dsq = middle_back(1, d2, a, mv1, gb, msk, op)
    g_rest = grad(
        all_grad_kernel, shares_of("whole", 2432, 4608, 2048), [d3, mid, d2, mix, dlog, sq, diff, dsq], patch
    )
    dx1, d1, s1, dz, keep, send = first_back(
        dn1, links.swap(dn1), a, mv1, *links.to_all(st, *g_rest), gb, dz, slope0, kept[0][10]
    )
    norms_1 = (s1, s2, s3)
    g_in1 = grad(first_grad_kernel, shares_of("split", 2048, 0), [d1, x])
    meanwhile = g_in1
    if links.split:
        late = links.half_sums(*g_rest)
        meanwhile = (late, *g_in1)
        late = links.scatter_whole(late)

    gb, gbo = gains[0]
    x, a, mv1, diff, sq, op, mix, second, mv2, mid, xhat, mv3 = kept[0]
    dn2, st, d3, s3 = wide_back(
        0, dz, xhat, mv3, *pairs(False, keep, send, *meanwhile), gbo, second, mv2, gb
    )
    g_out = grad(wide_grad_kernel, shares_of("split", 0, 2048), [d3, mid])
    *g_mid, d2, s2 = second_back(
        shares_of("split", 2048, 2560), dn2, second, mv2, *links.to_all(st, *g_out), gb, mix
    )
    dn1, st, dlog, dsq = middle_back(0, d2, a, mv1, gb, msk, op)
    g_branch = grad(branch_grad_kernel, shares_of("split", 0, 2432), [dlog, sq, diff, dsq], patch)
    *g_in, d1, s1 = last_grad(
        shares_of("split", 2048, 0), dn1, links.swap(dn1), a, mv1, *links.to_all(st, *g_branch), gb, x
    )
    norms_0 = (s1, s2, s3)
    dx0 = last_back(after(d1, *g_in), dz)
    input_grads = restore(place, dx0, dx1, *crossed(dx0, dx1))[0]

    if links.split:
        pair = links.scatter_split((*g_in1, *g_out), (dn1, d1, None, None))
        in_1, out_0 = pair[:, :2048], pair[:, 2048:]
        mid_0 = links.scatter_split(g_mid, (d1, None, None, None))
        pair = links.scatter_split((*g_in, *g_branch), (d1, None, None, None))
        in_0, branch_0 = pair[:, :2048], pair[:, 2048:]
        f_in = links.to_owner(in_0, in_1)
        f_branch = links.to_owner(branch_0, late[:, :2432])
        f_mid = links.to_owner(mid_0, late[:, 2432:7040])
        f_out = links.wide_rows(links.to_owner(out_0, late[:, 7040:]))
    else:
        rest = [v[..., :2432] for v in g_rest], [v[..., 2432:7040] for v in g_rest], [v[..., 7040:] for v in g_rest]
        f_branch = links.scatter_pairs(g_branch, rest[0], False)
        f_mid = links.scatter_pairs(g_mid, rest[1], False)
        f_out = links.scatter_pairs(g_out, rest[2], True)
        f_in = links.scatter_pairs(g_in, g_in1, False)
    grad_w_in = f_in.T[None]
    grad_w_squeeze = f_branch[:, :128][None]
    grad_w_near = f_branch[:, 128:1280].T[None]
    grad_w_far = f_branch[:, 1280:].T[None]
    grad_w_mid = f_mid.T[None]
    grad_w_out = f_out.T[None]

    s1, s2, s3 = [jnp.where(core == 0, e, l) for e, l in zip(norms_0, norms_1)]
    dp_index = lax.axis_index("dp")
    mid_sums = jnp.stack(
        [jnp.stack([s1[0:3].sum(0), s2[0:3].sum(0)]), jnp.stack([s1[4:7].sum(0), s2[4:7].sum(0)])]
    )
    mid_sums = lax.dynamic_slice_in_dim(mid_sums, dp_index * n, n, 2)
    out_sums = jnp.stack([s3[0:3].sum(0), s3[4:7].sum(0)])
    out_sums = lax.dynamic_slice_in_dim(out_sums, dp_index * 4 * n, 4 * n, 1)
    return (
        activations[None], input_grads[None], grad_w_in, grad_w_squeeze, grad_w_near, grad_w_far,
        grad_w_mid, grad_w_out, mid_sums[1][None], mid_sums[0][None], out_sums[1][None],
        out_sums[0][None],
    )


def solution(mesh):
    split = P("pipe", None, "dp")
    rows = P("pipe", "dp", None)
    vec = P("pipe", "dp")
    clips = P(None, "dp", None)
    weights = (split, rows, split, split, split, split, split, split, vec, vec)
    whole = P("pipe", None, "dp", None)
    return jax.shard_map(
        local,
        mesh=mesh,
        in_specs=(clips, clips, clips) + weights,
        out_specs=(whole, whole) + weights,
        check_vma=False,
    )
```

```python
import functools

import jax
import jax.numpy as jnp
from jax import lax
from jax.experimental import pallas as pl
from jax.experimental.pallas import tpu as pltpu
from jax.sharding import PartitionSpec as P

SEG = 8
SIDE = 7
PIX = SIDE * SIDE
HALF = SEG // 2
STRIDE = HALF + 1
LINE = 16
ROWS = PIX * LINE
EPS = 1e-05
F32 = jnp.float32
BF16 = jnp.bfloat16
VMEM_BYTES = 36 * 1024 * 1024


def dot(left, right):
    return lax.dot_general(left, right, (((1,), (0,)), ((), ())), preferred_element_type=F32)


def dot_nt(left, right):
    return lax.dot_general(left, right, (((1,), (1,)), ((), ())), preferred_element_type=F32)


def dot_tn(left, right):
    return lax.dot_general(left, right, (((0,), (0,)), ((), ())), preferred_element_type=F32)


def sigmoid(v):
    return 0.5 * jnp.tanh(0.5 * v) + 0.5


def line_of(width):
    return lax.broadcasted_iota(jnp.int32, (LINE, width), 0)


def own_lines(width):
    r = line_of(width)
    inside = (r < 4) | ((r >= 5) & (r < 9)) | ((r >= 10) & (r < 14))
    return inside.astype(F32)


def per_line(values):
    width = values.shape[1]
    r = line_of(width)
    return jnp.where(r < 5, values[0:1], jnp.where(r < 10, values[1:2], values[2:3]))


def per_batch(lines, count):
    r = line_of(lines.shape[1])
    pieces = []
    for b in range(3):
        keep = (r >= 5 * b) & (r < 5 * b + count)
        pieces.append(jnp.sum(jnp.where(keep, lines, 0.0), axis=0, keepdims=True))
    return pieces


def flat(v):
    return v.reshape(-1, v.shape[-1])


def chunks(body, init=0):
    return lax.fori_loop(0, SIDE, body, init)


def ref_stats(a_ref, first, width):
    lanes = pl.ds(first, width)

    def add(i, s):
        return s + jnp.sum(a_ref[pl.ds(i * SIDE, SIDE), :, lanes], axis=0)

    sums = per_batch(chunks(add, jnp.zeros((LINE, width), F32)), HALF)
    means = [s / (HALF * PIX) for s in sums]
    mean_lines = per_line(jnp.concatenate(means, axis=0))

    def add_sq(i, s):
        d = a_ref[pl.ds(i * SIDE, SIDE), :, lanes] - mean_lines[None]
        return s + jnp.sum(d * d, axis=0)

    sq = per_batch(chunks(add_sq, jnp.zeros((LINE, width), F32)), HALF)
    zero = jnp.zeros((1, width), F32)
    return jnp.concatenate(means + [zero] + sq + [zero], axis=0)


def pack(st):
    cut = st.shape[1] * 3 // 4
    rest = [
        jnp.concatenate([st[r : r + 1, cut:] for r in rows], axis=1)
        for rows in ((0, 1, 2), (4, 5, 6))
    ]
    return jnp.concatenate([st[0:3, :cut], st[4:7, :cut]] + rest, axis=0)


def unpack(p, group):
    third = p.shape[1] // 3
    row = p[6 + group : 7 + group]
    rest = jnp.concatenate([row[:, third * k : third * (k + 1)] for k in range(3)], axis=0)
    return jnp.concatenate([p[3 * group : 3 * group + 3], rest], axis=1)


def spread(st, out_ref):
    packed = pack(st)
    for k in range(out_ref.shape[0]):
        out_ref[k] = packed


def merge_norm(gs, rows_each):
    count = sum(g.shape[0] for g in gs)
    total = sum(jnp.sum(g[...], axis=0) for g in gs)
    mean = total / count
    off = 0.0
    for g in gs:
        d = g[...] - mean[None]
        off = off + jnp.sum(d * d, axis=0)
    var = (unpack(total, 1) + rows_each * unpack(off, 0)) / (rows_each * count)
    return eight(unpack(mean, 0), var)


def merge_sums(gs, rows_each):
    total = sum(jnp.sum(g[...], axis=0) for g in gs)
    return eight(unpack(total, 0), unpack(total, 1))


def eight(first, second):
    zero = jnp.zeros((1, first.shape[1]), F32)
    return jnp.concatenate([first, zero, second, zero], axis=0)


def merge_wide(merge, place, g, g_other, out_ref):
    core = place[0]
    rows_each = float(2 * HALF * PIX)
    half = out_ref.shape[1] // 2
    out_ref[:, pl.ds(pl.multiple_of(core * half, half), half)] = merge([g], rows_each)
    out_ref[:, pl.ds(pl.multiple_of((1 - core) * half, half), half)] = merge([g_other], rows_each)


def split_wide(place, st, keep_ref, send_ref):
    core = place[0]
    half = st.shape[1] // 2
    keep_ref[...] = st[:, pl.ds(pl.multiple_of(core * half, half), half)]
    send_ref[...] = st[:, pl.ds(pl.multiple_of((1 - core) * half, half), half)]


def pair_kernel(norm, keep, recv, out_ref):
    a, b = keep[...], recv[...]
    if norm:
        d = a[0:3] - b[0:3]
        mean = 0.5 * (a[0:3] + b[0:3])
        st = eight(mean, a[4:7] + b[4:7] + (HALF * PIX / 2.0) * d * d)
    else:
        st = a + b
    spread(st, out_ref)


OWN_ROWS = float(HALF * PIX)


def gains_kernel(wt, place, *rest):
    refs, (gb_ref, gbo_ref, buf, sems) = rest[: wt.count], rest[wt.count :]
    wait_all(wt.copies("gain", place, refs, buf, Moves(sems)))
    i = lax.broadcasted_iota(jnp.int32, (128, 512), 0)
    j = lax.broadcasted_iota(jnp.int32, (128, 512), 1)
    mid = jnp.zeros((16, 512), F32)
    for k in range(16):
        g = buf[k // 4, k // 2 % 2, k % 2, 0]
        hot = jnp.where((i < 32) & (j == 32 * k + i), 1.0, 0.0).astype(BF16)
        mid = mid + dot(g, hot)
        gbo_ref[:, 128 * k : 128 * k + 128] = g[4:12].astype(F32)
    gb_ref[...] = mid[0:8]


class Moves:
    def __init__(self, sems):
        self.sems, self.used, self.leaving = sems, 0, []

    def fetch(self, source, target):
        copy = pltpu.make_async_copy(source, target, self.sems.at[self.used])
        self.used += 1
        copy.start()
        return copy

    def store(self, source, target):
        self.leaving.append(self.fetch(source, target))

    def chunks_of(self, source, target):
        return [self.fetch(source.at[rows], target.at[rows]) for rows in CHUNKS]

    def tiles_of(self, source, target):
        return [self.fetch(source.at[:, :, lanes], target.at[:, :, lanes]) for lanes in TILES]

    def finish(self):
        wait_all(self.leaving)


CHUNKS = [pl.ds(SIDE * i, SIDE) for i in range(SIDE)]
TILES = [pl.ds(512 * j, 512) for j in range(4)]


def wait_all(copies):
    for c in copies:
        c.wait()


class Weights:
    def __init__(self, kind, segments):
        self.kind, self.segments = kind, segments

    @property
    def count(self):
        return 2 if self.kind == "whole" else 8

    def copies(self, name, place, refs, buf, moves):
        core, y, x = place[0], place[1], place[2]
        found = []
        for part, start, at, width in self.segments[name]:
            for side in range(2):
                c = core if side == 0 else 1 - core
                if self.kind == "whole":
                    pairs = [(refs[side], (ALL, ALL, ALL))]
                elif part == "P":
                    pairs = [(refs[4 * side], (ALL, y, ALL)), (refs[4 * side + 1], (ALL, 1 - y, ALL))]
                else:
                    pairs = [(refs[4 * side + 2], (ALL, ALL, x)), (refs[4 * side + 3], (ALL, ALL, 1 - x))]
                for ref, where in pairs:
                    source = ref.at[..., pl.ds(start, width)]
                    if isinstance(at, tuple):
                        target = buf.at[where + (c, at[0])]
                    else:
                        target = buf.at[where + (c, ALL, pl.ds(at, width))]
                    found.append(moves.fetch(source, target))
        return found


ALL = slice(None)


def first_matmul(x_buf, w_buf, a_ref, stb_ref):
    for j in range(2):
        w = w_buf[2 * j : 2 * j + 2].reshape(256, 2048)
        a_ref[:, :, pl.ds(256 * j, 256)] = dot_nt(flat(x_buf[...]), w).reshape(PIX, LINE, 256)
    spread(ref_stats(a_ref, 0, 512), stb_ref)


def permute_kernel(core_ref, x_ref, out_ref, x_buf, buf, sems):
    moves = Moves(sems)
    loads = moves.tiles_of(x_ref, x_buf)
    core = core_ref[0]
    i = lax.broadcasted_iota(jnp.int32, (ROWS, SEG * PIX), 0)
    j = lax.broadcasted_iota(jnp.int32, (ROWS, SEG * PIX), 1)
    pixel, line = i >> 4, i & 15
    hots = []
    for b in range(3):
        t = line - 5 * b
        target = (HALF * core + t) * PIX + pixel
        hots.append(jnp.where((t >= 0) & (t < HALF) & (j == target), 1.0, 0.0).astype(BF16))
    for load, lanes in zip(loads, TILES):
        load.wait()
        total = dot(hots[0], x_buf[0, :, lanes])
        total = total + dot(hots[1], x_buf[1, :, lanes])
        total = total + dot(hots[2], x_buf[2, :, lanes])
        buf[:, :, lanes] = total.astype(BF16).reshape(PIX, LINE, 512)
        moves.store(buf.at[:, :, lanes], out_ref.at[:, :, lanes])
    moves.finish()


def restore_kernel(place, early_ref, late_ref, early_in, late_in, out_ref, buf, out_buf, sems):
    core = place[0]

    def copies(mine, received):
        found = []
        for k, lanes in enumerate(TILES):
            for n, (v, side) in enumerate(((mine, core), (received, 1 - core))):
                found.append(
                    pltpu.make_async_copy(
                        v.at[:, :, lanes], buf.at[side, :, :, lanes], sems.at[2 * k + n]
                    )
                )
        return found

    @pl.when(core == 0)
    def _():
        for c in copies(early_ref, early_in):
            c.start()

    @pl.when(core == 1)
    def _():
        for c in copies(late_ref, late_in):
            c.start()

    def hot(first, count, side, b):
        j = lax.broadcasted_iota(jnp.int32, (count, ROWS), 0) + first
        i = lax.broadcasted_iota(jnp.int32, (count, ROWS), 1)
        seg = jnp.zeros_like(j)
        for k in range(1, SEG):
            seg = seg + jnp.where(j >= PIX * k, 1, 0)
        t = seg - HALF * side
        target = (j - PIX * seg) * LINE + 5 * b + t
        return jnp.where((t >= 0) & (t < HALF) & (i == target), 1.0, 0.0).astype(BF16)

    hots = [(hot(0, 208, 0, b), hot(192, 200, 1, b)) for b in range(3)]
    loads = copies(early_ref, early_in)
    leaving = []
    for k, lanes in enumerate(TILES):
        wait_all(loads[2 * k : 2 * k + 2])
        for b, (lower, upper) in enumerate(hots):
            low = dot(lower, flat(buf[0, :, :, lanes])).astype(BF16)
            high = dot(upper, flat(buf[1, :, :, lanes])).astype(BF16)
            out_buf[b, 0:192, lanes] = low[:192]
            out_buf[b, 192:208, lanes] = low[192:] + high[:16]
            out_buf[b, 208:392, lanes] = high[16:]
        copy = pltpu.make_async_copy(out_buf.at[:, :, lanes], out_ref.at[:, :, lanes], sems.at[8 + k])
        copy.start()
        leaving.append(copy)
    wait_all(leaving)


def first_kernel(wt, place, x_ref, *rest):
    refs, (a_ref, stb_ref, w_buf, sems) = rest[: wt.count], rest[wt.count :]
    wait_all(wt.copies("in", place, refs, w_buf, Moves(sems)))
    first_matmul(x_ref, w_buf, a_ref, stb_ref)


def tap_ranges(shift):
    return max(0, -shift), min(SIDE, SIDE - shift)


def build_patches(sq, patch):
    patch[...] = jnp.zeros(patch.shape, BF16)
    sq4 = sq.reshape(SIDE, SIDE, LINE, 128)
    for k in (1, 2):
        for tap in range(9):
            dy, dx = k * (tap // 3 - 1), k * (tap % 3 - 1)
            (y0, y1), (x0, x1) = tap_ranges(dy), tap_ranges(dx)
            col = ((k - 1) * 9 + tap) * 128
            patch[y0:y1, x0:x1, :, col : col + 128] = sq4[y0 + dy : y1 + dy, x0 + dx : x1 + dx]


def clear_border(pad):
    zero_row = jnp.zeros((9, LINE, 512), BF16)
    pad[0] = zero_row
    pad[8] = zero_row
    for y in range(1, 8):
        pad[y, 0] = jnp.zeros((LINE, 512), BF16)
        pad[y, 8] = jnp.zeros((LINE, 512), BF16)


def middle_kernel(wt, place, a_in, a_other, g, g_other, gb_ref, msk_ref, *rest):
    refs = rest[: wt.count]
    (
        a_ref, diff_ref, sq_ref, op_ref, mix_ref, second, second_ref, st_ref, mv_ref,
        sq_buf, nf_buf, mid_buf, a_buf, diff, sq_out, op, mixp, hid, patch, sems,
    ) = rest[wt.count :]
    core = place[0]
    moves = Moves(sems)
    sq_copies = wt.copies("sq", place, refs, sq_buf, moves)
    nf_copies = wt.copies("nf", place, refs, nf_buf, moves)
    mid_copies = wt.copies("mid", place, refs, mid_buf, moves)
    clear_border(mixp)
    mv_ref[...] = merge_norm([g, g_other], OWN_ROWS)
    r = line_of(512)
    halo = ((r == 4) | (r == 9) | (r == 14)) & (core == 0)
    mean = per_line(mv_ref[0:3])
    scale = lax.rsqrt(per_line(mv_ref[4:7]) + EPS) * gb_ref[0:1]
    shift = gb_ref[1:2]
    m = msk_ref[:, 0:1]
    for rows in CHUNKS:
        a = jnp.where(halo[None], pltpu.roll(a_other[rows], 4, 1), a_in[rows])
        a_buf[rows] = a
        n1 = (a - mean[None]) * scale[None] + shift[None]
        h = n1 * sigmoid(n1)
        hid[rows] = h
        diff[rows] = (m[None] * (pltpu.roll(h, LINE - 1, 1) - h)).astype(BF16)
    moves.store(a_buf, a_ref)
    moves.store(diff, diff_ref)
    wait_all(sq_copies)
    sq = dot(flat(diff[...]), sq_buf[...].reshape(512, 128)).astype(BF16)
    sq_out[...] = sq.reshape(PIX, LINE, 128)
    moves.store(sq_out, sq_ref)
    build_patches(sq, patch)
    wait_all(nf_copies)
    for j in range(2):
        lanes = pl.ds(256 * j, 256)
        w = nf_buf[2 * j : 2 * j + 2].reshape(256, 2304)
        logits = dot_nt(patch[...].reshape(ROWS, 2304), w).reshape(PIX, LINE, 256)
        opening = sigmoid(logits)
        op[:, :, lanes] = opening.astype(BF16)
        mixed = (hid[:, :, lanes] * (0.5 + opening)).astype(BF16)
        mixp[1:8, 1:8, :, lanes] = mixed.reshape(SIDE, SIDE, LINE, 256)
    moves.store(op, op_ref)
    moves.store(mixp, mix_ref)
    wait_all(mid_copies)

    total = 0.0
    for k in range(9):
        v = mixp[k // 3 : k // 3 + SIDE, k % 3 : k % 3 + SIDE].reshape(ROWS, 512)
        total = total + dot_nt(v, mid_buf[..., pl.ds(512 * k, 512)].reshape(512, 512))
    second[...] = total.reshape(PIX, LINE, 512)
    moves.store(second, second_ref)
    spread(ref_stats(second, 0, 512), st_ref)
    moves.finish()


def wide_kernel(wt, place, second, g, g_other, gb_ref, *rest):
    refs = rest[: wt.count]
    mid_ref, keep_ref, send_ref, mv_ref, buf, mid, third, st_ref, sems = rest[wt.count :]
    moves = Moves(sems)
    copies = wt.copies("out", place, refs, buf, moves)
    mv_ref[...] = merge_norm([g, g_other], OWN_ROWS)
    mean = per_line(mv_ref[0:3])
    scale = lax.rsqrt(per_line(mv_ref[4:7]) + EPS) * gb_ref[2:3]
    shift = gb_ref[3:4]
    for rows in CHUNKS:
        n2 = (second[rows] - mean[None]) * scale[None] + shift[None]
        mid[rows] = (n2 * sigmoid(n2)).astype(BF16)
    moves.store(mid, mid_ref)
    wait_all(copies)
    for j, lanes in enumerate(TILES):
        w = buf[j].reshape(512, 512)
        third[...] = dot_nt(flat(mid[...]), w).reshape(PIX, LINE, 512)
        st_ref[:, lanes] = ref_stats(third, 0, 512)
    split_wide(place, st_ref, keep_ref, send_ref)
    moves.finish()


def finish(mid, wide_buf, third, x_buf, loads, mv_ref, gb_ref, each, after_tile):
    for j, lanes in enumerate(TILES):
        third[...] = dot_nt(flat(mid[...]), wide_buf[j].reshape(512, 512)).reshape(PIX, LINE, 512)
        wait_all([load[j] for load in loads])
        mean = per_line(mv_ref[0:3, lanes])
        inv = lax.rsqrt(per_line(mv_ref[4:7, lanes]) + EPS)
        gain, bias = gb_ref[0:1, lanes], gb_ref[1:2, lanes]

        def chunk(i, carry):
            rows = pl.ds(i * SIDE, SIDE)
            xhat = (third[rows] - mean[None]) * inv[None]
            z = x_buf[rows, :, lanes].astype(F32) + xhat * gain[None] + bias[None]
            sg = sigmoid(z)
            return each(rows, lanes, xhat, z * sg, sg, carry)

        zero = jnp.zeros((LINE, 512), F32)
        after_tile(lanes, chunks(chunk, (zero, zero)))


def sums_of(dh, dg):
    zero = jnp.zeros((1, dh.shape[1]), F32)
    return jnp.concatenate(per_batch(dh, STRIDE) + [zero] + per_batch(dg, STRIDE) + [zero], axis=0)


def turn_kernel(wide_wt, wt, place, mid, x_ref, g, g_other, gb_ref, *rest):
    wide_refs, rest = rest[: wide_wt.count], rest[wide_wt.count :]
    refs = rest[: wt.count]
    (
        act_ref, xhat_ref, slope_ref, a_ref, st_ref, mv_ref,
        wide_buf, w_buf, third, x_buf, act, xhat_buf, slope, sems,
    ) = rest[wt.count :]
    moves = Moves(sems)
    wide_copies = wide_wt.copies("out", place, wide_refs, wide_buf, moves)
    loads = [moves.tiles_of(x_ref, x_buf)]
    copies = wt.copies("in", place, refs, w_buf, moves)
    merge_wide(merge_norm, place, g, g_other, mv_ref)

    def each(rows, lanes, xhat, y, sg, carry):
        act[rows, :, lanes] = y.astype(BF16)
        xhat_buf[rows, :, lanes] = xhat.astype(BF16)
        slope[rows, :, lanes] = (sg + y * (1.0 - sg)).astype(BF16)
        return carry

    def after_tile(lanes, _):
        for buf, ref in ((act, act_ref), (xhat_buf, xhat_ref), (slope, slope_ref)):
            moves.store(buf.at[:, :, lanes], ref.at[:, :, lanes])

    wait_all(wide_copies)
    finish(mid, wide_buf, third, x_buf, loads, mv_ref, gb_ref, each, after_tile)
    wait_all(copies)
    first_matmul(act, w_buf, a_ref, st_ref)
    moves.finish()


def top_kernel(
    wide_wt, place, mid, x_ref, g, g_other, gb_ref, dy_ref, *rest,
):
    wide_refs, rest = rest[: wide_wt.count], rest[wide_wt.count :]
    (
        act_ref, xhat_ref, dz, keep_ref, send_ref, mv_ref,
        wide_buf, third, x_buf, dy, act, xhat_buf, sums_ref, sems,
    ) = rest
    moves = Moves(sems)
    wide_copies = wide_wt.copies("out", place, wide_refs, wide_buf, moves)
    loads = [moves.tiles_of(r, b) for r, b in ((x_ref, x_buf), (dy_ref, dy))]
    merge_wide(merge_norm, place, g, g_other, mv_ref)

    def each(rows, lanes, xhat, y, sg, carry):
        act[rows, :, lanes] = y.astype(BF16)
        xhat_buf[rows, :, lanes] = xhat.astype(BF16)
        d = dy[rows, :, lanes].astype(F32) * (sg + y * (1.0 - sg))
        dz[rows, :, lanes] = d.astype(BF16)
        return carry[0] + jnp.sum(d, axis=0), carry[1] + jnp.sum(d * xhat, axis=0)

    def after_tile(lanes, carry):
        for buf, ref in ((act, act_ref), (xhat_buf, xhat_ref)):
            moves.store(buf.at[:, :, lanes], ref.at[:, :, lanes])
        sums_ref[:, lanes] = sums_of(*carry)

    wait_all(wide_copies)
    finish(mid, wide_buf, third, x_buf, loads, mv_ref, gb_ref, each, after_tile)
    split_wide(place, sums_ref, keep_ref, send_ref)
    moves.finish()


class Shares:
    def __init__(self, kind, parts):
        self.kind, self.parts = kind, parts

    @property
    def count(self):
        return 2 if self.kind == "whole" else 4 * sum(1 for width in self.parts if width)

    def outs(self):
        if self.kind == "whole":
            width = sum(self.parts)
            return [((4, 2, 2, 16, width), BF16)] * 2
        return [((4, 2, 16, width), BF16) for width in self.parts if width for _ in range(4)]

    def buffers(self):
        return [pltpu.VMEM(shape, dtype) for shape, dtype in self.outs()]

    def store(self, place, out, first, result, zs=ALL):
        refs, bufs, moves = out

        def put(ref, buf, v, lanes):
            buf[zs, ..., lanes] = v
            moves.store(buf.at[zs, ..., lanes], ref.at[zs, ..., lanes])

        core, y, x = place[0], place[1], place[2]
        width = result.shape[1]
        parts = result.astype(BF16).reshape(-1, 2, 2, 2, 16, width)
        lower, upper = parts[:, :, :, 0], parts[:, :, :, 1]
        sides = [jnp.where(core == 0, lower, upper), jnp.where(core == 0, upper, lower)]
        if self.kind == "whole":
            for ref, buf, v in zip(refs, bufs, sides):
                put(ref, buf, v, pl.ds(first, width))
            return
        is_p = first < self.parts[0]
        start = first if is_p else first - self.parts[0]
        lanes = pl.ds(start, width)
        refs = refs[:4] if is_p else refs[-4:]
        bufs = bufs[:4] if is_p else bufs[-4:]
        for k, v in enumerate(sides):
            if is_p:
                two, at = (v[:, 0], v[:, 1]), y
            else:
                two, at = (v[:, :, 0], v[:, :, 1]), x
            put(refs[2 * k], bufs[2 * k], jnp.where(at == 0, two[0], two[1]), lanes)
            put(refs[2 * k + 1], bufs[2 * k + 1], jnp.where(at == 0, two[1], two[0]), lanes)


def wide_back_kernel(
    rows_total, wt, place, dz, xhat_ref, mv3_ref, g, g_other, gbo_ref, second_ref, mv2_ref, gb_ref, *rest
):
    refs = rest[: wt.count]
    dn2, stb_ref, d3_ref, s3_ref, buf, xhat, second, d3, lines, sems = rest[wt.count :]
    moves = Moves(sems)
    loads = moves.chunks_of(xhat_ref, xhat)
    copies = wt.copies("out", place, refs, buf, moves)
    second_load = moves.fetch(second_ref, second)
    merge_wide(merge_sums, place, g, g_other, s3_ref)
    own = own_lines(512)
    for lanes in TILES:
        lines[0, :, lanes] = lax.rsqrt(per_line(mv3_ref[4:7, lanes]) + EPS) * gbo_ref[0:1, lanes] * own
        lines[1, :, lanes] = per_line(s3_ref[0:3, lanes]) / rows_total
        lines[2, :, lanes] = per_line(s3_ref[4:7, lanes]) / rows_total
    for load, rows in zip(loads, CHUNKS):
        load.wait()
        for lanes in TILES:
            v = dz[rows, :, lanes].astype(F32) - lines[1, :, lanes][None]
            v = v - xhat[rows, :, lanes].astype(F32) * lines[2, :, lanes][None]
            d3[rows, :, lanes] = (lines[0, :, lanes][None] * v).astype(BF16)
    moves.store(d3, d3_ref)
    wait_all(copies)
    for j, lanes in enumerate(TILES):
        part = dot(flat(d3[:, :, lanes]), buf[j].reshape(512, 512)).reshape(PIX, LINE, 512)
        dn2[...] = part if j == 0 else dn2[...] + part
    second_load.wait()
    mean = per_line(mv2_ref[0:3])
    inv = lax.rsqrt(per_line(mv2_ref[4:7]) + EPS)
    gain, bias = gb_ref[2:3], gb_ref[3:4]

    def chunk(i, carry):
        rows = pl.ds(i * SIDE, SIDE)
        xh = (second[rows] - mean[None]) * inv[None]
        n2 = xh * gain[None] + bias[None]
        sg = sigmoid(n2)
        dn = dn2[rows] * (sg * (1.0 + n2 * (1.0 - sg)))
        dn2[rows] = dn
        return carry[0] + jnp.sum(dn, axis=0), carry[1] + jnp.sum(dn * xh, axis=0)

    zero = jnp.zeros((LINE, 512), F32)
    spread(sums_of(*chunks(chunk, (zero, zero))), stb_ref)
    moves.finish()


def wide_grad(sh, place, refs, start, d3, mid):
    for j in range(4):
        v = flat(d3[:, :, pl.ds(512 * j, 512)])
        res = dot_tn(v, flat(mid[...])).reshape(2, 2, 2, 4, 16, 512)
        for g in range(4):
            sh.store(place, refs, start + 512 * g, res[:, :, :, g].reshape(128, 512), slice(j, j + 1))


def middle_grad(sh, place, refs, start, d2, mixp):
    for tap in range(9):
        mixed = mixp[tap // 3 : tap // 3 + SIDE, tap % 3 : tap % 3 + SIDE].reshape(ROWS, 512)
        sh.store(place, refs, start + 512 * tap, dot_tn(flat(d2[...]), mixed))


def branch_grad(sh, place, refs, start, dlog, sq_ref, diff, dsq, patch):
    build_patches(flat(sq_ref[...]), patch)
    for j in range(3):
        pv = patch[:, :, :, pl.ds(768 * j, 768)].reshape(ROWS, 768)
        sh.store(place, refs, start + 128 + 768 * j, dot_tn(flat(dlog[...]), pv))
    sh.store(place, refs, start, dot_tn(flat(diff[...]), flat(dsq[...])))


def fetch_all(moves, refs, bufs):
    return [moves.fetch(r, b) for r, b in zip(refs, bufs)]


def branch_grad_kernel(sh, place, dlog, dsq, sq_ref, diff_ref, *rest):
    refs, (sq, diff, patch), bufs = rest[: sh.count], rest[sh.count : -1 - sh.count], rest[-1 - sh.count : -1]
    moves = Moves(rest[-1])
    wait_all(fetch_all(moves, (sq_ref, diff_ref), (sq, diff)))
    branch_grad(sh, place, (refs, bufs, moves), 0, dlog, sq, diff, dsq, patch)
    moves.finish()


def all_grad_kernel(sh, place, d2, dlog, dsq, d3_ref, mid_ref, mix_ref, sq_ref, diff_ref, *rest):
    refs, (d3, mid, mixp, sq, diff, patch) = rest[: sh.count], rest[sh.count : -1 - sh.count]
    bufs, moves = rest[-1 - sh.count : -1], Moves(rest[-1])
    out = (refs, bufs, moves)
    mix_load = moves.fetch(mix_ref, mixp)
    loads = fetch_all(moves, (sq_ref, diff_ref, d3_ref, mid_ref), (sq, diff, d3, mid))
    mix_load.wait()
    middle_grad(sh, place, out, 2432, d2, mixp)
    wait_all(loads)
    wide_grad(sh, place, out, 7040, d3, mid)
    branch_grad(sh, place, out, 0, dlog, sq, diff, dsq, patch)
    moves.finish()


def mixed_grad_kernel(sh, place, d3, mid_ref, d1, x_ref, *rest):
    refs, (mid, x), bufs = rest[: sh.count], rest[sh.count : -1 - sh.count], rest[-1 - sh.count : -1]
    moves = Moves(rest[-1])
    wait_all(fetch_all(moves, (mid_ref, x_ref), (mid, x)))
    wide_grad(sh, place, (refs, bufs, moves), 0, d3, mid)
    first_grad(sh, place, (refs, bufs, moves), 2048, d1, x)
    moves.finish()


def second_back_kernel(rows_total, sh, place, dn2, second_ref, mv2_ref, g, g_other, gb_ref, *rest):
    if sh is not None:
        mix_ref, refs, rest = rest[0], rest[1 : 1 + sh.count], rest[1 + sh.count :]
        d2, s2_ref, second, mixp, *bufs, sems = rest
    else:
        d2, s2_ref, second, sems = rest
    moves = Moves(sems)
    second_loads = moves.chunks_of(second_ref, second)
    if sh is not None:
        mix_load = moves.fetch(mix_ref, mixp)
    s2_ref[...] = merge_sums([g, g_other], OWN_ROWS)
    own = own_lines(512)
    mean2 = per_line(mv2_ref[0:3])
    inv2 = lax.rsqrt(per_line(mv2_ref[4:7]) + EPS)
    k2 = inv2 * gb_ref[2:3] * own
    dh2 = per_line(s2_ref[0:3]) / rows_total
    dg2 = per_line(s2_ref[4:7]) / rows_total
    for i, rows in enumerate(CHUNKS):
        second_loads[i].wait()
        xh = (second[rows] - mean2[None]) * inv2[None]
        d2[rows] = (k2[None] * (dn2[rows] - dh2[None] - xh * dg2[None])).astype(BF16)
    if sh is not None:
        mix_load.wait()
        middle_grad(sh, place, (refs, bufs, moves), 0, d2, mixp)
    moves.finish()


def middle_back_kernel(wt, place, d2, a_ref, mv1_ref, gb_ref, msk_ref, op_ref, *rest):
    refs = rest[: wt.count]
    (
        dn1, stb_ref, dlog, dsq_out,
        sq_buf, nf_buf, mid_buf, d2p, a, op, dmix, dsq, sems,
    ) = rest[wt.count :]
    moves = Moves(sems)
    mid_copies = wt.copies("mid", place, refs, mid_buf, moves)
    late_loads = [moves.fetch(a_ref, a), moves.fetch(op_ref, op)]
    nf_copies = wt.copies("nf", place, refs, nf_buf, moves)
    sq_copies = wt.copies("sq", place, refs, sq_buf, moves)
    clear_border(d2p)
    for i, rows in enumerate(CHUNKS):
        d2p[i + 1, 1:8] = d2[rows]
    wait_all(mid_copies)

    total = 0.0
    for k in range(9):
        y, x = 2 - k // 3, 2 - k % 3
        v = d2p[y : y + SIDE, x : x + SIDE].reshape(ROWS, 512)
        total = total + dot(v, mid_buf[..., pl.ds(512 * k, 512)].reshape(512, 512))
    dmix[...] = total.reshape(PIX, LINE, 512)
    wait_all(late_loads)
    mean1 = per_line(mv1_ref[0:3])
    inv1 = lax.rsqrt(per_line(mv1_ref[4:7]) + EPS)
    gain1, bias1 = gb_ref[0:1], gb_ref[1:2]

    def log_chunk(i, c):
        rows = pl.ds(i * SIDE, SIDE)
        n1 = (a[rows] - mean1[None]) * inv1[None] * gain1[None] + bias1[None]
        h = n1 * sigmoid(n1)
        o = op[rows].astype(F32)
        dlog[rows] = (dmix[rows] * h * o * (1.0 - o)).astype(BF16)
        return c

    chunks(log_chunk)
    wait_all(nf_copies)
    dsq[...] = jnp.zeros(dsq.shape, F32)
    for k in (1, 2):
        for ty in range(3):
            w = nf_buf[..., pl.ds(((k - 1) * 9 + ty * 3) * 128, 384)].reshape(512, 384)
            res = dot(flat(dlog[...]), w).reshape(SIDE, SIDE, LINE, 384)
            for tx in range(3):
                dy, dx = k * (ty - 1), k * (tx - 1)
                (y0, y1), (x0, x1) = tap_ranges(dy), tap_ranges(dx)
                dsq[y0 + dy : y1 + dy, x0 + dx : x1 + dx] += res[
                    y0:y1, x0:x1, :, 128 * tx : 128 * tx + 128
                ]
    dsq_low = dsq[...].astype(BF16).reshape(ROWS, 128)
    dsq_out[...] = dsq_low.reshape(PIX, LINE, 128)
    wait_all(sq_copies)
    dn1[...] = dot_nt(dsq_low, sq_buf[...].reshape(512, 128)).reshape(PIX, LINE, 512)
    m = msk_ref[:, 0:1]

    def last_chunk(i, carry):
        rows = pl.ds(i * SIDE, SIDE)
        xh = (a[rows] - mean1[None]) * inv1[None]
        n1 = xh * gain1[None] + bias1[None]
        sg = sigmoid(n1)
        e = dn1[rows] * m[None]
        o = op[rows].astype(F32)
        dhid = dmix[rows] * (0.5 + o) - e + pltpu.roll(e, 1, 1)
        dn = dhid * (sg * (1.0 + n1 * (1.0 - sg)))
        dn1[rows] = dn
        return carry[0] + jnp.sum(dn, axis=0), carry[1] + jnp.sum(dn * xh, axis=0)

    zero = jnp.zeros((LINE, 512), F32)
    spread(sums_of(*chunks(last_chunk, (zero, zero))), stb_ref)


def first_d1(rows_total, place, loads, dn1, dn1_other, a, mv1_ref, s1_ref, gb_ref, d1):
    own = own_lines(512)
    r = line_of(512)
    first = ((r == 0) | (r == 5) | (r == 10)) & (place[0] == 1)
    mean = per_line(mv1_ref[0:3])
    inv = lax.rsqrt(per_line(mv1_ref[4:7]) + EPS)
    k = inv * gb_ref[0:1] * own
    dh = per_line(s1_ref[0:3]) / rows_total
    dg = per_line(s1_ref[4:7]) / rows_total
    for i, rows in enumerate(CHUNKS):
        loads[i].wait()
        xh = (a[rows] - mean[None]) * inv[None]
        dn = dn1[rows] + jnp.where(first[None], pltpu.roll(dn1_other[rows], LINE - 4, 1), 0.0)
        d1[rows] = (k[None] * (dn - dh[None] - xh * dg[None])).astype(BF16)


def first_back_kernel(
    rows_total, wt, place, dn1, other, a_ref, mv1_ref, g, g_other, gb_ref, dz_ref, slope_ref, xhat_ref, *rest
):
    refs = rest[: wt.count]
    (
        dx_ref, d1, s1_ref, below, keep_ref, send_ref,
        w_buf, a, dz, slope, xhat, dx, sums_ref, sems,
    ) = rest[wt.count :]
    moves = Moves(sems)
    loads = moves.chunks_of(a_ref, a)
    copies = wt.copies("in", place, refs, w_buf, moves)
    tiles = [moves.tiles_of(r, b) for r, b in ((dz_ref, dz), (slope_ref, slope), (xhat_ref, xhat))]
    s1_ref[...] = merge_sums([g, g_other], OWN_ROWS)
    first_d1(rows_total, place, loads, dn1, other, a, mv1_ref, s1_ref, gb_ref, d1)
    wait_all(copies)
    for j, lanes in enumerate(TILES):
        wait_all([load[j] for load in tiles])
        w = w_buf[..., lanes].reshape(512, 512)
        v = dot(flat(d1[...]), w).reshape(PIX, LINE, 512) + dz[:, :, lanes].astype(F32)
        low = v.astype(BF16)
        dx[:, :, lanes] = low
        d = low.astype(F32) * slope[:, :, lanes].astype(F32)
        below[:, :, lanes] = d.astype(BF16)
        moves.store(dx.at[:, :, lanes], dx_ref.at[:, :, lanes])
        sums_ref[:, lanes] = sums_of(
            jnp.sum(d, axis=0), jnp.sum(d * xhat[:, :, lanes].astype(F32), axis=0)
        )
    split_wide(place, sums_ref, keep_ref, send_ref)
    moves.finish()


def first_grad(sh, place, out, start, d1, x_ref):
    for j in range(4):
        x = flat(x_ref[:, :, pl.ds(512 * j, 512)])
        sh.store(place, out, start + 512 * j, dot_tn(flat(d1[...]), x))


def last_grad_kernel(rows_total, sh, place, dn1, other, a_ref, mv1_ref, g, g_other, gb_ref, x_ref, *rest):
    refs, rest = rest[: sh.count], rest[sh.count :]
    d1, s1_ref, a, x, *bufs, sems = rest
    moves = Moves(sems)
    loads = moves.chunks_of(a_ref, a)
    x_load = moves.fetch(x_ref, x)
    s1_ref[...] = merge_sums([g, g_other], OWN_ROWS)
    first_d1(rows_total, place, loads, dn1, other, a, mv1_ref, s1_ref, gb_ref, d1)
    x_load.wait()
    first_grad(sh, place, (refs, bufs, moves), 0, d1, x)
    moves.finish()


def last_back_kernel(wt, place, d1, dz_ref, *rest):
    refs, (dx_ref, w_buf, dz, dx, sems) = rest[: wt.count], rest[wt.count :]
    moves = Moves(sems)
    copies = wt.copies("in", place, refs, w_buf, moves)
    loads = moves.tiles_of(dz_ref, dz)
    wait_all(copies)
    for j, lanes in enumerate(TILES):
        loads[j].wait()
        w = w_buf[..., lanes].reshape(512, 512)
        v = dot(flat(d1[...]), w).reshape(PIX, LINE, 512) + dz[:, :, lanes].astype(F32)
        dx[:, :, lanes] = v.astype(BF16)
        moves.store(dx.at[:, :, lanes], dx_ref.at[:, :, lanes])
    moves.finish()


VM = pl.BlockSpec(memory_space=pltpu.VMEM)
HB = pl.BlockSpec(memory_space=pltpu.HBM)
SM = pl.BlockSpec(memory_space=pltpu.SMEM)
AN = pl.BlockSpec(memory_space=pl.ANY)


class Near:
    def __init__(self, value):
        self.value = value


class Near2(Near):
    pass


def is_big(shape):
    return len(shape) >= 4 or (len(shape) == 3 and shape[0] in (PIX, 3))


def size_of(shape, dtype):
    size = jnp.dtype(dtype).itemsize
    for k in shape:
        size *= k
    return size


def call(kernel, outs, scratch=(), us=5):
    def run(place, *values):
        specs = [SM]
        need = 6 * 1024 * 1024
        need += sum(size_of(v.shape, v.dtype) for v in scratch)
        need += sum(size_of(*o[:2]) for o in outs if not (is_big(o[0]) and len(o) == 2))
        for v in values:
            u = v.value if isinstance(v, Near) else v
            if not is_big(u.shape) or (isinstance(v, Near) and not isinstance(v, Near2)):
                need += size_of(u.shape, u.dtype)
        for v in values:
            if isinstance(v, Near):
                specs.append(AN if isinstance(v, Near2) else VM)
            else:
                specs.append(HB if is_big(v.shape) else VM)
        return pl.pallas_call(
            kernel,
            in_specs=specs,
            out_specs=tuple(HB if is_big(o[0]) and len(o) == 2 else VM for o in outs),
            out_shape=tuple(jax.ShapeDtypeStruct(o[0], o[1]) for o in outs),
            scratch_shapes=list(scratch) + [pltpu.SemaphoreType.DMA((96,))],
            compiler_params=pltpu.CompilerParams(vmem_limit_bytes=52 * 1024 * 1024),
            cost_estimate=pl.CostEstimate(flops=us * 10**9, bytes_accessed=us * 3 * 10**6, transcendentals=0),
        )(place, *[v.value if isinstance(v, Near) else v for v in values])

    return run


def near(width, dtype):
    return ((PIX, LINE, width), dtype, True)


def pm(width, dtype):
    return ((PIX, LINE, width), dtype)


def buf(width, dtype):
    return pltpu.VMEM((PIX, LINE, width), dtype)


def wbuf(width):
    return pltpu.VMEM((4, 2, 2, 2, 16, width), BF16)


STAT = ((8, 512), F32)
WIDE_STAT = ((8, 2048), F32)
PAIR = [(0, 1), (1, 0)]


class Links:
    def __init__(self, dp, core):
        self.dp, self.core = dp, core
        self.at = lax.axis_index("dp")

    def bit(self, k):
        return (self.at // k) % 2

    def place(self):
        y, x = (self.bit(2), self.bit(1)) if self.split else (0, 0)
        return jnp.stack([self.core, jnp.int32(y), jnp.int32(x)]).astype(jnp.int32)

    split = True

    def swap(self, v):
        return lax.ppermute(v, "pipe", PAIR)

    def across(self, v, k):
        return lax.ppermute(v, "dp", [(i, i ^ k) for i in range(self.dp)])

    def to_all(self, spread, *meanwhile):
        g = lax.all_to_all(spread, "dp", 0, 0)
        if meanwhile:
            g = after(g, *meanwhile)
        return g, self.swap(g)

    def by_core(self, own, other):
        first = self.core == 0
        return jnp.where(first, own, other), jnp.where(first, other, own)

    def in_order(self, which, own, other, axis):
        pair = jnp.where(which == 0, jnp.stack([own, other], axis), jnp.stack([other, own], axis))
        return pair

    def halves(self, piece):
        two = piece.reshape(2, 16, piece.shape[1])
        keep = lax.dynamic_index_in_dim(two, self.core, 0, keepdims=False)
        recv = self.swap(lax.dynamic_index_in_dim(two, 1 - self.core, 0, keepdims=False))
        return self.by_core(keep, recv)

    def gather_first(self, v, cut):
        p, q = v[..., :cut], v[..., cut:]
        p_other, q_other = self.across(p, 1), self.across(q, 2)
        return self.in_order(self.bit(1), p, p_other, 1), self.in_order(self.bit(2), q, q_other, 1)

    def gather_second(self, p, q):
        mine = (p, self.across(p, 2), q, self.across(q, 1))
        return mine + tuple(self.swap(v) for v in mine)

    def gather_whole(self, own):
        return lax.all_gather(own, "dp").reshape(4, 2, 2, 16, -1)

    def gather_blocks(self, gains, inner, rest, wide, permute, clips, cotangent):
        rows = jnp.concatenate([jnp.pad(v, ((0, 0), (0, 128 - v.shape[1]))) for v in gains], axis=0)
        tail = jnp.pad(rows, ((0, 32 - rows.shape[0]), (0, 0)))
        a = self.halves(jnp.concatenate([inner, tail], axis=1))
        b, c = self.halves(rest), self.halves(self.narrow_rows(wide))
        b0 = self.gather_whole(b[0])
        v = after(a[0], b[0])
        v = self.in_order(self.bit(8), v, self.across(v, 8), 0)
        x = permute(after(clips, v, b[0]))
        moved = after(self.across(v, 4), x)
        v = self.in_order(self.bit(4), v, moved, 1).reshape(4, 16, -1)
        ca = jnp.concatenate([c[0], a[1]], axis=1)
        ca = self.in_order(self.bit(8), ca, self.across(after(ca, v), 8), 0)
        dy = permute(after(cotangent, v))
        moved = after(self.across(ca, 4), dy)
        ca = self.in_order(self.bit(4), ca, moved, 1).reshape(4, 16, -1)
        a0 = self.gather_second(*self.gather_first(v, 1024))
        block_0 = {"A": (Weights("split", SPLIT_A), a0)}
        return (block_0, (ca, b0, jnp.concatenate([c[1], b[1]], axis=1))), x, dy

    def gather_middle(self, blocks, pieces, then):
        block_0, (_, b0, bc) = blocks
        ca = self.gather_second(*pieces)
        block_0["C"] = (Weights("split", SPLIT_C), ca)
        b0 = after(b0, then)
        block_0["B"] = (Weights("whole", middle_at(0)), (b0, self.swap(b0)))
        return block_0, (ca, self.gather_whole(after(bc, b0)))

    def gather_last(self, blocks, third):
        block_0, (ca, bc) = blocks
        bc = after(bc, third)
        bc = (bc, self.swap(bc))
        return block_0, {
            "A": (Weights("split", SPLIT_A1), ca),
            "B": (Weights("whole", middle_at(2048)), bc),
            "C": (Weights("whole", wide_at(0)), bc),
        }

    def gains_of(self, group, place):
        wt, refs = group
        return call(functools.partial(gains_kernel, wt), [STAT, WIDE_STAT], [wbuf(128)])(place, *refs)

    def add(self, a, b):
        return (a.astype(F32) + b.astype(F32)).astype(BF16)

    def halve(self, v, axis, k, then=None):
        which = self.bit(k)
        keep = lax.dynamic_index_in_dim(v, which, axis, keepdims=False)
        send = lax.dynamic_index_in_dim(v, 1 - which, axis, keepdims=False)
        moved = self.across(send, k)
        if then is not None:
            moved = after(moved, then)
        return self.add(keep, moved)

    def scatter_first(self, g):
        return [self.add(g[k], self.swap(g[k + 2])) for k in (1, 5)]

    def scatter_xy(self, g, sent, then=(None, None)):
        done = []
        for own, send_own, other, k in ((g[0], g[2], sent[0], 2), (g[4], g[6], sent[1], 1)):
            moved = self.across(other, k)
            if then[0] is not None:
                moved = after(moved, then[0])
            v = self.add(self.add(own, self.swap(send_own)), moved)
            done.append(self.halve(v, 1, 3 - k, then[1]))
        return jnp.concatenate(done, axis=-1)

    def scatter_z(self, v, then=(None, None)):
        half = self.halve(v.reshape(2, 2, 16, -1), 1, 4, then[0])
        return self.halve(half, 0, 8, then[1]), half

    def half_sums(self, keep, send):
        return self.add(keep, self.swap(send)).reshape(16, 16, -1)

    def scatter_whole(self, v):
        return lax.psum_scatter(v, "dp", scatter_dimension=0, tiled=True)[0]

    def scatter_at_once(self, v, *then):
        v = lax.all_to_all(v, "dp", 0, 0)
        if then:
            v = after(v, *then)
        return jnp.sum(v.astype(F32), axis=0)

    def handed(self, early, late):
        return lax.ppermute(early, "pipe", [(1, 0)]), lax.ppermute(late, "pipe", [(0, 1)])

    def to_owner(self, early, early_other, late, late_other):
        at_0 = jnp.concatenate([early, early_other], axis=0).astype(F32)
        at_1 = jnp.concatenate([late_other, late], axis=0).astype(F32)
        return jnp.where(self.core == 0, at_0, at_1)

    def wide_rows(self, v):
        return v.reshape(2, 16, 4, -1).transpose(0, 2, 1, 3).reshape(128, -1)

    def narrow_rows(self, v):
        return v.reshape(2, 4, 16, -1).transpose(0, 2, 1, 3).reshape(32, -1)


class AnyLinks(Links):
    split = False

    def gather_blocks(self, gains, inner, rest, wide, permute, clips, cotangent):
        full = [lax.all_gather(v, "dp", tiled=True) for v in (inner, wide, rest)]
        full[1] = jnp.stack([self.narrow_rows(f) for f in full[1].reshape(16, 128, -1)]).reshape(512, -1)
        own = jnp.concatenate(full, axis=1)
        vectors = [lax.all_gather(v, "dp", axis=1, tiled=True).astype(F32) for v in gains]
        mid = jnp.pad(jnp.concatenate(vectors[:4]), ((0, 4), (0, 0)))
        out = jnp.pad(jnp.concatenate(vectors[4:]), ((0, 6), (0, 0)))
        mids, outs = self.by_core(mid, self.swap(mid)), self.by_core(out, self.swap(out))
        blocks = []
        for s, full in enumerate(self.by_core(own, self.swap(own))):
            parts = full.reshape(16, 2, 16, -1)
            mine = lax.dynamic_index_in_dim(parts, self.core, 1, keepdims=False)
            theirs = lax.dynamic_index_in_dim(parts, 1 - self.core, 1, keepdims=False)
            refs = tuple(v.reshape(4, 2, 2, 16, -1) for v in (mine, theirs))
            groups = (("A", {"in": [("W", 0, 0, 2048)]}), ("B", middle_at(4096)), ("C", wide_at(2048)))
            blocks.append({k: (Weights("whole", v), refs) for k, v in groups})
            blocks[s]["gains"] = (mids[s], outs[s])
        return blocks, permute(clips), permute(cotangent)

    def gather_middle(self, blocks, pieces, then):
        return blocks

    def gather_last(self, blocks, third):
        return blocks

    def gains_of(self, group, place):
        return group

    def scatter_pairs(self, early, late, wide):
        full = []
        for keep, send in (early, late):
            half = self.add(keep, self.swap(send)).reshape(16, 16, -1)
            full.append(jnp.stack(self.by_core(half, self.swap(half)), axis=1))
        total = jnp.where(self.core == 0, full[0], full[1])
        if wide:
            total = jnp.stack([self.wide_rows(v.reshape(32, -1)) for v in total])
        total = total.reshape(-1, total.shape[-1])
        return lax.psum_scatter(total, "dp", scatter_dimension=0, tiled=True).astype(F32)


def after(v, *others):
    return lax.optimization_barrier((v, others))[0]


SPLIT_A = {"in": [("P", 0, 0, 1024), ("Q", 0, 1024, 1024)], "gain": [("Q", 1024, 0, 128)]}
SPLIT_C = {"out": [("P", 512 * g, (g,), 512) for g in range(4)]}
SPLIT_A1 = {"in": [("Q", 0, 0, 2048)], "gain": [("Q", 2048, 0, 128)]}


def middle_at(first):
    return {
        "sq": [("W", first, 0, 128)],
        "nf": [("W", first + 128, 0, 2304)],
        "mid": [("W", first + 2432, 0, 4608)],
    }


def wide_at(first):
    return {"out": [("W", first + 512 * g, (g,), 512) for g in range(4)]}


def local(
    clips_in, cotangent, segment_ids, w_in, w_squeeze, w_near, w_far, w_mid, w_out,
    gain_mid, bias_mid, gain_out, bias_out,
):
    dp = lax.axis_size("dp")
    core = lax.axis_index("pipe")
    links = (Links if dp == 16 else AnyLinks)(dp, core)
    place = links.place()
    rows_total = float(clips_in.shape[1] * dp)

    def low(v):
        return v[0].astype(BF16)

    n = w_in.shape[2]
    gain_rows = [low(gain_mid)[0:1], low(bias_mid)[0:1], low(gain_mid)[1:2], low(bias_mid)[1:2]]
    def permute(v):
        scratch = [pltpu.VMEM((3, SEG * PIX, 2048), BF16), buf(2048, BF16)]
        return call(permute_kernel, [pm(2048, BF16)], scratch)(place, v)[0]

    gathered, x0, dy = links.gather_blocks(
        gain_rows + [low(gain_out)[None], low(bias_out)[None]],
        low(w_in).T,
        jnp.concatenate([low(w_squeeze), low(w_near).T, low(w_far).T, low(w_mid).T], axis=1),
        low(w_out).T,
        permute, clips_in, cotangent,
    )

    def gains_of(s):
        return links.gains_of(gathered[s]["A" if links.split else "gains"], place)

    gains = [gains_of(0)]

    same = (segment_ids[:, 0, 1:] == segment_ids[:, 0, :-1]).astype(F32)
    same = jnp.concatenate([same, jnp.zeros((3, 1), F32)], axis=1)
    mine_seg = lax.dynamic_slice_in_dim(same, core * HALF, HALF, 1)
    msk = jnp.concatenate([mine_seg, jnp.zeros((3, 1), F32)], axis=1).reshape(15)
    msk = jnp.broadcast_to(jnp.concatenate([msk, jnp.zeros((1,), F32)])[:, None], (LINE, 128))


    wide_buf = pltpu.VMEM((4, 2, 2, 2, 4, 16, 512), BF16)

    stb = ((dp, 8, 384), F32)
    half_stat = ((8, 1024), F32)
    buffers = {"in": wbuf(2048), "sq": wbuf(128), "nf": wbuf(2304), "mid": wbuf(4608), "out": wide_buf}
    groups = {"A": ("in",), "B": ("sq", "nf", "mid"), "C": ("out",)}

    def kernel(body, group, values, outs, scratch, *static):
        wt, refs = group[1]
        names = groups[group[0]]
        refs = [Near2(v) if names == ("out",) and wt.kind == "split" else v for v in refs]
        return call(functools.partial(body, *static, wt), outs, [buffers[k] for k in names] + scratch)(
            place, *values, *refs
        )

    def group(s, k):
        return k, gathered[s][k]

    wide_sums = pltpu.VMEM((8, 2048), F32)
    lines = pltpu.VMEM((3, LINE, 2048), F32)
    padded = pltpu.VMEM((9, 9, LINE, 512), BF16)
    patch = pltpu.VMEM((SIDE, SIDE, LINE, 2304), BF16)

    def first(s, x):
        return kernel(first_kernel, group(s, "A"), [Near(x)], [near(512, F32), stb], [])

    def middle(s, a, other, *values):
        outs = [pm(512, F32), pm(512, BF16), pm(128, BF16), pm(512, BF16),
                ((9, 9, LINE, 512), BF16), near(512, F32), pm(512, F32), stb, STAT]
        scratch = [buf(512, F32), buf(512, BF16), buf(128, BF16), buf(512, BF16), padded, buf(512, F32), patch]
        return kernel(middle_kernel, group(s, "B"), [Near(a), Near(other), *values], outs, scratch)

    def widen(s, second, *values):
        outs = [pm(512, BF16), half_stat, half_stat, STAT]
        scratch = [buf(512, BF16), buf(512, F32), wide_sums]
        return kernel(wide_kernel, group(s, "C"), [Near(second), *values], outs, scratch)

    def turn(mid, *values):
        outs = [pm(2048, BF16)] * 3 + [near(512, F32), stb, WIDE_STAT]
        wide_wt, wide_refs = gathered[0]["C"]
        scratch = [buf(512, F32)] + [buf(2048, BF16)] * 4
        wt, refs = gathered[1]["A"]
        return call(
            functools.partial(turn_kernel, wide_wt, wt), outs, [wide_buf, buffers["in"]] + scratch
        )(place, Near(mid), *values, *[Near2(v) for v in wide_refs], *refs)

    def top(mid, *values):
        outs = [pm(2048, BF16)] * 2 + [near(2048, BF16), half_stat, half_stat, WIDE_STAT]
        wide_wt, wide_refs = gathered[1]["C"]
        scratch = [wide_buf, buf(512, F32)] + [buf(2048, BF16)] * 4 + [wide_sums]
        return call(functools.partial(top_kernel, wide_wt), outs, scratch)(
            place, Near(mid), *values, *wide_refs
        )

    def pairs(norm, keep, send, *meanwhile):
        recv = links.swap(send)
        v = pl.pallas_call(
            functools.partial(pair_kernel, norm), in_specs=[VM, VM], out_specs=VM,
            out_shape=jax.ShapeDtypeStruct((dp, 8, 768), F32),
            compiler_params=pltpu.CompilerParams(vmem_limit_bytes=8 * 1024 * 1024),
        )(keep, recv)
        return links.to_all(v, *meanwhile)

    def wide_back(s, dz, *values):
        outs = [near(512, F32), stb, pm(2048, BF16), WIDE_STAT]
        scratch = [buf(2048, BF16), buf(512, F32), buf(2048, BF16), lines]
        return kernel(wide_back_kernel, group(s, "C"), [Near(dz), *values], outs, scratch, rows_total)

    def second_back(sh, dn2, *values):
        outs = [near(512, BF16), STAT]
        scratch = [buf(512, F32)]
        if sh:
            outs, scratch = sh.outs() + outs, scratch + [padded] + sh.buffers()
        return call(functools.partial(second_back_kernel, rows_total, sh), outs, scratch)(
            place, Near(dn2), *values
        )

    def middle_back(s, d2, *values):
        outs = [near(512, F32), stb, near(512, BF16), near(128, BF16)]
        scratch = [padded, buf(512, F32), buf(512, BF16), buf(512, F32), pltpu.VMEM((SIDE, SIDE, LINE, 128), F32)]
        return kernel(middle_back_kernel, group(s, "B"), [Near(d2), *values], outs, scratch)

    def first_back(dn1, other, *values):
        outs = [pm(2048, BF16), near(512, BF16), STAT, near(2048, BF16), half_stat, half_stat]
        scratch = [buf(512, F32)] + [buf(2048, BF16)] * 4 + [wide_sums]
        return kernel(
            first_back_kernel, group(1, "A"), [Near(dn1), Near(other), *values], outs, scratch, rows_total
        )

    def last_grad(sh, dn1, other, *values):
        scratch = [buf(512, F32), buf(2048, BF16)] + sh.buffers()
        return call(
            functools.partial(last_grad_kernel, rows_total, sh), sh.outs() + [near(512, BF16), STAT], scratch
        )(place, Near(dn1), Near(other), *values)

    def last_back(d1, *values):
        scratch = [buf(2048, BF16), buf(2048, BF16)]
        return kernel(last_back_kernel, group(0, "A"), [Near(d1), *values], [pm(2048, BF16)], scratch)[0]

    def shares_of(kind, *parts):
        return Shares(kind if links.split else "whole", parts)

    def grad(body, sh, values, *scratch):
        bufs = [pltpu.VMEM(v.shape, v.dtype) for v in values if not isinstance(v, Near)]
        return call(
            functools.partial(body, sh), sh.outs(), bufs + list(scratch) + sh.buffers()
        )(place, *values)

    restore = call(
        restore_kernel, [((3, SEG * PIX, 2048), BF16)],
        [pltpu.VMEM((2, PIX, LINE, 2048), BF16), pltpu.VMEM((3, SEG * PIX, 2048), BF16)],
    )

    def crossed(early, late):
        return lax.ppermute(early, "pipe", [(1, 0)]), lax.ppermute(late, "pipe", [(0, 1)])

    kept = []
    x = x0
    if links.split:
        x = after(x, gathered[1][0])
    a, st = first(0, x)
    for s in range(2):
        gb, gbo = gains[s]
        if s == 0:
            pieces = links.gather_first(after(gathered[1][0], a), 2048) if links.split else ()
            sums = links.to_all(st, dy, *pieces, gb)
            gathered = links.gather_middle(gathered, pieces, sums[0])
        else:
            sums = links.to_all(st, gb)
        a, diff, sq, op, mix, second, second_far, st, mv1 = middle(s, a, links.swap(a), *sums, gb, msk)
        mid, keep, send, mv2 = widen(s, second, *links.to_all(st), gb)
        stats = pairs(True, keep, send)
        if s == 0:
            if links.split:
                gathered = (gathered[0], {"A": (Weights("split", SPLIT_A1), gathered[1][0])}, gathered[1])
                gains.append(gains_of(1))
            act0, xhat, slope0, a_next, st, mv3 = turn(mid, x, *stats, gbo)
            if links.split:
                gathered = links.gather_last((gathered[0], gathered[2]), a_next)
            else:
                gains.append(gains_of(1))
        else:
            act1, xhat, dz, keep, send, mv3 = top(mid, x, *stats, gbo, dy)
        kept.append((x, a, mv1, diff, sq, op, mix, second_far, mv2, mid, xhat, mv3))
        if s == 0:
            x, a = act0, a_next

    gb, gbo = gains[1]
    x, a, mv1, diff, sq, op, mix, second, mv2, mid, xhat, mv3 = kept[1]
    dn2, st, d3, s3 = wide_back(
        1, dz, xhat, mv3, *pairs(False, keep, send), gbo, second, mv2, gb
    )
    d2, s2 = second_back(None, dn2, second, mv2, *links.to_all(st), gb)
    dn1, st, dlog, dsq = middle_back(1, d2, a, mv1, gb, msk, op)
    g_rest = grad(
        all_grad_kernel, shares_of("whole", 2432, 4608, 2048),
        [Near(d2), Near(dlog), Near(dsq), d3, mid, mix, sq, diff], patch,
    )
    split = links.split
    sums = links.to_all(st, *g_rest)
    dx1, d1_late, s1, dz, keep, send = first_back(
        dn1, links.swap(dn1), a, mv1, *sums, gb, dz, slope0, kept[0][10]
    )
    meanwhile = []
    if split:
        late = links.half_sums(g_rest[0], after(g_rest[1], sums[0]))
        keep = after(keep, late)
        late = links.scatter_whole(late)
    norms_1 = (s1, s2, s3)
    x_late = x

    gb, gbo = gains[0]
    x, a, mv1, diff, sq, op, mix, second, mv2, mid, xhat, mv3 = kept[0]
    dn2, st, d3, s3 = wide_back(
        0, dz, xhat, mv3, *pairs(False, keep, send, *meanwhile), gbo, second, mv2, gb
    )
    g_mixed = grad(
        mixed_grad_kernel, shares_of("whole", 4096), [Near(d3), mid, Near(d1_late), x_late]
    )
    *g_mid, d2, s2 = second_back(
        shares_of("split", 2048, 2560), dn2, second, mv2, *links.to_all(st, *g_mixed), gb, mix
    )
    dn1, st, dlog, dsq = middle_back(0, d2, a, mv1, gb, msk, op)
    if split:
        sent = links.scatter_first(g_mid)
        mixed = links.half_sums(*g_mixed)
        dlog = after(dlog, mixed, *sent)
        mixed = links.scatter_whole(mixed)
    g_branch = grad(branch_grad_kernel, shares_of("whole", 2432), [Near(dlog), Near(dsq), sq, diff], patch)
    meanwhile = g_branch
    if split:
        rest_0 = [links.half_sums(*g_branch)]
    *g_in, d1, s1 = last_grad(
        shares_of("whole", 2048), dn1, links.swap(dn1), a, mv1, *links.to_all(st, *meanwhile), gb, x
    )
    norms_0 = (s1, s2, s3)
    if split:
        last = jnp.concatenate([links.half_sums(*g_in), *rest_0], axis=-1)
        dx0 = last_back(after(d1, last), dz)
        act0, act1 = after((act0, act1), last)
        early = links.scatter_xy(g_mid, sent, (d1, None))
        activations = restore(place, act0, act1, *crossed(act0, act1))[0]
        input_grads = restore(place, after(dx0, activations), dx1, *crossed(dx0, dx1))[0]
        mid_0, _ = links.scatter_z(early, (input_grads, None))
        last = links.scatter_at_once(last, input_grads, mid_0)
        in_0, branch_0 = jnp.split(last, [2048], axis=-1)
        mixed = after(mixed, late)
        out_0, in_1 = jnp.split(mixed, 2, axis=-1)
        branch_1, mid_1, out_1 = jnp.split(late, [2432, 7040], axis=-1)
        mid_other, late_other = links.handed(mid_0, late)
        branch_1o, mid_1o, out_1o = jnp.split(late_other, [2432, 7040], axis=-1)
        out_0o, in_1o = links.handed(out_0, in_1)
        in_0o, branch_0o = jnp.split(lax.ppermute(last, "pipe", [(1, 0)]), [2048], axis=-1)
        f_in = links.to_owner(in_0, in_0o, in_1, in_1o)
        f_branch = links.to_owner(branch_0, branch_0o, branch_1, branch_1o)
        f_mid = links.to_owner(mid_0, mid_other, mid_1, mid_1o)
        f_out = links.wide_rows(links.to_owner(out_0, out_0o, out_1, out_1o))
    else:
        activations = restore(place, act0, act1, *crossed(act0, act1))[0]
        dx0 = last_back(d1, dz)
        input_grads = restore(place, dx0, dx1, *crossed(dx0, dx1))[0]
        rest = [v[..., :2432] for v in g_rest], [v[..., 2432:7040] for v in g_rest], [v[..., 7040:] for v in g_rest]
        f_branch = links.scatter_pairs(g_branch, rest[0], False)
        f_mid = links.scatter_pairs(g_mid, rest[1], False)
        g_out, in_1 = [v[..., :2048] for v in g_mixed], [v[..., 2048:] for v in g_mixed]
        f_out = links.scatter_pairs(g_out, rest[2], True)
        f_in = links.scatter_pairs(g_in, in_1, False)

    grad_w_in = f_in.T[None]
    grad_w_squeeze = f_branch[:, :128][None]
    grad_w_near = f_branch[:, 128:1280].T[None]
    grad_w_far = f_branch[:, 1280:].T[None]
    grad_w_mid = f_mid.T[None]
    grad_w_out = f_out.T[None]

    s1, s2, s3 = [jnp.where(core == 0, e, l) for e, l in zip(norms_0, norms_1)]
    dp_index = lax.axis_index("dp")
    mid_sums = jnp.stack(
        [jnp.stack([s1[0:3].sum(0), s2[0:3].sum(0)]), jnp.stack([s1[4:7].sum(0), s2[4:7].sum(0)])]
    )
    mid_sums = lax.dynamic_slice_in_dim(mid_sums, dp_index * n, n, 2)
    out_sums = jnp.stack([s3[0:3].sum(0), s3[4:7].sum(0)])
    out_sums = lax.dynamic_slice_in_dim(out_sums, dp_index * 4 * n, 4 * n, 1)
    return (
        activations[None], input_grads[None], grad_w_in, grad_w_squeeze, grad_w_near, grad_w_far,
        grad_w_mid, grad_w_out, mid_sums[1][None], mid_sums[0][None], out_sums[1][None],
        out_sums[0][None],
    )


def solution(mesh):
    split = P("pipe", None, "dp")
    rows = P("pipe", "dp", None)
    vec = P("pipe", "dp")
    clips = P(None, "dp", None)
    weights = (split, rows, split, split, split, split, split, split, vec, vec)
    whole = P("pipe", None, "dp", None)
    return jax.shard_map(
        local,
        mesh=mesh,
        in_specs=(clips, clips, clips) + weights,
        out_specs=(whole, whole) + weights,
        check_vma=False,
    )
```

```python
import functools

import jax
import jax.numpy as jnp
from jax import lax
from jax.experimental import pallas as pl
from jax.experimental.pallas import tpu as pltpu
from jax.sharding import PartitionSpec as P

SEG = 8
SIDE = 7
PIX = SIDE * SIDE
HALF = SEG // 2
STRIDE = HALF + 1
LINE = 16
ROWS = PIX * LINE
EPS = 1e-05
F32 = jnp.float32
BF16 = jnp.bfloat16
VMEM_BYTES = 36 * 1024 * 1024


def dot(left, right):
    return lax.dot_general(left, right, (((1,), (0,)), ((), ())), preferred_element_type=F32)


def dot_nt(left, right):
    return lax.dot_general(left, right, (((1,), (1,)), ((), ())), preferred_element_type=F32)


def dot_tn(left, right):
    return lax.dot_general(left, right, (((0,), (0,)), ((), ())), preferred_element_type=F32)


def sigmoid(v):
    return 0.5 * jnp.tanh(0.5 * v) + 0.5


def line_of(width):
    return lax.broadcasted_iota(jnp.int32, (LINE, width), 0)


def own_lines(width):
    r = line_of(width)
    inside = (r < 4) | ((r >= 5) & (r < 9)) | ((r >= 10) & (r < 14))
    return inside.astype(F32)


def per_line(values):
    width = values.shape[1]
    r = line_of(width)
    return jnp.where(r < 5, values[0:1], jnp.where(r < 10, values[1:2], values[2:3]))


def per_batch(lines, count):
    r = line_of(lines.shape[1])
    pieces = []
    for b in range(3):
        keep = (r >= 5 * b) & (r < 5 * b + count)
        pieces.append(jnp.sum(jnp.where(keep, lines, 0.0), axis=0, keepdims=True))
    return pieces


def flat(v):
    return v.reshape(-1, v.shape[-1])


def chunks(body, init=0):
    return lax.fori_loop(0, SIDE, body, init)


def ref_stats(a_ref, first, width):
    lanes = pl.ds(first, width)

    def add(i, s):
        return s + jnp.sum(a_ref[pl.ds(i * SIDE, SIDE), :, lanes], axis=0)

    sums = per_batch(chunks(add, jnp.zeros((LINE, width), F32)), HALF)
    means = [s / (HALF * PIX) for s in sums]
    mean_lines = per_line(jnp.concatenate(means, axis=0))

    def add_sq(i, s):
        d = a_ref[pl.ds(i * SIDE, SIDE), :, lanes] - mean_lines[None]
        return s + jnp.sum(d * d, axis=0)

    sq = per_batch(chunks(add_sq, jnp.zeros((LINE, width), F32)), HALF)
    zero = jnp.zeros((1, width), F32)
    return jnp.concatenate(means + [zero] + sq + [zero], axis=0)


def pack(st):
    cut = st.shape[1] * 3 // 4
    rest = [
        jnp.concatenate([st[r : r + 1, cut:] for r in rows], axis=1)
        for rows in ((0, 1, 2), (4, 5, 6))
    ]
    return jnp.concatenate([st[0:3, :cut], st[4:7, :cut]] + rest, axis=0)


def unpack(p, group):
    third = p.shape[1] // 3
    row = p[6 + group : 7 + group]
    rest = jnp.concatenate([row[:, third * k : third * (k + 1)] for k in range(3)], axis=0)
    return jnp.concatenate([p[3 * group : 3 * group + 3], rest], axis=1)


def spread(st, out_ref):
    packed = pack(st)
    for k in range(out_ref.shape[0]):
        out_ref[k] = packed


def merge_norm(gs, rows_each):
    count = sum(g.shape[0] for g in gs)
    total = sum(jnp.sum(g[...], axis=0) for g in gs)
    mean = total / count
    off = 0.0
    for g in gs:
        d = g[...] - mean[None]
        off = off + jnp.sum(d * d, axis=0)
    var = (unpack(total, 1) + rows_each * unpack(off, 0)) / (rows_each * count)
    return eight(unpack(mean, 0), var)


def merge_sums(gs, rows_each):
    total = sum(jnp.sum(g[...], axis=0) for g in gs)
    return eight(unpack(total, 0), unpack(total, 1))


def eight(first, second):
    zero = jnp.zeros((1, first.shape[1]), F32)
    return jnp.concatenate([first, zero, second, zero], axis=0)


def merge_wide(merge, place, g, g_other, out_ref):
    core = place[0]
    rows_each = float(2 * HALF * PIX)
    half = out_ref.shape[1] // 2
    out_ref[:, pl.ds(pl.multiple_of(core * half, half), half)] = merge([g], rows_each)
    out_ref[:, pl.ds(pl.multiple_of((1 - core) * half, half), half)] = merge([g_other], rows_each)


def split_wide(place, st, keep_ref, send_ref):
    core = place[0]
    half = st.shape[1] // 2
    keep_ref[...] = st[:, pl.ds(pl.multiple_of(core * half, half), half)]
    send_ref[...] = st[:, pl.ds(pl.multiple_of((1 - core) * half, half), half)]


def pair_kernel(norm, keep, recv, out_ref):
    a, b = keep[...], recv[...]
    if norm:
        d = a[0:3] - b[0:3]
        mean = 0.5 * (a[0:3] + b[0:3])
        st = eight(mean, a[4:7] + b[4:7] + (HALF * PIX / 2.0) * d * d)
    else:
        st = a + b
    spread(st, out_ref)


OWN_ROWS = float(HALF * PIX)


def gains_kernel(wt, place, *rest):
    refs, (gb_ref, gbo_ref, buf, sems) = rest[: wt.count], rest[wt.count :]
    wait_all(wt.copies("gain", place, refs, buf, Moves(sems)))
    i = lax.broadcasted_iota(jnp.int32, (128, 512), 0)
    j = lax.broadcasted_iota(jnp.int32, (128, 512), 1)
    mid = jnp.zeros((16, 512), F32)
    for k in range(16):
        g = buf[k // 4, k // 2 % 2, k % 2, 0]
        hot = jnp.where((i < 32) & (j == 32 * k + i), 1.0, 0.0).astype(BF16)
        mid = mid + dot(g, hot)
        gbo_ref[:, 128 * k : 128 * k + 128] = g[4:12].astype(F32)
    gb_ref[...] = mid[0:8]


class Moves:
    def __init__(self, sems):
        self.sems, self.used, self.leaving = sems, 0, []

    def fetch(self, source, target):
        copy = pltpu.make_async_copy(source, target, self.sems.at[self.used])
        self.used += 1
        copy.start()
        return copy

    def store(self, source, target):
        self.leaving.append(self.fetch(source, target))

    def chunks_of(self, source, target):
        return [self.fetch(source.at[rows], target.at[rows]) for rows in CHUNKS]

    def tiles_of(self, source, target):
        return [self.fetch(source.at[:, :, lanes], target.at[:, :, lanes]) for lanes in TILES]

    def finish(self):
        wait_all(self.leaving)


CHUNKS = [pl.ds(SIDE * i, SIDE) for i in range(SIDE)]
TILES = [pl.ds(512 * j, 512) for j in range(4)]


def wait_all(copies):
    for c in copies:
        c.wait()


class Weights:
    def __init__(self, kind, segments):
        self.kind, self.segments = kind, segments

    @property
    def count(self):
        return 2 if self.kind == "whole" else 8

    def copies(self, name, place, refs, buf, moves):
        core, y, x = place[0], place[1], place[2]
        found = []
        for part, start, at, width in self.segments[name]:
            for side in range(2):
                c = core if side == 0 else 1 - core
                if self.kind == "whole":
                    pairs = [(refs[side], (ALL, ALL, ALL))]
                elif part == "P":
                    pairs = [(refs[4 * side], (ALL, y, ALL)), (refs[4 * side + 1], (ALL, 1 - y, ALL))]
                else:
                    pairs = [(refs[4 * side + 2], (ALL, ALL, x)), (refs[4 * side + 3], (ALL, ALL, 1 - x))]
                for ref, where in pairs:
                    source = ref.at[..., pl.ds(start, width)]
                    if isinstance(at, tuple):
                        target = buf.at[where + (c, at[0])]
                    else:
                        target = buf.at[where + (c, ALL, pl.ds(at, width))]
                    found.append(moves.fetch(source, target))
        return found


ALL = slice(None)


def first_matmul(x_buf, w_buf, a_ref, stb_ref):
    for j in range(2):
        w = w_buf[2 * j : 2 * j + 2].reshape(256, 2048)
        a_ref[:, :, pl.ds(256 * j, 256)] = dot_nt(flat(x_buf[...]), w).reshape(PIX, LINE, 256)
    spread(ref_stats(a_ref, 0, 512), stb_ref)


def permute_kernel(core_ref, x_ref, out_ref, x_buf, buf, sems):
    moves = Moves(sems)
    loads = moves.tiles_of(x_ref, x_buf)
    core = core_ref[0]
    i = lax.broadcasted_iota(jnp.int32, (ROWS, SEG * PIX), 0)
    j = lax.broadcasted_iota(jnp.int32, (ROWS, SEG * PIX), 1)
    pixel, line = i >> 4, i & 15
    hots = []
    for b in range(3):
        t = line - 5 * b
        target = (HALF * core + t) * PIX + pixel
        hots.append(jnp.where((t >= 0) & (t < HALF) & (j == target), 1.0, 0.0).astype(BF16))
    for load, lanes in zip(loads, TILES):
        load.wait()
        total = dot(hots[0], x_buf[0, :, lanes])
        total = total + dot(hots[1], x_buf[1, :, lanes])
        total = total + dot(hots[2], x_buf[2, :, lanes])
        buf[:, :, lanes] = total.astype(BF16).reshape(PIX, LINE, 512)
        moves.store(buf.at[:, :, lanes], out_ref.at[:, :, lanes])
    moves.finish()


def restore_kernel(place, early_ref, late_ref, early_in, late_in, out_ref, buf, out_buf, sems):
    core = place[0]

    def copies(mine, received):
        found = []
        for k, lanes in enumerate(TILES):
            for n, (v, side) in enumerate(((mine, core), (received, 1 - core))):
                found.append(
                    pltpu.make_async_copy(
                        v.at[:, :, lanes], buf.at[side, :, :, lanes], sems.at[2 * k + n]
                    )
                )
        return found

    @pl.when(core == 0)
    def _():
        for c in copies(early_ref, early_in):
            c.start()

    @pl.when(core == 1)
    def _():
        for c in copies(late_ref, late_in):
            c.start()

    def hot(first, count, side, b):
        j = lax.broadcasted_iota(jnp.int32, (count, ROWS), 0) + first
        i = lax.broadcasted_iota(jnp.int32, (count, ROWS), 1)
        seg = jnp.zeros_like(j)
        for k in range(1, SEG):
            seg = seg + jnp.where(j >= PIX * k, 1, 0)
        t = seg - HALF * side
        target = (j - PIX * seg) * LINE + 5 * b + t
        return jnp.where((t >= 0) & (t < HALF) & (i == target), 1.0, 0.0).astype(BF16)

    hots = [(hot(0, 208, 0, b), hot(192, 200, 1, b)) for b in range(3)]
    loads = copies(early_ref, early_in)
    leaving = []
    for k, lanes in enumerate(TILES):
        wait_all(loads[2 * k : 2 * k + 2])
        for b, (lower, upper) in enumerate(hots):
            low = dot(lower, flat(buf[0, :, :, lanes])).astype(BF16)
            high = dot(upper, flat(buf[1, :, :, lanes])).astype(BF16)
            out_buf[b, 0:192, lanes] = low[:192]
            out_buf[b, 192:208, lanes] = low[192:] + high[:16]
            out_buf[b, 208:392, lanes] = high[16:]
        copy = pltpu.make_async_copy(out_buf.at[:, :, lanes], out_ref.at[:, :, lanes], sems.at[8 + k])
        copy.start()
        leaving.append(copy)
    wait_all(leaving)


def first_kernel(wt, place, x_ref, *rest):
    refs, (a_ref, stb_ref, w_buf, sems) = rest[: wt.count], rest[wt.count :]
    wait_all(wt.copies("in", place, refs, w_buf, Moves(sems)))
    first_matmul(x_ref, w_buf, a_ref, stb_ref)


def tap_ranges(shift):
    return max(0, -shift), min(SIDE, SIDE - shift)


def build_patches(sq, patch):
    patch[...] = jnp.zeros(patch.shape, BF16)
    sq4 = sq.reshape(SIDE, SIDE, LINE, 128)
    for k in (1, 2):
        for tap in range(9):
            dy, dx = k * (tap // 3 - 1), k * (tap % 3 - 1)
            (y0, y1), (x0, x1) = tap_ranges(dy), tap_ranges(dx)
            col = ((k - 1) * 9 + tap) * 128
            patch[y0:y1, x0:x1, :, col : col + 128] = sq4[y0 + dy : y1 + dy, x0 + dx : x1 + dx]


def clear_border(pad):
    zero_row = jnp.zeros((9, LINE, 512), BF16)
    pad[0] = zero_row
    pad[8] = zero_row
    for y in range(1, 8):
        pad[y, 0] = jnp.zeros((LINE, 512), BF16)
        pad[y, 8] = jnp.zeros((LINE, 512), BF16)


def middle_kernel(wt, place, a_in, a_other, g, g_other, gb_ref, msk_ref, *rest):
    refs = rest[: wt.count]
    (
        a_ref, diff_ref, sq_ref, op_ref, mix_ref, second, second_ref, st_ref, mv_ref,
        sq_buf, nf_buf, mid_buf, a_buf, diff, sq_out, op, mixp, hid, patch, sems,
    ) = rest[wt.count :]
    core = place[0]
    moves = Moves(sems)
    sq_copies = wt.copies("sq", place, refs, sq_buf, moves)
    nf_copies = wt.copies("nf", place, refs, nf_buf, moves)
    mid_copies = wt.copies("mid", place, refs, mid_buf, moves)
    clear_border(mixp)
    mv_ref[...] = merge_norm([g, g_other], OWN_ROWS)
    r = line_of(512)
    halo = ((r == 4) | (r == 9) | (r == 14)) & (core == 0)
    mean = per_line(mv_ref[0:3])
    scale = lax.rsqrt(per_line(mv_ref[4:7]) + EPS) * gb_ref[0:1]
    shift = gb_ref[1:2]
    m = msk_ref[:, 0:1]
    for rows in CHUNKS:
        a = jnp.where(halo[None], pltpu.roll(a_other[rows], 4, 1), a_in[rows])
        a_buf[rows] = a
        n1 = (a - mean[None]) * scale[None] + shift[None]
        h = n1 * sigmoid(n1)
        hid[rows] = h
        diff[rows] = (m[None] * (pltpu.roll(h, LINE - 1, 1) - h)).astype(BF16)
    moves.store(a_buf, a_ref)
    moves.store(diff, diff_ref)
    wait_all(sq_copies)
    sq = dot(flat(diff[...]), sq_buf[...].reshape(512, 128)).astype(BF16)
    sq_out[...] = sq.reshape(PIX, LINE, 128)
    moves.store(sq_out, sq_ref)
    build_patches(sq, patch)
    wait_all(nf_copies)
    for j in range(2):
        lanes = pl.ds(256 * j, 256)
        w = nf_buf[2 * j : 2 * j + 2].reshape(256, 2304)
        logits = dot_nt(patch[...].reshape(ROWS, 2304), w).reshape(PIX, LINE, 256)
        opening = sigmoid(logits)
        op[:, :, lanes] = opening.astype(BF16)
        mixed = (hid[:, :, lanes] * (0.5 + opening)).astype(BF16)
        mixp[1:8, 1:8, :, lanes] = mixed.reshape(SIDE, SIDE, LINE, 256)
    moves.store(op, op_ref)
    moves.store(mixp, mix_ref)
    wait_all(mid_copies)

    total = 0.0
    for k in range(9):
        v = mixp[k // 3 : k // 3 + SIDE, k % 3 : k % 3 + SIDE].reshape(ROWS, 512)
        total = total + dot_nt(v, mid_buf[..., pl.ds(512 * k, 512)].reshape(512, 512))
    second[...] = total.reshape(PIX, LINE, 512)
    moves.store(second, second_ref)
    spread(ref_stats(second, 0, 512), st_ref)
    moves.finish()


def wide_kernel(wt, place, second, g, g_other, gb_ref, *rest):
    refs = rest[: wt.count]
    mid_ref, keep_ref, send_ref, mv_ref, buf, mid, third, st_ref, sems = rest[wt.count :]
    moves = Moves(sems)
    copies = wt.copies("out", place, refs, buf, moves)
    mv_ref[...] = merge_norm([g, g_other], OWN_ROWS)
    mean = per_line(mv_ref[0:3])
    scale = lax.rsqrt(per_line(mv_ref[4:7]) + EPS) * gb_ref[2:3]
    shift = gb_ref[3:4]
    for rows in CHUNKS:
        n2 = (second[rows] - mean[None]) * scale[None] + shift[None]
        mid[rows] = (n2 * sigmoid(n2)).astype(BF16)
    moves.store(mid, mid_ref)
    wait_all(copies)
    for j, lanes in enumerate(TILES):
        w = buf[j].reshape(512, 512)
        third[...] = dot_nt(flat(mid[...]), w).reshape(PIX, LINE, 512)
        st_ref[:, lanes] = ref_stats(third, 0, 512)
    split_wide(place, st_ref, keep_ref, send_ref)
    moves.finish()


def finish(mid, wide_buf, third, x_buf, loads, mv_ref, gb_ref, each, after_tile):
    for j, lanes in enumerate(TILES):
        third[...] = dot_nt(flat(mid[...]), wide_buf[j].reshape(512, 512)).reshape(PIX, LINE, 512)
        wait_all([load[j] for load in loads])
        mean = per_line(mv_ref[0:3, lanes])
        inv = lax.rsqrt(per_line(mv_ref[4:7, lanes]) + EPS)
        gain, bias = gb_ref[0:1, lanes], gb_ref[1:2, lanes]

        def chunk(i, carry):
            rows = pl.ds(i * SIDE, SIDE)
            xhat = (third[rows] - mean[None]) * inv[None]
            z = x_buf[rows, :, lanes].astype(F32) + xhat * gain[None] + bias[None]
            sg = sigmoid(z)
            return each(rows, lanes, xhat, z * sg, sg, carry)

        zero = jnp.zeros((LINE, 512), F32)
        after_tile(lanes, chunks(chunk, (zero, zero)))


def sums_of(dh, dg):
    zero = jnp.zeros((1, dh.shape[1]), F32)
    return jnp.concatenate(per_batch(dh, STRIDE) + [zero] + per_batch(dg, STRIDE) + [zero], axis=0)


def turn_kernel(wide_wt, wt, place, mid, x_ref, g, g_other, gb_ref, *rest):
    wide_refs, rest = rest[: wide_wt.count], rest[wide_wt.count :]
    refs = rest[: wt.count]
    (
        act_ref, xhat_ref, slope_ref, a_ref, st_ref, mv_ref,
        wide_buf, w_buf, third, x_buf, act, xhat_buf, slope, sems,
    ) = rest[wt.count :]
    moves = Moves(sems)
    wide_copies = wide_wt.copies("out", place, wide_refs, wide_buf, moves)
    loads = [moves.tiles_of(x_ref, x_buf)]
    copies = wt.copies("in", place, refs, w_buf, moves)
    merge_wide(merge_norm, place, g, g_other, mv_ref)

    def each(rows, lanes, xhat, y, sg, carry):
        act[rows, :, lanes] = y.astype(BF16)
        xhat_buf[rows, :, lanes] = xhat.astype(BF16)
        slope[rows, :, lanes] = (sg + y * (1.0 - sg)).astype(BF16)
        return carry

    def after_tile(lanes, _):
        for buf, ref in ((act, act_ref), (xhat_buf, xhat_ref), (slope, slope_ref)):
            moves.store(buf.at[:, :, lanes], ref.at[:, :, lanes])

    wait_all(wide_copies)
    finish(mid, wide_buf, third, x_buf, loads, mv_ref, gb_ref, each, after_tile)
    wait_all(copies)
    first_matmul(act, w_buf, a_ref, st_ref)
    moves.finish()


def top_kernel(
    wide_wt, place, mid, x_ref, g, g_other, gb_ref, dy_ref, *rest,
):
    wide_refs, rest = rest[: wide_wt.count], rest[wide_wt.count :]
    (
        act_ref, xhat_ref, dz, keep_ref, send_ref, mv_ref,
        wide_buf, third, x_buf, dy, act, xhat_buf, sums_ref, sems,
    ) = rest
    moves = Moves(sems)
    wide_copies = wide_wt.copies("out", place, wide_refs, wide_buf, moves)
    loads = [moves.tiles_of(r, b) for r, b in ((x_ref, x_buf), (dy_ref, dy))]
    merge_wide(merge_norm, place, g, g_other, mv_ref)

    def each(rows, lanes, xhat, y, sg, carry):
        act[rows, :, lanes] = y.astype(BF16)
        xhat_buf[rows, :, lanes] = xhat.astype(BF16)
        d = dy[rows, :, lanes].astype(F32) * (sg + y * (1.0 - sg))
        dz[rows, :, lanes] = d.astype(BF16)
        return carry[0] + jnp.sum(d, axis=0), carry[1] + jnp.sum(d * xhat, axis=0)

    def after_tile(lanes, carry):
        for buf, ref in ((act, act_ref), (xhat_buf, xhat_ref)):
            moves.store(buf.at[:, :, lanes], ref.at[:, :, lanes])
        sums_ref[:, lanes] = sums_of(*carry)

    wait_all(wide_copies)
    finish(mid, wide_buf, third, x_buf, loads, mv_ref, gb_ref, each, after_tile)
    split_wide(place, sums_ref, keep_ref, send_ref)
    moves.finish()


class Shares:
    def __init__(self, kind, parts):
        self.kind, self.parts = kind, parts

    @property
    def count(self):
        return 2 if self.kind == "whole" else 4 * sum(1 for width in self.parts if width)

    def outs(self):
        if self.kind == "whole":
            width = sum(self.parts)
            return [((4, 2, 2, 16, width), BF16)] * 2
        return [((4, 2, 16, width), BF16) for width in self.parts if width for _ in range(4)]

    def buffers(self):
        return [pltpu.VMEM(shape, dtype) for shape, dtype in self.outs()]

    def store(self, place, out, first, result, zs=ALL):
        refs, bufs, moves = out

        def put(ref, buf, v, lanes):
            buf[zs, ..., lanes] = v
            moves.store(buf.at[zs, ..., lanes], ref.at[zs, ..., lanes])

        core, y, x = place[0], place[1], place[2]
        width = result.shape[1]
        parts = result.astype(BF16).reshape(-1, 2, 2, 2, 16, width)
        lower, upper = parts[:, :, :, 0], parts[:, :, :, 1]
        sides = [jnp.where(core == 0, lower, upper), jnp.where(core == 0, upper, lower)]
        if self.kind == "whole":
            for ref, buf, v in zip(refs, bufs, sides):
                put(ref, buf, v, pl.ds(first, width))
            return
        is_p = first < self.parts[0]
        start = first if is_p else first - self.parts[0]
        lanes = pl.ds(start, width)
        refs = refs[:4] if is_p else refs[-4:]
        bufs = bufs[:4] if is_p else bufs[-4:]
        for k, v in enumerate(sides):
            if is_p:
                two, at = (v[:, 0], v[:, 1]), y
            else:
                two, at = (v[:, :, 0], v[:, :, 1]), x
            put(refs[2 * k], bufs[2 * k], jnp.where(at == 0, two[0], two[1]), lanes)
            put(refs[2 * k + 1], bufs[2 * k + 1], jnp.where(at == 0, two[1], two[0]), lanes)


def wide_back_kernel(
    rows_total, wt, place, dz, xhat_ref, mv3_ref, g, g_other, gbo_ref, second_ref, mv2_ref, gb_ref, *rest
):
    refs = rest[: wt.count]
    dn2, stb_ref, d3_ref, s3_ref, buf, xhat, second, d3, lines, sems = rest[wt.count :]
    moves = Moves(sems)
    loads = moves.chunks_of(xhat_ref, xhat)
    copies = wt.copies("out", place, refs, buf, moves)
    second_load = moves.fetch(second_ref, second)
    merge_wide(merge_sums, place, g, g_other, s3_ref)
    own = own_lines(512)
    for lanes in TILES:
        lines[0, :, lanes] = lax.rsqrt(per_line(mv3_ref[4:7, lanes]) + EPS) * gbo_ref[0:1, lanes] * own
        lines[1, :, lanes] = per_line(s3_ref[0:3, lanes]) / rows_total
        lines[2, :, lanes] = per_line(s3_ref[4:7, lanes]) / rows_total
    for load, rows in zip(loads, CHUNKS):
        load.wait()
        for lanes in TILES:
            v = dz[rows, :, lanes].astype(F32) - lines[1, :, lanes][None]
            v = v - xhat[rows, :, lanes].astype(F32) * lines[2, :, lanes][None]
            d3[rows, :, lanes] = (lines[0, :, lanes][None] * v).astype(BF16)
    moves.store(d3, d3_ref)
    wait_all(copies)
    for j, lanes in enumerate(TILES):
        part = dot(flat(d3[:, :, lanes]), buf[j].reshape(512, 512)).reshape(PIX, LINE, 512)
        dn2[...] = part if j == 0 else dn2[...] + part
    second_load.wait()
    mean = per_line(mv2_ref[0:3])
    inv = lax.rsqrt(per_line(mv2_ref[4:7]) + EPS)
    gain, bias = gb_ref[2:3], gb_ref[3:4]

    def chunk(i, carry):
        rows = pl.ds(i * SIDE, SIDE)
        xh = (second[rows] - mean[None]) * inv[None]
        n2 = xh * gain[None] + bias[None]
        sg = sigmoid(n2)
        dn = dn2[rows] * (sg * (1.0 + n2 * (1.0 - sg)))
        dn2[rows] = dn
        return carry[0] + jnp.sum(dn, axis=0), carry[1] + jnp.sum(dn * xh, axis=0)

    zero = jnp.zeros((LINE, 512), F32)
    spread(sums_of(*chunks(chunk, (zero, zero))), stb_ref)
    moves.finish()


def wide_grad(sh, place, refs, start, d3, mid):
    for j in range(4):
        v = flat(d3[:, :, pl.ds(512 * j, 512)])
        res = dot_tn(v, flat(mid[...])).reshape(2, 2, 2, 4, 16, 512)
        for g in range(4):
            sh.store(place, refs, start + 512 * g, res[:, :, :, g].reshape(128, 512), slice(j, j + 1))


def middle_grad(sh, place, refs, start, d2, mixp):
    for tap in range(9):
        mixed = mixp[tap // 3 : tap // 3 + SIDE, tap % 3 : tap % 3 + SIDE].reshape(ROWS, 512)
        sh.store(place, refs, start + 512 * tap, dot_tn(flat(d2[...]), mixed))


def branch_grad(sh, place, refs, start, dlog, sq_ref, diff, dsq, patch):
    build_patches(flat(sq_ref[...]), patch)
    for j in range(3):
        pv = patch[:, :, :, pl.ds(768 * j, 768)].reshape(ROWS, 768)
        sh.store(place, refs, start + 128 + 768 * j, dot_tn(flat(dlog[...]), pv))
    sh.store(place, refs, start, dot_tn(flat(diff[...]), flat(dsq[...])))


def fetch_all(moves, refs, bufs):
    return [moves.fetch(r, b) for r, b in zip(refs, bufs)]


def branch_grad_kernel(sh, place, dlog, dsq, sq_ref, diff_ref, *rest):
    refs, (sq, diff, patch), bufs = rest[: sh.count], rest[sh.count : -1 - sh.count], rest[-1 - sh.count : -1]
    moves = Moves(rest[-1])
    wait_all(fetch_all(moves, (sq_ref, diff_ref), (sq, diff)))
    branch_grad(sh, place, (refs, bufs, moves), 0, dlog, sq, diff, dsq, patch)
    moves.finish()


def all_grad_kernel(sh, place, d2, dlog, dsq, d3_ref, mid_ref, mix_ref, sq_ref, diff_ref, *rest):
    refs, (d3, mid, mixp, sq, diff, patch) = rest[: sh.count], rest[sh.count : -1 - sh.count]
    bufs, moves = rest[-1 - sh.count : -1], Moves(rest[-1])
    out = (refs, bufs, moves)
    mix_load = moves.fetch(mix_ref, mixp)
    loads = fetch_all(moves, (sq_ref, diff_ref, d3_ref, mid_ref), (sq, diff, d3, mid))
    mix_load.wait()
    middle_grad(sh, place, out, 2432, d2, mixp)
    wait_all(loads)
    wide_grad(sh, place, out, 7040, d3, mid)
    branch_grad(sh, place, out, 0, dlog, sq, diff, dsq, patch)
    moves.finish()


def mixed_grad_kernel(sh, place, d3, mid_ref, d1, x_ref, *rest):
    refs, (mid, x), bufs = rest[: sh.count], rest[sh.count : -1 - sh.count], rest[-1 - sh.count : -1]
    moves = Moves(rest[-1])
    wait_all(fetch_all(moves, (mid_ref, x_ref), (mid, x)))
    wide_grad(sh, place, (refs, bufs, moves), 0, d3, mid)
    first_grad(sh, place, (refs, bufs, moves), 2048, d1, x)
    moves.finish()


def second_back_kernel(rows_total, sh, place, dn2, second_ref, mv2_ref, g, g_other, gb_ref, *rest):
    if sh is not None:
        mix_ref, refs, rest = rest[0], rest[1 : 1 + sh.count], rest[1 + sh.count :]
        d2, s2_ref, second, mixp, *bufs, sems = rest
    else:
        d2, s2_ref, second, sems = rest
    moves = Moves(sems)
    second_loads = moves.chunks_of(second_ref, second)
    if sh is not None:
        mix_load = moves.fetch(mix_ref, mixp)
    s2_ref[...] = merge_sums([g, g_other], OWN_ROWS)
    own = own_lines(512)
    mean2 = per_line(mv2_ref[0:3])
    inv2 = lax.rsqrt(per_line(mv2_ref[4:7]) + EPS)
    k2 = inv2 * gb_ref[2:3] * own
    dh2 = per_line(s2_ref[0:3]) / rows_total
    dg2 = per_line(s2_ref[4:7]) / rows_total
    for i, rows in enumerate(CHUNKS):
        second_loads[i].wait()
        xh = (second[rows] - mean2[None]) * inv2[None]
        d2[rows] = (k2[None] * (dn2[rows] - dh2[None] - xh * dg2[None])).astype(BF16)
    if sh is not None:
        mix_load.wait()
        middle_grad(sh, place, (refs, bufs, moves), 0, d2, mixp)
    moves.finish()


def middle_back_kernel(wt, place, d2, a_ref, mv1_ref, gb_ref, msk_ref, op_ref, *rest):
    refs = rest[: wt.count]
    (
        dn1, stb_ref, dlog, dsq_out,
        sq_buf, nf_buf, mid_buf, d2p, a, op, dmix, dsq, sems,
    ) = rest[wt.count :]
    moves = Moves(sems)
    mid_copies = wt.copies("mid", place, refs, mid_buf, moves)
    late_loads = [moves.fetch(a_ref, a), moves.fetch(op_ref, op)]
    nf_copies = wt.copies("nf", place, refs, nf_buf, moves)
    sq_copies = wt.copies("sq", place, refs, sq_buf, moves)
    clear_border(d2p)
    for i, rows in enumerate(CHUNKS):
        d2p[i + 1, 1:8] = d2[rows]
    wait_all(mid_copies)

    total = 0.0
    for k in range(9):
        y, x = 2 - k // 3, 2 - k % 3
        v = d2p[y : y + SIDE, x : x + SIDE].reshape(ROWS, 512)
        total = total + dot(v, mid_buf[..., pl.ds(512 * k, 512)].reshape(512, 512))
    dmix[...] = total.reshape(PIX, LINE, 512)
    wait_all(late_loads)
    mean1 = per_line(mv1_ref[0:3])
    inv1 = lax.rsqrt(per_line(mv1_ref[4:7]) + EPS)
    gain1, bias1 = gb_ref[0:1], gb_ref[1:2]

    def log_chunk(i, c):
        rows = pl.ds(i * SIDE, SIDE)
        n1 = (a[rows] - mean1[None]) * inv1[None] * gain1[None] + bias1[None]
        h = n1 * sigmoid(n1)
        o = op[rows].astype(F32)
        dlog[rows] = (dmix[rows] * h * o * (1.0 - o)).astype(BF16)
        return c

    chunks(log_chunk)
    wait_all(nf_copies)
    dsq[...] = jnp.zeros(dsq.shape, F32)
    for k in (1, 2):
        for ty in range(3):
            w = nf_buf[..., pl.ds(((k - 1) * 9 + ty * 3) * 128, 384)].reshape(512, 384)
            res = dot(flat(dlog[...]), w).reshape(SIDE, SIDE, LINE, 384)
            for tx in range(3):
                dy, dx = k * (ty - 1), k * (tx - 1)
                (y0, y1), (x0, x1) = tap_ranges(dy), tap_ranges(dx)
                dsq[y0 + dy : y1 + dy, x0 + dx : x1 + dx] += res[
                    y0:y1, x0:x1, :, 128 * tx : 128 * tx + 128
                ]
    dsq_low = dsq[...].astype(BF16).reshape(ROWS, 128)
    dsq_out[...] = dsq_low.reshape(PIX, LINE, 128)
    wait_all(sq_copies)
    dn1[...] = dot_nt(dsq_low, sq_buf[...].reshape(512, 128)).reshape(PIX, LINE, 512)
    m = msk_ref[:, 0:1]

    def last_chunk(i, carry):
        rows = pl.ds(i * SIDE, SIDE)
        xh = (a[rows] - mean1[None]) * inv1[None]
        n1 = xh * gain1[None] + bias1[None]
        sg = sigmoid(n1)
        e = dn1[rows] * m[None]
        o = op[rows].astype(F32)
        dhid = dmix[rows] * (0.5 + o) - e + pltpu.roll(e, 1, 1)
        dn = dhid * (sg * (1.0 + n1 * (1.0 - sg)))
        dn1[rows] = dn
        return carry[0] + jnp.sum(dn, axis=0), carry[1] + jnp.sum(dn * xh, axis=0)

    zero = jnp.zeros((LINE, 512), F32)
    spread(sums_of(*chunks(last_chunk, (zero, zero))), stb_ref)


def first_d1(rows_total, place, loads, dn1, dn1_other, a, mv1_ref, s1_ref, gb_ref, d1):
    own = own_lines(512)
    r = line_of(512)
    first = ((r == 0) | (r == 5) | (r == 10)) & (place[0] == 1)
    mean = per_line(mv1_ref[0:3])
    inv = lax.rsqrt(per_line(mv1_ref[4:7]) + EPS)
    k = inv * gb_ref[0:1] * own
    dh = per_line(s1_ref[0:3]) / rows_total
    dg = per_line(s1_ref[4:7]) / rows_total
    for i, rows in enumerate(CHUNKS):
        loads[i].wait()
        xh = (a[rows] - mean[None]) * inv[None]
        dn = dn1[rows] + jnp.where(first[None], pltpu.roll(dn1_other[rows], LINE - 4, 1), 0.0)
        d1[rows] = (k[None] * (dn - dh[None] - xh * dg[None])).astype(BF16)


def first_back_kernel(
    rows_total, wt, place, dn1, other, a_ref, mv1_ref, g, g_other, gb_ref, dz_ref, slope_ref, xhat_ref, *rest
):
    refs = rest[: wt.count]
    (
        dx_ref, d1, s1_ref, below, keep_ref, send_ref,
        w_buf, a, dz, slope, xhat, dx, sums_ref, sems,
    ) = rest[wt.count :]
    moves = Moves(sems)
    loads = moves.chunks_of(a_ref, a)
    copies = wt.copies("in", place, refs, w_buf, moves)
    tiles = [moves.tiles_of(r, b) for r, b in ((dz_ref, dz), (slope_ref, slope), (xhat_ref, xhat))]
    s1_ref[...] = merge_sums([g, g_other], OWN_ROWS)
    first_d1(rows_total, place, loads, dn1, other, a, mv1_ref, s1_ref, gb_ref, d1)
    wait_all(copies)
    for j, lanes in enumerate(TILES):
        wait_all([load[j] for load in tiles])
        w = w_buf[..., lanes].reshape(512, 512)
        v = dot(flat(d1[...]), w).reshape(PIX, LINE, 512) + dz[:, :, lanes].astype(F32)
        low = v.astype(BF16)
        dx[:, :, lanes] = low
        d = low.astype(F32) * slope[:, :, lanes].astype(F32)
        below[:, :, lanes] = d.astype(BF16)
        moves.store(dx.at[:, :, lanes], dx_ref.at[:, :, lanes])
        sums_ref[:, lanes] = sums_of(
            jnp.sum(d, axis=0), jnp.sum(d * xhat[:, :, lanes].astype(F32), axis=0)
        )
    split_wide(place, sums_ref, keep_ref, send_ref)
    moves.finish()


def first_grad(sh, place, out, start, d1, x_ref):
    for j in range(4):
        x = flat(x_ref[:, :, pl.ds(512 * j, 512)])
        sh.store(place, out, start + 512 * j, dot_tn(flat(d1[...]), x))


def last_grad_kernel(rows_total, sh, place, dn1, other, a_ref, mv1_ref, g, g_other, gb_ref, x_ref, *rest):
    refs, rest = rest[: sh.count], rest[sh.count :]
    d1, s1_ref, a, x, *bufs, sems = rest
    moves = Moves(sems)
    loads = moves.chunks_of(a_ref, a)
    x_load = moves.fetch(x_ref, x)
    s1_ref[...] = merge_sums([g, g_other], OWN_ROWS)
    first_d1(rows_total, place, loads, dn1, other, a, mv1_ref, s1_ref, gb_ref, d1)
    x_load.wait()
    first_grad(sh, place, (refs, bufs, moves), 0, d1, x)
    moves.finish()


def last_back_kernel(wt, place, d1, dz_ref, *rest):
    refs, (dx_ref, w_buf, dz, dx, sems) = rest[: wt.count], rest[wt.count :]
    moves = Moves(sems)
    copies = wt.copies("in", place, refs, w_buf, moves)
    loads = moves.tiles_of(dz_ref, dz)
    wait_all(copies)
    for j, lanes in enumerate(TILES):
        loads[j].wait()
        w = w_buf[..., lanes].reshape(512, 512)
        v = dot(flat(d1[...]), w).reshape(PIX, LINE, 512) + dz[:, :, lanes].astype(F32)
        dx[:, :, lanes] = v.astype(BF16)
        moves.store(dx.at[:, :, lanes], dx_ref.at[:, :, lanes])
    moves.finish()


VM = pl.BlockSpec(memory_space=pltpu.VMEM)
HB = pl.BlockSpec(memory_space=pltpu.HBM)
SM = pl.BlockSpec(memory_space=pltpu.SMEM)
AN = pl.BlockSpec(memory_space=pl.ANY)


class Near:
    def __init__(self, value):
        self.value = value


class Near2(Near):
    pass


def is_big(shape):
    return len(shape) >= 4 or (len(shape) == 3 and shape[0] in (PIX, 3))


def size_of(shape, dtype):
    size = jnp.dtype(dtype).itemsize
    for k in shape:
        size *= k
    return size


def call(kernel, outs, scratch=(), us=5):
    def run(place, *values):
        specs = [SM]
        need = 6 * 1024 * 1024
        need += sum(size_of(v.shape, v.dtype) for v in scratch)
        need += sum(size_of(*o[:2]) for o in outs if not (is_big(o[0]) and len(o) == 2))
        for v in values:
            u = v.value if isinstance(v, Near) else v
            if not is_big(u.shape) or (isinstance(v, Near) and not isinstance(v, Near2)):
                need += size_of(u.shape, u.dtype)
        for v in values:
            if isinstance(v, Near):
                specs.append(AN if isinstance(v, Near2) else VM)
            else:
                specs.append(HB if is_big(v.shape) else VM)
        return pl.pallas_call(
            kernel,
            in_specs=specs,
            out_specs=tuple(HB if is_big(o[0]) and len(o) == 2 else VM for o in outs),
            out_shape=tuple(jax.ShapeDtypeStruct(o[0], o[1]) for o in outs),
            scratch_shapes=list(scratch) + [pltpu.SemaphoreType.DMA((96,))],
            compiler_params=pltpu.CompilerParams(vmem_limit_bytes=52 * 1024 * 1024),
            cost_estimate=pl.CostEstimate(flops=us * 10**9, bytes_accessed=us * 3 * 10**6, transcendentals=0),
        )(place, *[v.value if isinstance(v, Near) else v for v in values])

    return run


def near(width, dtype):
    return ((PIX, LINE, width), dtype, True)


def pm(width, dtype):
    return ((PIX, LINE, width), dtype)


def buf(width, dtype):
    return pltpu.VMEM((PIX, LINE, width), dtype)


def wbuf(width):
    return pltpu.VMEM((4, 2, 2, 2, 16, width), BF16)


STAT = ((8, 512), F32)
WIDE_STAT = ((8, 2048), F32)
PAIR = [(0, 1), (1, 0)]


class Links:
    def __init__(self, dp, core):
        self.dp, self.core = dp, core
        self.at = lax.axis_index("dp")

    def bit(self, k):
        return (self.at // k) % 2

    def place(self):
        y, x = (self.bit(2), self.bit(1)) if self.split else (0, 0)
        return jnp.stack([self.core, jnp.int32(y), jnp.int32(x)]).astype(jnp.int32)

    split = True

    def swap(self, v):
        return lax.ppermute(v, "pipe", PAIR)

    def across(self, v, k):
        return lax.ppermute(v, "dp", [(i, i ^ k) for i in range(self.dp)])

    def to_all(self, spread, *meanwhile):
        g = lax.all_to_all(spread, "dp", 0, 0)
        if meanwhile:
            g = after(g, *meanwhile)
        return g, self.swap(g)

    def by_core(self, own, other):
        first = self.core == 0
        return jnp.where(first, own, other), jnp.where(first, other, own)

    def in_order(self, which, own, other, axis):
        pair = jnp.where(which == 0, jnp.stack([own, other], axis), jnp.stack([other, own], axis))
        return pair

    def halves(self, piece):
        two = piece.reshape(2, 16, piece.shape[1])
        keep = lax.dynamic_index_in_dim(two, self.core, 0, keepdims=False)
        recv = self.swap(lax.dynamic_index_in_dim(two, 1 - self.core, 0, keepdims=False))
        return self.by_core(keep, recv)

    def gather_first(self, v, cut):
        p, q = v[..., :cut], v[..., cut:]
        p_other, q_other = self.across(p, 1), self.across(q, 2)
        return self.in_order(self.bit(1), p, p_other, 1), self.in_order(self.bit(2), q, q_other, 1)

    def gather_second(self, p, q):
        mine = (p, self.across(p, 2), q, self.across(q, 1))
        return mine + tuple(self.swap(v) for v in mine)

    def gather_whole(self, own):
        return lax.all_gather(own, "dp").reshape(4, 2, 2, 16, -1)

    def gather_blocks(self, gains, inner, rest, wide, permute, clips, cotangent):
        rows = jnp.concatenate([jnp.pad(v, ((0, 0), (0, 128 - v.shape[1]))) for v in gains], axis=0)
        tail = jnp.pad(rows, ((0, 32 - rows.shape[0]), (0, 0)))
        a = self.halves(jnp.concatenate([inner, tail], axis=1))
        b, c = self.halves(rest), self.halves(self.narrow_rows(wide))
        b0 = self.gather_whole(b[0])
        v = after(a[0], b[0])
        v = self.in_order(self.bit(8), v, self.across(v, 8), 0)
        x = permute(after(clips, v, b[0]))
        moved = after(self.across(v, 4), x)
        v = self.in_order(self.bit(4), v, moved, 1).reshape(4, 16, -1)
        ca = jnp.concatenate([c[0], a[1]], axis=1)
        ca = self.in_order(self.bit(8), ca, self.across(after(ca, v), 8), 0)
        dy = permute(after(cotangent, v))
        moved = after(self.across(ca, 4), dy)
        ca = self.in_order(self.bit(4), ca, moved, 1).reshape(4, 16, -1)
        a0 = self.gather_second(*self.gather_first(v, 1024))
        block_0 = {"A": (Weights("split", SPLIT_A), a0)}
        return (block_0, (ca, b0, jnp.concatenate([c[1], b[1]], axis=1))), x, dy

    def gather_middle(self, blocks, pieces, then):
        block_0, (_, b0, bc) = blocks
        ca = self.gather_second(*pieces)
        block_0["C"] = (Weights("split", SPLIT_C), ca)
        b0 = after(b0, then)
        block_0["B"] = (Weights("whole", middle_at(0)), (b0, self.swap(b0)))
        return block_0, (ca, self.gather_whole(after(bc, b0)))

    def gather_last(self, blocks, third):
        block_0, (ca, bc) = blocks
        bc = after(bc, third)
        bc = (bc, self.swap(bc))
        return block_0, {
            "A": (Weights("split", SPLIT_A1), ca),
            "B": (Weights("whole", middle_at(2048)), bc),
            "C": (Weights("whole", wide_at(0)), bc),
        }

    def gains_of(self, group, place):
        wt, refs = group
        return call(functools.partial(gains_kernel, wt), [STAT, WIDE_STAT], [wbuf(128)])(place, *refs)

    def add(self, a, b):
        return (a.astype(F32) + b.astype(F32)).astype(BF16)

    def halve(self, v, axis, k, then=None):
        which = self.bit(k)
        keep = lax.dynamic_index_in_dim(v, which, axis, keepdims=False)
        send = lax.dynamic_index_in_dim(v, 1 - which, axis, keepdims=False)
        moved = self.across(send, k)
        if then is not None:
            moved = after(moved, then)
        return self.add(keep, moved)

    def scatter_first(self, g):
        return [self.add(g[k], self.swap(g[k + 2])) for k in (1, 5)]

    def scatter_xy(self, g, sent, then=(None, None)):
        done = []
        for own, send_own, other, k in ((g[0], g[2], sent[0], 2), (g[4], g[6], sent[1], 1)):
            moved = self.across(other, k)
            if then[0] is not None:
                moved = after(moved, then[0])
            v = self.add(self.add(own, self.swap(send_own)), moved)
            done.append(self.halve(v, 1, 3 - k, then[1]))
        return jnp.concatenate(done, axis=-1)

    def scatter_z(self, v, then=(None, None)):
        half = self.halve(v.reshape(2, 2, 16, -1), 1, 4, then[0])
        return self.halve(half, 0, 8, then[1]), half

    def half_sums(self, keep, send):
        return self.add(keep, self.swap(send)).reshape(16, 16, -1)

    def scatter_whole(self, v):
        return lax.psum_scatter(v, "dp", scatter_dimension=0, tiled=True)[0]

    def scatter_at_once(self, v, *then):
        v = lax.all_to_all(v, "dp", 0, 0)
        if then:
            v = after(v, *then)
        return jnp.sum(v.astype(F32), axis=0)

    def handed(self, early, late):
        return lax.ppermute(early, "pipe", [(1, 0)]), lax.ppermute(late, "pipe", [(0, 1)])

    def to_owner(self, early, early_other, late, late_other):
        at_0 = jnp.concatenate([early, early_other], axis=0).astype(F32)
        at_1 = jnp.concatenate([late_other, late], axis=0).astype(F32)
        return jnp.where(self.core == 0, at_0, at_1)

    def wide_rows(self, v):
        return v.reshape(2, 16, 4, -1).transpose(0, 2, 1, 3).reshape(128, -1)

    def narrow_rows(self, v):
        return v.reshape(2, 4, 16, -1).transpose(0, 2, 1, 3).reshape(32, -1)


class AnyLinks(Links):
    split = False

    def gather_blocks(self, gains, inner, rest, wide, permute, clips, cotangent):
        full = [lax.all_gather(v, "dp", tiled=True) for v in (inner, wide, rest)]
        full[1] = jnp.stack([self.narrow_rows(f) for f in full[1].reshape(16, 128, -1)]).reshape(512, -1)
        own = jnp.concatenate(full, axis=1)
        vectors = [lax.all_gather(v, "dp", axis=1, tiled=True).astype(F32) for v in gains]
        mid = jnp.pad(jnp.concatenate(vectors[:4]), ((0, 4), (0, 0)))
        out = jnp.pad(jnp.concatenate(vectors[4:]), ((0, 6), (0, 0)))
        mids, outs = self.by_core(mid, self.swap(mid)), self.by_core(out, self.swap(out))
        blocks = []
        for s, full in enumerate(self.by_core(own, self.swap(own))):
            parts = full.reshape(16, 2, 16, -1)
            mine = lax.dynamic_index_in_dim(parts, self.core, 1, keepdims=False)
            theirs = lax.dynamic_index_in_dim(parts, 1 - self.core, 1, keepdims=False)
            refs = tuple(v.reshape(4, 2, 2, 16, -1) for v in (mine, theirs))
            groups = (("A", {"in": [("W", 0, 0, 2048)]}), ("B", middle_at(4096)), ("C", wide_at(2048)))
            blocks.append({k: (Weights("whole", v), refs) for k, v in groups})
            blocks[s]["gains"] = (mids[s], outs[s])
        return blocks, permute(clips), permute(cotangent)

    def gather_middle(self, blocks, pieces, then):
        return blocks

    def gather_last(self, blocks, third):
        return blocks

    def gains_of(self, group, place):
        return group

    def scatter_pairs(self, early, late, wide):
        full = []
        for keep, send in (early, late):
            half = self.add(keep, self.swap(send)).reshape(16, 16, -1)
            full.append(jnp.stack(self.by_core(half, self.swap(half)), axis=1))
        total = jnp.where(self.core == 0, full[0], full[1])
        if wide:
            total = jnp.stack([self.wide_rows(v.reshape(32, -1)) for v in total])
        total = total.reshape(-1, total.shape[-1])
        return lax.psum_scatter(total, "dp", scatter_dimension=0, tiled=True).astype(F32)


def after(v, *others):
    return lax.optimization_barrier((v, others))[0]


SPLIT_A = {"in": [("P", 0, 0, 1024), ("Q", 0, 1024, 1024)], "gain": [("Q", 1024, 0, 128)]}
SPLIT_C = {"out": [("P", 512 * g, (g,), 512) for g in range(4)]}
SPLIT_A1 = {"in": [("Q", 0, 0, 2048)], "gain": [("Q", 2048, 0, 128)]}


def middle_at(first):
    return {
        "sq": [("W", first, 0, 128)],
        "nf": [("W", first + 128, 0, 2304)],
        "mid": [("W", first + 2432, 0, 4608)],
    }


def wide_at(first):
    return {"out": [("W", first + 512 * g, (g,), 512) for g in range(4)]}


def local(
    clips_in, cotangent, segment_ids, w_in, w_squeeze, w_near, w_far, w_mid, w_out,
    gain_mid, bias_mid, gain_out, bias_out,
):
    dp = lax.axis_size("dp")
    core = lax.axis_index("pipe")
    links = (Links if dp == 16 else AnyLinks)(dp, core)
    place = links.place()
    rows_total = float(clips_in.shape[1] * dp)

    def low(v):
        return v[0].astype(BF16)

    n = w_in.shape[2]
    gain_rows = [low(gain_mid)[0:1], low(bias_mid)[0:1], low(gain_mid)[1:2], low(bias_mid)[1:2]]
    def permute(v):
        scratch = [pltpu.VMEM((3, SEG * PIX, 2048), BF16), buf(2048, BF16)]
        return call(permute_kernel, [pm(2048, BF16)], scratch)(place, v)[0]

    gathered, x0, dy = links.gather_blocks(
        gain_rows + [low(gain_out)[None], low(bias_out)[None]],
        low(w_in).T,
        jnp.concatenate([low(w_squeeze), low(w_near).T, low(w_far).T, low(w_mid).T], axis=1),
        low(w_out).T,
        permute, clips_in, cotangent,
    )

    def gains_of(s):
        return links.gains_of(gathered[s]["A" if links.split else "gains"], place)

    gains = [gains_of(0)]

    same = (segment_ids[:, 0, 1:] == segment_ids[:, 0, :-1]).astype(F32)
    same = jnp.concatenate([same, jnp.zeros((3, 1), F32)], axis=1)
    mine_seg = lax.dynamic_slice_in_dim(same, core * HALF, HALF, 1)
    msk = jnp.concatenate([mine_seg, jnp.zeros((3, 1), F32)], axis=1).reshape(15)
    msk = jnp.broadcast_to(jnp.concatenate([msk, jnp.zeros((1,), F32)])[:, None], (LINE, 128))


    wide_buf = pltpu.VMEM((4, 2, 2, 2, 4, 16, 512), BF16)

    stb = ((dp, 8, 384), F32)
    half_stat = ((8, 1024), F32)
    buffers = {"in": wbuf(2048), "sq": wbuf(128), "nf": wbuf(2304), "mid": wbuf(4608), "out": wide_buf}
    groups = {"A": ("in",), "B": ("sq", "nf", "mid"), "C": ("out",)}

    def kernel(body, group, values, outs, scratch, *static):
        wt, refs = group[1]
        names = groups[group[0]]
        refs = [Near2(v) if names == ("out",) and wt.kind == "split" else v for v in refs]
        return call(functools.partial(body, *static, wt), outs, [buffers[k] for k in names] + scratch)(
            place, *values, *refs
        )

    def group(s, k):
        return k, gathered[s][k]

    wide_sums = pltpu.VMEM((8, 2048), F32)
    lines = pltpu.VMEM((3, LINE, 2048), F32)
    padded = pltpu.VMEM((9, 9, LINE, 512), BF16)
    patch = pltpu.VMEM((SIDE, SIDE, LINE, 2304), BF16)

    def first(s, x):
        return kernel(first_kernel, group(s, "A"), [Near(x)], [near(512, F32), stb], [])

    def middle(s, a, other, *values):
        outs = [pm(512, F32), pm(512, BF16), pm(128, BF16), pm(512, BF16),
                ((9, 9, LINE, 512), BF16), near(512, F32), pm(512, F32), stb, STAT]
        scratch = [buf(512, F32), buf(512, BF16), buf(128, BF16), buf(512, BF16), padded, buf(512, F32), patch]
        return kernel(middle_kernel, group(s, "B"), [Near(a), Near(other), *values], outs, scratch)

    def widen(s, second, *values):
        outs = [pm(512, BF16), half_stat, half_stat, STAT]
        scratch = [buf(512, BF16), buf(512, F32), wide_sums]
        return kernel(wide_kernel, group(s, "C"), [Near(second), *values], outs, scratch)

    def turn(mid, *values):
        outs = [pm(2048, BF16)] * 3 + [near(512, F32), stb, WIDE_STAT]
        wide_wt, wide_refs = gathered[0]["C"]
        scratch = [buf(512, F32)] + [buf(2048, BF16)] * 4
        wt, refs = gathered[1]["A"]
        return call(
            functools.partial(turn_kernel, wide_wt, wt), outs, [wide_buf, buffers["in"]] + scratch
        )(place, Near(mid), *values, *[Near2(v) for v in wide_refs], *refs)

    def top(mid, *values):
        outs = [pm(2048, BF16)] * 2 + [near(2048, BF16), half_stat, half_stat, WIDE_STAT]
        wide_wt, wide_refs = gathered[1]["C"]
        scratch = [wide_buf, buf(512, F32)] + [buf(2048, BF16)] * 4 + [wide_sums]
        return call(functools.partial(top_kernel, wide_wt), outs, scratch)(
            place, Near(mid), *values, *wide_refs
        )

    def pairs(norm, keep, send, *meanwhile):
        recv = links.swap(send)
        v = pl.pallas_call(
            functools.partial(pair_kernel, norm), in_specs=[VM, VM], out_specs=VM,
            out_shape=jax.ShapeDtypeStruct((dp, 8, 768), F32),
            compiler_params=pltpu.CompilerParams(vmem_limit_bytes=8 * 1024 * 1024),
        )(keep, recv)
        return links.to_all(v, *meanwhile)

    def wide_back(s, dz, *values):
        outs = [near(512, F32), stb, pm(2048, BF16), WIDE_STAT]
        scratch = [buf(2048, BF16), buf(512, F32), buf(2048, BF16), lines]
        return kernel(wide_back_kernel, group(s, "C"), [Near(dz), *values], outs, scratch, rows_total)

    def second_back(sh, dn2, *values):
        outs = [near(512, BF16), STAT]
        scratch = [buf(512, F32)]
        if sh:
            outs, scratch = sh.outs() + outs, scratch + [padded] + sh.buffers()
        return call(functools.partial(second_back_kernel, rows_total, sh), outs, scratch)(
            place, Near(dn2), *values
        )

    def middle_back(s, d2, *values):
        outs = [near(512, F32), stb, near(512, BF16), near(128, BF16)]
        scratch = [padded, buf(512, F32), buf(512, BF16), buf(512, F32), pltpu.VMEM((SIDE, SIDE, LINE, 128), F32)]
        return kernel(middle_back_kernel, group(s, "B"), [Near(d2), *values], outs, scratch)

    def first_back(dn1, other, *values):
        outs = [pm(2048, BF16), near(512, BF16), STAT, near(2048, BF16), half_stat, half_stat]
        scratch = [buf(512, F32)] + [buf(2048, BF16)] * 4 + [wide_sums]
        return kernel(
            first_back_kernel, group(1, "A"), [Near(dn1), Near(other), *values], outs, scratch, rows_total
        )

    def last_grad(sh, dn1, other, *values):
        scratch = [buf(512, F32), buf(2048, BF16)] + sh.buffers()
        return call(
            functools.partial(last_grad_kernel, rows_total, sh), sh.outs() + [near(512, BF16), STAT], scratch
        )(place, Near(dn1), Near(other), *values)

    def last_back(d1, *values):
        scratch = [buf(2048, BF16), buf(2048, BF16)]
        return kernel(last_back_kernel, group(0, "A"), [Near(d1), *values], [pm(2048, BF16)], scratch)[0]

    def shares_of(kind, *parts):
        return Shares(kind if links.split else "whole", parts)

    def grad(body, sh, values, *scratch):
        bufs = [pltpu.VMEM(v.shape, v.dtype) for v in values if not isinstance(v, Near)]
        return call(
            functools.partial(body, sh), sh.outs(), bufs + list(scratch) + sh.buffers()
        )(place, *values)

    restore = call(
        restore_kernel, [((3, SEG * PIX, 2048), BF16)],
        [pltpu.VMEM((2, PIX, LINE, 2048), BF16), pltpu.VMEM((3, SEG * PIX, 2048), BF16)],
    )

    def crossed(early, late):
        return lax.ppermute(early, "pipe", [(1, 0)]), lax.ppermute(late, "pipe", [(0, 1)])

    kept = []
    x = x0
    if links.split:
        x = after(x, gathered[1][0])
    a, st = first(0, x)
    for s in range(2):
        gb, gbo = gains[s]
        if s == 0:
            pieces = links.gather_first(after(gathered[1][0], a), 2048) if links.split else ()
            sums = links.to_all(st, dy, *pieces, gb)
            gathered = links.gather_middle(gathered, pieces, sums[0])
        else:
            sums = links.to_all(st, gb)
        a, diff, sq, op, mix, second, second_far, st, mv1 = middle(s, a, links.swap(a), *sums, gb, msk)
        mid, keep, send, mv2 = widen(s, second, *links.to_all(st), gb)
        stats = pairs(True, keep, send)
        if s == 0:
            if links.split:
                gathered = (gathered[0], {"A": (Weights("split", SPLIT_A1), gathered[1][0])}, gathered[1])
                gains.append(gains_of(1))
            act0, xhat, slope0, a_next, st, mv3 = turn(mid, x, *stats, gbo)
            if links.split:
                gathered = links.gather_last((gathered[0], gathered[2]), a_next)
            else:
                gains.append(gains_of(1))
        else:
            act1, xhat, dz, keep, send, mv3 = top(mid, x, *stats, gbo, dy)
        kept.append((x, a, mv1, diff, sq, op, mix, second_far, mv2, mid, xhat, mv3))
        if s == 0:
            x, a = act0, a_next

    gb, gbo = gains[1]
    x, a, mv1, diff, sq, op, mix, second, mv2, mid, xhat, mv3 = kept[1]
    dn2, st, d3, s3 = wide_back(
        1, dz, xhat, mv3, *pairs(False, keep, send), gbo, second, mv2, gb
    )
    d2, s2 = second_back(None, dn2, second, mv2, *links.to_all(st), gb)
    dn1, st, dlog, dsq = middle_back(1, d2, a, mv1, gb, msk, op)
    g_rest = grad(
        all_grad_kernel, shares_of("whole", 2432, 4608, 2048),
        [Near(d2), Near(dlog), Near(dsq), d3, mid, mix, sq, diff], patch,
    )
    split = links.split
    sums = links.to_all(st, *g_rest)
    dn1_other = links.swap(dn1)
    dx1, d1_late, s1, dz, keep, send = first_back(
        dn1, dn1_other, a, mv1, *sums, gb, dz, slope0, kept[0][10]
    )
    meanwhile = []
    if split:
        recv = after(links.swap(after(g_rest[1], sums[1], dn1_other)), dx1)
        late = links.add(g_rest[0], recv).reshape(16, 16, -1)
        keep = after(keep, late)
        late = links.scatter_whole(late)
    norms_1 = (s1, s2, s3)
    x_late = x

    gb, gbo = gains[0]
    x, a, mv1, diff, sq, op, mix, second, mv2, mid, xhat, mv3 = kept[0]
    dn2, st, d3, s3 = wide_back(
        0, dz, xhat, mv3, *pairs(False, keep, send, *meanwhile), gbo, second, mv2, gb
    )
    g_mixed = grad(
        mixed_grad_kernel, shares_of("whole", 4096), [Near(d3), mid, Near(d1_late), x_late]
    )
    sums = links.to_all(st, *g_mixed)
    mixed_sums = sums
    *g_mid, d2, s2 = second_back(shares_of("split", 2048, 2560), dn2, second, mv2, *sums, gb, mix)
    dn1, st, dlog, dsq = middle_back(0, d2, a, mv1, gb, msk, op)
    if split:
        sent = links.scatter_first(g_mid)
        mixed = links.half_sums(g_mixed[0], after(g_mixed[1], mixed_sums[1]))
        dlog = after(dlog, mixed, *sent)
        mixed = links.scatter_whole(mixed)
    g_branch = grad(branch_grad_kernel, shares_of("whole", 2432), [Near(dlog), Near(dsq), sq, diff], patch)
    meanwhile = g_branch
    if split:
        rest_0 = [links.half_sums(*g_branch)]
    *g_in, d1, s1 = last_grad(
        shares_of("whole", 2048), dn1, links.swap(dn1), a, mv1, *links.to_all(st, *meanwhile), gb, x
    )
    norms_0 = (s1, s2, s3)
    if split:
        last = jnp.concatenate([links.half_sums(*g_in), *rest_0], axis=-1)
        dx0 = last_back(after(d1, last), dz)
        act0, act1, dx1 = after((act0, act1, dx1), last)
        early = links.scatter_xy(g_mid, sent, (d1, None))
        activations = restore(place, act0, act1, *crossed(act0, act1))[0]
        last = links.scatter_at_once(last, activations)
        input_grads = restore(place, after(dx0, last), dx1, *crossed(dx0, dx1))[0]
        mid_0, _ = links.scatter_z(early, (activations, input_grads))
        in_0, branch_0 = jnp.split(last, [2048], axis=-1)
        mixed = after(mixed, late)
        out_0, in_1 = jnp.split(mixed, 2, axis=-1)
        branch_1, mid_1, out_1 = jnp.split(late, [2432, 7040], axis=-1)
        mid_other, late_other = links.handed(mid_0, late)
        branch_1o, mid_1o, out_1o = jnp.split(late_other, [2432, 7040], axis=-1)
        out_0o, in_1o = links.handed(out_0, in_1)
        in_0o, branch_0o = jnp.split(lax.ppermute(last, "pipe", [(1, 0)]), [2048], axis=-1)
        f_in = links.to_owner(in_0, in_0o, in_1, in_1o)
        f_branch = links.to_owner(branch_0, branch_0o, branch_1, branch_1o)
        f_mid = links.to_owner(mid_0, mid_other, mid_1, mid_1o)
        f_out = links.wide_rows(links.to_owner(out_0, out_0o, out_1, out_1o))
    else:
        activations = restore(place, act0, act1, *crossed(act0, act1))[0]
        dx0 = last_back(d1, dz)
        input_grads = restore(place, dx0, dx1, *crossed(dx0, dx1))[0]
        rest = [v[..., :2432] for v in g_rest], [v[..., 2432:7040] for v in g_rest], [v[..., 7040:] for v in g_rest]
        f_branch = links.scatter_pairs(g_branch, rest[0], False)
        f_mid = links.scatter_pairs(g_mid, rest[1], False)
        g_out, in_1 = [v[..., :2048] for v in g_mixed], [v[..., 2048:] for v in g_mixed]
        f_out = links.scatter_pairs(g_out, rest[2], True)
        f_in = links.scatter_pairs(g_in, in_1, False)

    grad_w_in = f_in.T[None]
    grad_w_squeeze = f_branch[:, :128][None]
    grad_w_near = f_branch[:, 128:1280].T[None]
    grad_w_far = f_branch[:, 1280:].T[None]
    grad_w_mid = f_mid.T[None]
    grad_w_out = f_out.T[None]

    s1, s2, s3 = [jnp.where(core == 0, e, l) for e, l in zip(norms_0, norms_1)]
    dp_index = lax.axis_index("dp")
    mid_sums = jnp.stack(
        [jnp.stack([s1[0:3].sum(0), s2[0:3].sum(0)]), jnp.stack([s1[4:7].sum(0), s2[4:7].sum(0)])]
    )
    mid_sums = lax.dynamic_slice_in_dim(mid_sums, dp_index * n, n, 2)
    out_sums = jnp.stack([s3[0:3].sum(0), s3[4:7].sum(0)])
    out_sums = lax.dynamic_slice_in_dim(out_sums, dp_index * 4 * n, 4 * n, 1)
    return (
        activations[None], input_grads[None], grad_w_in, grad_w_squeeze, grad_w_near, grad_w_far,
        grad_w_mid, grad_w_out, mid_sums[1][None], mid_sums[0][None], out_sums[1][None],
        out_sums[0][None],
    )


def solution(mesh):
    split = P("pipe", None, "dp")
    rows = P("pipe", "dp", None)
    vec = P("pipe", "dp")
    clips = P(None, "dp", None)
    weights = (split, rows, split, split, split, split, split, split, vec, vec)
    whole = P("pipe", None, "dp", None)
    return jax.shard_map(
        local,
        mesh=mesh,
        in_specs=(clips, clips, clips) + weights,
        out_specs=(whole, whole) + weights,
        check_vma=False,
    )
```

```python
import functools

import jax
import jax.numpy as jnp
from jax import lax
from jax.experimental import pallas as pl
from jax.experimental.pallas import tpu as pltpu
from jax.sharding import PartitionSpec as P

SEG = 8
SIDE = 7
PIX = SIDE * SIDE
HALF = SEG // 2
STRIDE = HALF + 1
LINE = 16
ROWS = PIX * LINE
EPS = 1e-05
F32 = jnp.float32
BF16 = jnp.bfloat16
VMEM_BYTES = 36 * 1024 * 1024


def dot(left, right):
    return lax.dot_general(left, right, (((1,), (0,)), ((), ())), preferred_element_type=F32)


def dot_nt(left, right):
    return lax.dot_general(left, right, (((1,), (1,)), ((), ())), preferred_element_type=F32)


def dot_tn(left, right):
    return lax.dot_general(left, right, (((0,), (0,)), ((), ())), preferred_element_type=F32)


def sigmoid(v):
    return 0.5 * jnp.tanh(0.5 * v) + 0.5


def line_of(width):
    return lax.broadcasted_iota(jnp.int32, (LINE, width), 0)


def own_lines(width):
    r = line_of(width)
    inside = (r < 4) | ((r >= 5) & (r < 9)) | ((r >= 10) & (r < 14))
    return inside.astype(F32)


def per_line(values):
    width = values.shape[1]
    r = line_of(width)
    return jnp.where(r < 5, values[0:1], jnp.where(r < 10, values[1:2], values[2:3]))


def per_batch(lines, count):
    r = line_of(lines.shape[1])
    pieces = []
    for b in range(3):
        keep = (r >= 5 * b) & (r < 5 * b + count)
        pieces.append(jnp.sum(jnp.where(keep, lines, 0.0), axis=0, keepdims=True))
    return pieces


def flat(v):
    return v.reshape(-1, v.shape[-1])


def chunks(body, init=0):
    return lax.fori_loop(0, SIDE, body, init)


def ref_stats(a_ref, first, width):
    lanes = pl.ds(first, width)

    def add(i, s):
        return s + jnp.sum(a_ref[pl.ds(i * SIDE, SIDE), :, lanes], axis=0)

    sums = per_batch(chunks(add, jnp.zeros((LINE, width), F32)), HALF)
    means = [s / (HALF * PIX) for s in sums]
    mean_lines = per_line(jnp.concatenate(means, axis=0))

    def add_sq(i, s):
        d = a_ref[pl.ds(i * SIDE, SIDE), :, lanes] - mean_lines[None]
        return s + jnp.sum(d * d, axis=0)

    sq = per_batch(chunks(add_sq, jnp.zeros((LINE, width), F32)), HALF)
    zero = jnp.zeros((1, width), F32)
    return jnp.concatenate(means + [zero] + sq + [zero], axis=0)


def pack(st):
    cut = st.shape[1] * 3 // 4
    rest = [
        jnp.concatenate([st[r : r + 1, cut:] for r in rows], axis=1)
        for rows in ((0, 1, 2), (4, 5, 6))
    ]
    return jnp.concatenate([st[0:3, :cut], st[4:7, :cut]] + rest, axis=0)


def unpack(p, group):
    third = p.shape[1] // 3
    row = p[6 + group : 7 + group]
    rest = jnp.concatenate([row[:, third * k : third * (k + 1)] for k in range(3)], axis=0)
    return jnp.concatenate([p[3 * group : 3 * group + 3], rest], axis=1)


def spread(st, out_ref):
    packed = pack(st)
    for k in range(out_ref.shape[0]):
        out_ref[k] = packed


def merge_norm(gs, rows_each):
    count = sum(g.shape[0] for g in gs)
    total = sum(jnp.sum(g[...], axis=0) for g in gs)
    mean = total / count
    off = 0.0
    for g in gs:
        d = g[...] - mean[None]
        off = off + jnp.sum(d * d, axis=0)
    var = (unpack(total, 1) + rows_each * unpack(off, 0)) / (rows_each * count)
    return eight(unpack(mean, 0), var)


def merge_sums(gs, rows_each):
    total = sum(jnp.sum(g[...], axis=0) for g in gs)
    return eight(unpack(total, 0), unpack(total, 1))


def eight(first, second):
    zero = jnp.zeros((1, first.shape[1]), F32)
    return jnp.concatenate([first, zero, second, zero], axis=0)


def merge_wide(merge, place, g, g_other, out_ref):
    core = place[0]
    rows_each = float(2 * HALF * PIX)
    half = out_ref.shape[1] // 2
    out_ref[:, pl.ds(pl.multiple_of(core * half, half), half)] = merge([g], rows_each)
    out_ref[:, pl.ds(pl.multiple_of((1 - core) * half, half), half)] = merge([g_other], rows_each)


def split_wide(place, st, keep_ref, send_ref):
    core = place[0]
    half = st.shape[1] // 2
    keep_ref[...] = st[:, pl.ds(pl.multiple_of(core * half, half), half)]
    send_ref[...] = st[:, pl.ds(pl.multiple_of((1 - core) * half, half), half)]


def pair_kernel(norm, keep, recv, out_ref):
    a, b = keep[...], recv[...]
    if norm:
        d = a[0:3] - b[0:3]
        mean = 0.5 * (a[0:3] + b[0:3])
        st = eight(mean, a[4:7] + b[4:7] + (HALF * PIX / 2.0) * d * d)
    else:
        st = a + b
    spread(st, out_ref)


OWN_ROWS = float(HALF * PIX)


def gains_kernel(wt, place, *rest):
    refs, (gb_ref, gbo_ref, buf, sems) = rest[: wt.count], rest[wt.count :]
    wait_all(wt.copies("gain", place, refs, buf, Moves(sems)))
    i = lax.broadcasted_iota(jnp.int32, (128, 512), 0)
    j = lax.broadcasted_iota(jnp.int32, (128, 512), 1)
    mid = jnp.zeros((16, 512), F32)
    for k in range(16):
        g = buf[k // 4, k // 2 % 2, k % 2, 0]
        hot = jnp.where((i < 32) & (j == 32 * k + i), 1.0, 0.0).astype(BF16)
        mid = mid + dot(g, hot)
        gbo_ref[:, 128 * k : 128 * k + 128] = g[4:12].astype(F32)
    gb_ref[...] = mid[0:8]


class Moves:
    def __init__(self, sems):
        self.sems, self.used, self.leaving = sems, 0, []

    def fetch(self, source, target):
        copy = pltpu.make_async_copy(source, target, self.sems.at[self.used])
        self.used += 1
        copy.start()
        return copy

    def store(self, source, target):
        self.leaving.append(self.fetch(source, target))

    def chunks_of(self, source, target):
        return [self.fetch(source.at[rows], target.at[rows]) for rows in CHUNKS]

    def tiles_of(self, source, target):
        return [self.fetch(source.at[:, :, lanes], target.at[:, :, lanes]) for lanes in TILES]

    def finish(self):
        wait_all(self.leaving)


CHUNKS = [pl.ds(SIDE * i, SIDE) for i in range(SIDE)]
TILES = [pl.ds(512 * j, 512) for j in range(4)]


def wait_all(copies):
    for c in copies:
        c.wait()


class Weights:
    def __init__(self, kind, segments):
        self.kind, self.segments = kind, segments

    @property
    def count(self):
        return 2 if self.kind == "whole" else 8

    def copies(self, name, place, refs, buf, moves):
        core, y, x = place[0], place[1], place[2]
        found = []
        for part, start, at, width in self.segments[name]:
            for side in range(2):
                c = core if side == 0 else 1 - core
                if self.kind == "whole":
                    pairs = [(refs[side], (ALL, ALL, ALL))]
                elif part == "P":
                    pairs = [(refs[4 * side], (ALL, y, ALL)), (refs[4 * side + 1], (ALL, 1 - y, ALL))]
                else:
                    pairs = [(refs[4 * side + 2], (ALL, ALL, x)), (refs[4 * side + 3], (ALL, ALL, 1 - x))]
                for ref, where in pairs:
                    source = ref.at[..., pl.ds(start, width)]
                    if isinstance(at, tuple):
                        target = buf.at[where + (c, at[0])]
                    else:
                        target = buf.at[where + (c, ALL, pl.ds(at, width))]
                    found.append(moves.fetch(source, target))
        return found


ALL = slice(None)


def first_matmul(x_buf, w_buf, a_ref, stb_ref):
    for j in range(2):
        w = w_buf[2 * j : 2 * j + 2].reshape(256, 2048)
        a_ref[:, :, pl.ds(256 * j, 256)] = dot_nt(flat(x_buf[...]), w).reshape(PIX, LINE, 256)
    spread(ref_stats(a_ref, 0, 512), stb_ref)


def permute_kernel(core_ref, x_ref, out_ref, x_buf, buf, sems):
    moves = Moves(sems)
    loads = moves.tiles_of(x_ref, x_buf)
    core = core_ref[0]
    i = lax.broadcasted_iota(jnp.int32, (ROWS, SEG * PIX), 0)
    j = lax.broadcasted_iota(jnp.int32, (ROWS, SEG * PIX), 1)
    pixel, line = i >> 4, i & 15
    hots = []
    for b in range(3):
        t = line - 5 * b
        target = (HALF * core + t) * PIX + pixel
        hots.append(jnp.where((t >= 0) & (t < HALF) & (j == target), 1.0, 0.0).astype(BF16))
    for load, lanes in zip(loads, TILES):
        load.wait()
        total = dot(hots[0], x_buf[0, :, lanes])
        total = total + dot(hots[1], x_buf[1, :, lanes])
        total = total + dot(hots[2], x_buf[2, :, lanes])
        buf[:, :, lanes] = total.astype(BF16).reshape(PIX, LINE, 512)
        moves.store(buf.at[:, :, lanes], out_ref.at[:, :, lanes])
    moves.finish()


def restore_kernel(place, early_ref, late_ref, early_in, late_in, out_ref, buf, out_buf, sems):
    core = place[0]

    def copies(mine, received):
        found = []
        for k, lanes in enumerate(TILES):
            for n, (v, side) in enumerate(((mine, core), (received, 1 - core))):
                found.append(
                    pltpu.make_async_copy(
                        v.at[:, :, lanes], buf.at[side, :, :, lanes], sems.at[2 * k + n]
                    )
                )
        return found

    @pl.when(core == 0)
    def _():
        for c in copies(early_ref, early_in):
            c.start()

    @pl.when(core == 1)
    def _():
        for c in copies(late_ref, late_in):
            c.start()

    def hot(first, count, side, b):
        j = lax.broadcasted_iota(jnp.int32, (count, ROWS), 0) + first
        i = lax.broadcasted_iota(jnp.int32, (count, ROWS), 1)
        seg = jnp.zeros_like(j)
        for k in range(1, SEG):
            seg = seg + jnp.where(j >= PIX * k, 1, 0)
        t = seg - HALF * side
        target = (j - PIX * seg) * LINE + 5 * b + t
        return jnp.where((t >= 0) & (t < HALF) & (i == target), 1.0, 0.0).astype(BF16)

    hots = [(hot(0, 208, 0, b), hot(192, 200, 1, b)) for b in range(3)]
    loads = copies(early_ref, early_in)
    leaving = []
    for k, lanes in enumerate(TILES):
        wait_all(loads[2 * k : 2 * k + 2])
        for b, (lower, upper) in enumerate(hots):
            low = dot(lower, flat(buf[0, :, :, lanes])).astype(BF16)
            high = dot(upper, flat(buf[1, :, :, lanes])).astype(BF16)
            out_buf[b, 0:192, lanes] = low[:192]
            out_buf[b, 192:208, lanes] = low[192:] + high[:16]
            out_buf[b, 208:392, lanes] = high[16:]
        copy = pltpu.make_async_copy(out_buf.at[:, :, lanes], out_ref.at[:, :, lanes], sems.at[8 + k])
        copy.start()
        leaving.append(copy)
    wait_all(leaving)


def first_kernel(wt, place, x_ref, *rest):
    refs, (a_ref, stb_ref, w_buf, sems) = rest[: wt.count], rest[wt.count :]
    wait_all(wt.copies("in", place, refs, w_buf, Moves(sems)))
    first_matmul(x_ref, w_buf, a_ref, stb_ref)


def tap_ranges(shift):
    return max(0, -shift), min(SIDE, SIDE - shift)


def build_patches(sq, patch):
    patch[...] = jnp.zeros(patch.shape, BF16)
    sq4 = sq.reshape(SIDE, SIDE, LINE, 128)
    for k in (1, 2):
        for tap in range(9):
            dy, dx = k * (tap // 3 - 1), k * (tap % 3 - 1)
            (y0, y1), (x0, x1) = tap_ranges(dy), tap_ranges(dx)
            col = ((k - 1) * 9 + tap) * 128
            patch[y0:y1, x0:x1, :, col : col + 128] = sq4[y0 + dy : y1 + dy, x0 + dx : x1 + dx]


def clear_border(pad):
    zero_row = jnp.zeros((9, LINE, 512), BF16)
    pad[0] = zero_row
    pad[8] = zero_row
    for y in range(1, 8):
        pad[y, 0] = jnp.zeros((LINE, 512), BF16)
        pad[y, 8] = jnp.zeros((LINE, 512), BF16)


def middle_kernel(wt, place, a_in, a_other, g, g_other, gb_ref, msk_ref, *rest):
    refs = rest[: wt.count]
    (
        a_ref, diff_ref, sq_ref, op_ref, mix_ref, second, second_ref, st_ref, mv_ref,
        sq_buf, nf_buf, mid_buf, a_buf, diff, sq_out, op, mixp, hid, patch, sems,
    ) = rest[wt.count :]
    core = place[0]
    moves = Moves(sems)
    sq_copies = wt.copies("sq", place, refs, sq_buf, moves)
    nf_copies = wt.copies("nf", place, refs, nf_buf, moves)
    mid_copies = wt.copies("mid", place, refs, mid_buf, moves)
    clear_border(mixp)
    mv_ref[...] = merge_norm([g, g_other], OWN_ROWS)
    r = line_of(512)
    halo = ((r == 4) | (r == 9) | (r == 14)) & (core == 0)
    mean = per_line(mv_ref[0:3])
    scale = lax.rsqrt(per_line(mv_ref[4:7]) + EPS) * gb_ref[0:1]
    shift = gb_ref[1:2]
    m = msk_ref[:, 0:1]
    for rows in CHUNKS:
        a = jnp.where(halo[None], pltpu.roll(a_other[rows], 4, 1), a_in[rows])
        a_buf[rows] = a
        n1 = (a - mean[None]) * scale[None] + shift[None]
        h = n1 * sigmoid(n1)
        hid[rows] = h
        diff[rows] = (m[None] * (pltpu.roll(h, LINE - 1, 1) - h)).astype(BF16)
    moves.store(a_buf, a_ref)
    moves.store(diff, diff_ref)
    wait_all(sq_copies)
    sq = dot(flat(diff[...]), sq_buf[...].reshape(512, 128)).astype(BF16)
    sq_out[...] = sq.reshape(PIX, LINE, 128)
    moves.store(sq_out, sq_ref)
    build_patches(sq, patch)
    wait_all(nf_copies)
    for j in range(2):
        lanes = pl.ds(256 * j, 256)
        w = nf_buf[2 * j : 2 * j + 2].reshape(256, 2304)
        logits = dot_nt(patch[...].reshape(ROWS, 2304), w).reshape(PIX, LINE, 256)
        opening = sigmoid(logits)
        op[:, :, lanes] = opening.astype(BF16)
        mixed = (hid[:, :, lanes] * (0.5 + opening)).astype(BF16)
        mixp[1:8, 1:8, :, lanes] = mixed.reshape(SIDE, SIDE, LINE, 256)
    moves.store(op, op_ref)
    moves.store(mixp, mix_ref)
    wait_all(mid_copies)

    total = 0.0
    for k in range(9):
        v = mixp[k // 3 : k // 3 + SIDE, k % 3 : k % 3 + SIDE].reshape(ROWS, 512)
        total = total + dot_nt(v, mid_buf[..., pl.ds(512 * k, 512)].reshape(512, 512))
    second[...] = total.reshape(PIX, LINE, 512)
    moves.store(second, second_ref)
    spread(ref_stats(second, 0, 512), st_ref)
    moves.finish()


def wide_kernel(wt, place, second, g, g_other, gb_ref, *rest):
    refs = rest[: wt.count]
    mid_ref, keep_ref, send_ref, mv_ref, buf, mid, third, st_ref, sems = rest[wt.count :]
    moves = Moves(sems)
    copies = wt.copies("out", place, refs, buf, moves)
    mv_ref[...] = merge_norm([g, g_other], OWN_ROWS)
    mean = per_line(mv_ref[0:3])
    scale = lax.rsqrt(per_line(mv_ref[4:7]) + EPS) * gb_ref[2:3]
    shift = gb_ref[3:4]
    for rows in CHUNKS:
        n2 = (second[rows] - mean[None]) * scale[None] + shift[None]
        mid[rows] = (n2 * sigmoid(n2)).astype(BF16)
    moves.store(mid, mid_ref)
    wait_all(copies)
    for j, lanes in enumerate(TILES):
        w = buf[j].reshape(512, 512)
        third[...] = dot_nt(flat(mid[...]), w).reshape(PIX, LINE, 512)
        st_ref[:, lanes] = ref_stats(third, 0, 512)
    split_wide(place, st_ref, keep_ref, send_ref)
    moves.finish()


def finish(mid, wide_buf, third, x_buf, loads, mv_ref, gb_ref, each, after_tile):
    for j, lanes in enumerate(TILES):
        third[...] = dot_nt(flat(mid[...]), wide_buf[j].reshape(512, 512)).reshape(PIX, LINE, 512)
        wait_all([load[j] for load in loads])
        mean = per_line(mv_ref[0:3, lanes])
        inv = lax.rsqrt(per_line(mv_ref[4:7, lanes]) + EPS)
        gain, bias = gb_ref[0:1, lanes], gb_ref[1:2, lanes]

        def chunk(i, carry):
            rows = pl.ds(i * SIDE, SIDE)
            xhat = (third[rows] - mean[None]) * inv[None]
            z = x_buf[rows, :, lanes].astype(F32) + xhat * gain[None] + bias[None]
            sg = sigmoid(z)
            return each(rows, lanes, xhat, z * sg, sg, carry)

        zero = jnp.zeros((LINE, 512), F32)
        after_tile(lanes, chunks(chunk, (zero, zero)))


def sums_of(dh, dg):
    zero = jnp.zeros((1, dh.shape[1]), F32)
    return jnp.concatenate(per_batch(dh, STRIDE) + [zero] + per_batch(dg, STRIDE) + [zero], axis=0)


def turn_kernel(wide_wt, wt, place, mid, x_ref, g, g_other, gb_ref, *rest):
    wide_refs, rest = rest[: wide_wt.count], rest[wide_wt.count :]
    refs = rest[: wt.count]
    (
        act_ref, xhat_ref, slope_ref, a_ref, st_ref, mv_ref,
        wide_buf, w_buf, third, x_buf, act, xhat_buf, slope, sems,
    ) = rest[wt.count :]
    moves = Moves(sems)
    wide_copies = wide_wt.copies("out", place, wide_refs, wide_buf, moves)
    loads = [moves.tiles_of(x_ref, x_buf)]
    copies = wt.copies("in", place, refs, w_buf, moves)
    merge_wide(merge_norm, place, g, g_other, mv_ref)

    def each(rows, lanes, xhat, y, sg, carry):
        act[rows, :, lanes] = y.astype(BF16)
        xhat_buf[rows, :, lanes] = xhat.astype(BF16)
        slope[rows, :, lanes] = (sg + y * (1.0 - sg)).astype(BF16)
        return carry

    def after_tile(lanes, _):
        for buf, ref in ((act, act_ref), (xhat_buf, xhat_ref), (slope, slope_ref)):
            moves.store(buf.at[:, :, lanes], ref.at[:, :, lanes])

    wait_all(wide_copies)
    finish(mid, wide_buf, third, x_buf, loads, mv_ref, gb_ref, each, after_tile)
    wait_all(copies)
    first_matmul(act, w_buf, a_ref, st_ref)
    moves.finish()


def top_kernel(
    wide_wt, place, mid, x_ref, g, g_other, gb_ref, dy_ref, *rest,
):
    wide_refs, rest = rest[: wide_wt.count], rest[wide_wt.count :]
    (
        act_ref, xhat_ref, dz, keep_ref, send_ref, mv_ref,
        wide_buf, third, x_buf, dy, act, xhat_buf, sums_ref, sems,
    ) = rest
    moves = Moves(sems)
    wide_copies = wide_wt.copies("out", place, wide_refs, wide_buf, moves)
    loads = [moves.tiles_of(r, b) for r, b in ((x_ref, x_buf), (dy_ref, dy))]
    merge_wide(merge_norm, place, g, g_other, mv_ref)

    def each(rows, lanes, xhat, y, sg, carry):
        act[rows, :, lanes] = y.astype(BF16)
        xhat_buf[rows, :, lanes] = xhat.astype(BF16)
        d = dy[rows, :, lanes].astype(F32) * (sg + y * (1.0 - sg))
        dz[rows, :, lanes] = d.astype(BF16)
        return carry[0] + jnp.sum(d, axis=0), carry[1] + jnp.sum(d * xhat, axis=0)

    def after_tile(lanes, carry):
        for buf, ref in ((act, act_ref), (xhat_buf, xhat_ref)):
            moves.store(buf.at[:, :, lanes], ref.at[:, :, lanes])
        sums_ref[:, lanes] = sums_of(*carry)

    wait_all(wide_copies)
    finish(mid, wide_buf, third, x_buf, loads, mv_ref, gb_ref, each, after_tile)
    split_wide(place, sums_ref, keep_ref, send_ref)
    moves.finish()


class Shares:
    def __init__(self, kind, parts):
        self.kind, self.parts = kind, parts

    @property
    def count(self):
        return 2 if self.kind == "whole" else 4 * sum(1 for width in self.parts if width)

    def outs(self):
        if self.kind == "whole":
            width = sum(self.parts)
            return [((4, 2, 2, 16, width), BF16)] * 2
        return [((4, 2, 16, width), BF16) for width in self.parts if width for _ in range(4)]

    def buffers(self):
        return [pltpu.VMEM(shape, dtype) for shape, dtype in self.outs()]

    def store(self, place, out, first, result, zs=ALL):
        refs, bufs, moves = out

        def put(ref, buf, v, lanes):
            buf[zs, ..., lanes] = v
            moves.store(buf.at[zs, ..., lanes], ref.at[zs, ..., lanes])

        core, y, x = place[0], place[1], place[2]
        width = result.shape[1]
        parts = result.astype(BF16).reshape(-1, 2, 2, 2, 16, width)
        lower, upper = parts[:, :, :, 0], parts[:, :, :, 1]
        sides = [jnp.where(core == 0, lower, upper), jnp.where(core == 0, upper, lower)]
        if self.kind == "whole":
            for ref, buf, v in zip(refs, bufs, sides):
                put(ref, buf, v, pl.ds(first, width))
            return
        is_p = first < self.parts[0]
        start = first if is_p else first - self.parts[0]
        lanes = pl.ds(start, width)
        refs = refs[:4] if is_p else refs[-4:]
        bufs = bufs[:4] if is_p else bufs[-4:]
        for k, v in enumerate(sides):
            if is_p:
                two, at = (v[:, 0], v[:, 1]), y
            else:
                two, at = (v[:, :, 0], v[:, :, 1]), x
            put(refs[2 * k], bufs[2 * k], jnp.where(at == 0, two[0], two[1]), lanes)
            put(refs[2 * k + 1], bufs[2 * k + 1], jnp.where(at == 0, two[1], two[0]), lanes)


def wide_back_kernel(
    rows_total, wt, place, dz, xhat_ref, mv3_ref, g, g_other, gbo_ref, second_ref, mv2_ref, gb_ref, *rest
):
    refs = rest[: wt.count]
    dn2, stb_ref, d3_ref, s3_ref, buf, xhat, second, d3, lines, sems = rest[wt.count :]
    moves = Moves(sems)
    loads = moves.chunks_of(xhat_ref, xhat)
    copies = wt.copies("out", place, refs, buf, moves)
    second_load = moves.fetch(second_ref, second)
    merge_wide(merge_sums, place, g, g_other, s3_ref)
    own = own_lines(512)
    for lanes in TILES:
        lines[0, :, lanes] = lax.rsqrt(per_line(mv3_ref[4:7, lanes]) + EPS) * gbo_ref[0:1, lanes] * own
        lines[1, :, lanes] = per_line(s3_ref[0:3, lanes]) / rows_total
        lines[2, :, lanes] = per_line(s3_ref[4:7, lanes]) / rows_total
    for load, rows in zip(loads, CHUNKS):
        load.wait()
        for lanes in TILES:
            v = dz[rows, :, lanes].astype(F32) - lines[1, :, lanes][None]
            v = v - xhat[rows, :, lanes].astype(F32) * lines[2, :, lanes][None]
            d3[rows, :, lanes] = (lines[0, :, lanes][None] * v).astype(BF16)
    moves.store(d3, d3_ref)
    wait_all(copies)
    for j, lanes in enumerate(TILES):
        part = dot(flat(d3[:, :, lanes]), buf[j].reshape(512, 512)).reshape(PIX, LINE, 512)
        dn2[...] = part if j == 0 else dn2[...] + part
    second_load.wait()
    mean = per_line(mv2_ref[0:3])
    inv = lax.rsqrt(per_line(mv2_ref[4:7]) + EPS)
    gain, bias = gb_ref[2:3], gb_ref[3:4]

    def chunk(i, carry):
        rows = pl.ds(i * SIDE, SIDE)
        xh = (second[rows] - mean[None]) * inv[None]
        n2 = xh * gain[None] + bias[None]
        sg = sigmoid(n2)
        dn = dn2[rows] * (sg * (1.0 + n2 * (1.0 - sg)))
        dn2[rows] = dn
        return carry[0] + jnp.sum(dn, axis=0), carry[1] + jnp.sum(dn * xh, axis=0)

    zero = jnp.zeros((LINE, 512), F32)
    spread(sums_of(*chunks(chunk, (zero, zero))), stb_ref)
    moves.finish()


def wide_grad(sh, place, refs, start, d3, mid):
    for j in range(4):
        v = flat(d3[:, :, pl.ds(512 * j, 512)])
        res = dot_tn(v, flat(mid[...])).reshape(2, 2, 2, 4, 16, 512)
        for g in range(4):
            sh.store(place, refs, start + 512 * g, res[:, :, :, g].reshape(128, 512), slice(j, j + 1))


def middle_grad(sh, place, refs, start, d2, mixp):
    for tap in range(9):
        mixed = mixp[tap // 3 : tap // 3 + SIDE, tap % 3 : tap % 3 + SIDE].reshape(ROWS, 512)
        sh.store(place, refs, start + 512 * tap, dot_tn(flat(d2[...]), mixed))


def branch_grad(sh, place, refs, start, dlog, sq_ref, diff, dsq, patch):
    build_patches(flat(sq_ref[...]), patch)
    for j in range(3):
        pv = patch[:, :, :, pl.ds(768 * j, 768)].reshape(ROWS, 768)
        sh.store(place, refs, start + 128 + 768 * j, dot_tn(flat(dlog[...]), pv))
    sh.store(place, refs, start, dot_tn(flat(diff[...]), flat(dsq[...])))


def fetch_all(moves, refs, bufs):
    return [moves.fetch(r, b) for r, b in zip(refs, bufs)]


def branch_grad_kernel(sh, place, dlog, dsq, sq_ref, diff_ref, *rest):
    refs, (sq, diff, patch), bufs = rest[: sh.count], rest[sh.count : -1 - sh.count], rest[-1 - sh.count : -1]
    moves = Moves(rest[-1])
    wait_all(fetch_all(moves, (sq_ref, diff_ref), (sq, diff)))
    branch_grad(sh, place, (refs, bufs, moves), 0, dlog, sq, diff, dsq, patch)
    moves.finish()


def all_grad_kernel(sh, place, d2, dlog, dsq, d3_ref, mid_ref, mix_ref, sq_ref, diff_ref, *rest):
    refs, (d3, mid, mixp, sq, diff, patch) = rest[: sh.count], rest[sh.count : -1 - sh.count]
    bufs, moves = rest[-1 - sh.count : -1], Moves(rest[-1])
    out = (refs, bufs, moves)
    mix_load = moves.fetch(mix_ref, mixp)
    loads = fetch_all(moves, (sq_ref, diff_ref, d3_ref, mid_ref), (sq, diff, d3, mid))
    mix_load.wait()
    middle_grad(sh, place, out, 2432, d2, mixp)
    wait_all(loads)
    wide_grad(sh, place, out, 7040, d3, mid)
    branch_grad(sh, place, out, 0, dlog, sq, diff, dsq, patch)
    moves.finish()


def mixed_grad_kernel(sh, place, d3, mid_ref, d1, x_ref, *rest):
    refs, (mid, x), bufs = rest[: sh.count], rest[sh.count : -1 - sh.count], rest[-1 - sh.count : -1]
    moves = Moves(rest[-1])
    wait_all(fetch_all(moves, (mid_ref, x_ref), (mid, x)))
    wide_grad(sh, place, (refs, bufs, moves), 0, d3, mid)
    first_grad(sh, place, (refs, bufs, moves), 2048, d1, x)
    moves.finish()


def second_back_kernel(rows_total, sh, place, dn2, second_ref, mv2_ref, g, g_other, gb_ref, *rest):
    if sh is not None:
        mix_ref, refs, rest = rest[0], rest[1 : 1 + sh.count], rest[1 + sh.count :]
        d2, s2_ref, second, mixp, *bufs, sems = rest
    else:
        d2, s2_ref, second, sems = rest
    moves = Moves(sems)
    second_loads = moves.chunks_of(second_ref, second)
    if sh is not None:
        mix_load = moves.fetch(mix_ref, mixp)
    s2_ref[...] = merge_sums([g, g_other], OWN_ROWS)
    own = own_lines(512)
    mean2 = per_line(mv2_ref[0:3])
    inv2 = lax.rsqrt(per_line(mv2_ref[4:7]) + EPS)
    k2 = inv2 * gb_ref[2:3] * own
    dh2 = per_line(s2_ref[0:3]) / rows_total
    dg2 = per_line(s2_ref[4:7]) / rows_total
    for i, rows in enumerate(CHUNKS):
        second_loads[i].wait()
        xh = (second[rows] - mean2[None]) * inv2[None]
        d2[rows] = (k2[None] * (dn2[rows] - dh2[None] - xh * dg2[None])).astype(BF16)
    if sh is not None:
        mix_load.wait()
        middle_grad(sh, place, (refs, bufs, moves), 0, d2, mixp)
    moves.finish()


def middle_back_kernel(wt, place, d2, a_ref, mv1_ref, gb_ref, msk_ref, op_ref, *rest):
    refs = rest[: wt.count]
    (
        dn1, stb_ref, dlog, dsq_out,
        sq_buf, nf_buf, mid_buf, d2p, a, op, dmix, dsq, sems,
    ) = rest[wt.count :]
    moves = Moves(sems)
    mid_copies = wt.copies("mid", place, refs, mid_buf, moves)
    late_loads = [moves.fetch(a_ref, a), moves.fetch(op_ref, op)]
    nf_copies = wt.copies("nf", place, refs, nf_buf, moves)
    sq_copies = wt.copies("sq", place, refs, sq_buf, moves)
    clear_border(d2p)
    for i, rows in enumerate(CHUNKS):
        d2p[i + 1, 1:8] = d2[rows]
    wait_all(mid_copies)

    total = 0.0
    for k in range(9):
        y, x = 2 - k // 3, 2 - k % 3
        v = d2p[y : y + SIDE, x : x + SIDE].reshape(ROWS, 512)
        total = total + dot(v, mid_buf[..., pl.ds(512 * k, 512)].reshape(512, 512))
    dmix[...] = total.reshape(PIX, LINE, 512)
    wait_all(late_loads)
    mean1 = per_line(mv1_ref[0:3])
    inv1 = lax.rsqrt(per_line(mv1_ref[4:7]) + EPS)
    gain1, bias1 = gb_ref[0:1], gb_ref[1:2]

    def log_chunk(i, c):
        rows = pl.ds(i * SIDE, SIDE)
        n1 = (a[rows] - mean1[None]) * inv1[None] * gain1[None] + bias1[None]
        h = n1 * sigmoid(n1)
        o = op[rows].astype(F32)
        dlog[rows] = (dmix[rows] * h * o * (1.0 - o)).astype(BF16)
        return c

    chunks(log_chunk)
    wait_all(nf_copies)
    dsq[...] = jnp.zeros(dsq.shape, F32)
    for k in (1, 2):
        for ty in range(3):
            w = nf_buf[..., pl.ds(((k - 1) * 9 + ty * 3) * 128, 384)].reshape(512, 384)
            res = dot(flat(dlog[...]), w).reshape(SIDE, SIDE, LINE, 384)
            for tx in range(3):
                dy, dx = k * (ty - 1), k * (tx - 1)
                (y0, y1), (x0, x1) = tap_ranges(dy), tap_ranges(dx)
                dsq[y0 + dy : y1 + dy, x0 + dx : x1 + dx] += res[
                    y0:y1, x0:x1, :, 128 * tx : 128 * tx + 128
                ]
    dsq_low = dsq[...].astype(BF16).reshape(ROWS, 128)
    dsq_out[...] = dsq_low.reshape(PIX, LINE, 128)
    wait_all(sq_copies)
    dn1[...] = dot_nt(dsq_low, sq_buf[...].reshape(512, 128)).reshape(PIX, LINE, 512)
    m = msk_ref[:, 0:1]

    def last_chunk(i, carry):
        rows = pl.ds(i * SIDE, SIDE)
        xh = (a[rows] - mean1[None]) * inv1[None]
        n1 = xh * gain1[None] + bias1[None]
        sg = sigmoid(n1)
        e = dn1[rows] * m[None]
        o = op[rows].astype(F32)
        dhid = dmix[rows] * (0.5 + o) - e + pltpu.roll(e, 1, 1)
        dn = dhid * (sg * (1.0 + n1 * (1.0 - sg)))
        dn1[rows] = dn
        return carry[0] + jnp.sum(dn, axis=0), carry[1] + jnp.sum(dn * xh, axis=0)

    zero = jnp.zeros((LINE, 512), F32)
    spread(sums_of(*chunks(last_chunk, (zero, zero))), stb_ref)


def first_d1(rows_total, place, loads, dn1, dn1_other, a, mv1_ref, s1_ref, gb_ref, d1):
    own = own_lines(512)
    r = line_of(512)
    first = ((r == 0) | (r == 5) | (r == 10)) & (place[0] == 1)
    mean = per_line(mv1_ref[0:3])
    inv = lax.rsqrt(per_line(mv1_ref[4:7]) + EPS)
    k = inv * gb_ref[0:1] * own
    dh = per_line(s1_ref[0:3]) / rows_total
    dg = per_line(s1_ref[4:7]) / rows_total
    for i, rows in enumerate(CHUNKS):
        loads[i].wait()
        xh = (a[rows] - mean[None]) * inv[None]
        dn = dn1[rows] + jnp.where(first[None], pltpu.roll(dn1_other[rows], LINE - 4, 1), 0.0)
        d1[rows] = (k[None] * (dn - dh[None] - xh * dg[None])).astype(BF16)


def first_back_kernel(
    rows_total, wt, place, dn1, other, a_ref, mv1_ref, g, g_other, gb_ref, dz_ref, slope_ref, xhat_ref, *rest
):
    refs = rest[: wt.count]
    (
        dx_ref, d1, s1_ref, below, keep_ref, send_ref,
        w_buf, a, dz, slope, xhat, dx, sums_ref, sems,
    ) = rest[wt.count :]
    moves = Moves(sems)
    loads = moves.chunks_of(a_ref, a)
    copies = wt.copies("in", place, refs, w_buf, moves)
    tiles = [moves.tiles_of(r, b) for r, b in ((dz_ref, dz), (slope_ref, slope), (xhat_ref, xhat))]
    s1_ref[...] = merge_sums([g, g_other], OWN_ROWS)
    first_d1(rows_total, place, loads, dn1, other, a, mv1_ref, s1_ref, gb_ref, d1)
    wait_all(copies)
    for j, lanes in enumerate(TILES):
        wait_all([load[j] for load in tiles])
        w = w_buf[..., lanes].reshape(512, 512)
        v = dot(flat(d1[...]), w).reshape(PIX, LINE, 512) + dz[:, :, lanes].astype(F32)
        low = v.astype(BF16)
        dx[:, :, lanes] = low
        d = low.astype(F32) * slope[:, :, lanes].astype(F32)
        below[:, :, lanes] = d.astype(BF16)
        moves.store(dx.at[:, :, lanes], dx_ref.at[:, :, lanes])
        sums_ref[:, lanes] = sums_of(
            jnp.sum(d, axis=0), jnp.sum(d * xhat[:, :, lanes].astype(F32), axis=0)
        )
    split_wide(place, sums_ref, keep_ref, send_ref)
    moves.finish()


def first_grad(sh, place, out, start, d1, x_ref):
    for j in range(4):
        x = flat(x_ref[:, :, pl.ds(512 * j, 512)])
        sh.store(place, out, start + 512 * j, dot_tn(flat(d1[...]), x))


def last_grad_kernel(rows_total, sh, place, dn1, other, a_ref, mv1_ref, g, g_other, gb_ref, x_ref, *rest):
    refs, rest = rest[: sh.count], rest[sh.count :]
    d1, s1_ref, a, x, *bufs, sems = rest
    moves = Moves(sems)
    loads = moves.chunks_of(a_ref, a)
    x_load = moves.fetch(x_ref, x)
    s1_ref[...] = merge_sums([g, g_other], OWN_ROWS)
    first_d1(rows_total, place, loads, dn1, other, a, mv1_ref, s1_ref, gb_ref, d1)
    x_load.wait()
    first_grad(sh, place, (refs, bufs, moves), 0, d1, x)
    moves.finish()


def last_back_kernel(wt, place, d1, dz_ref, *rest):
    refs, (dx_ref, w_buf, dz, dx, sems) = rest[: wt.count], rest[wt.count :]
    moves = Moves(sems)
    copies = wt.copies("in", place, refs, w_buf, moves)
    loads = moves.tiles_of(dz_ref, dz)
    wait_all(copies)
    for j, lanes in enumerate(TILES):
        loads[j].wait()
        w = w_buf[..., lanes].reshape(512, 512)
        v = dot(flat(d1[...]), w).reshape(PIX, LINE, 512) + dz[:, :, lanes].astype(F32)
        dx[:, :, lanes] = v.astype(BF16)
        moves.store(dx.at[:, :, lanes], dx_ref.at[:, :, lanes])
    moves.finish()


VM = pl.BlockSpec(memory_space=pltpu.VMEM)
HB = pl.BlockSpec(memory_space=pltpu.HBM)
SM = pl.BlockSpec(memory_space=pltpu.SMEM)
AN = pl.BlockSpec(memory_space=pl.ANY)


class Near:
    def __init__(self, value):
        self.value = value


class Near2(Near):
    pass


def is_big(shape):
    return len(shape) >= 4 or (len(shape) == 3 and shape[0] in (PIX, 3))


def size_of(shape, dtype):
    size = jnp.dtype(dtype).itemsize
    for k in shape:
        size *= k
    return size


def call(kernel, outs, scratch=(), us=5):
    def run(place, *values):
        specs = [SM]
        need = 6 * 1024 * 1024
        need += sum(size_of(v.shape, v.dtype) for v in scratch)
        need += sum(size_of(*o[:2]) for o in outs if not (is_big(o[0]) and len(o) == 2))
        for v in values:
            u = v.value if isinstance(v, Near) else v
            if not is_big(u.shape) or (isinstance(v, Near) and not isinstance(v, Near2)):
                need += size_of(u.shape, u.dtype)
        for v in values:
            if isinstance(v, Near):
                specs.append(AN if isinstance(v, Near2) else VM)
            else:
                specs.append(HB if is_big(v.shape) else VM)
        return pl.pallas_call(
            kernel,
            in_specs=specs,
            out_specs=tuple(HB if is_big(o[0]) and len(o) == 2 else VM for o in outs),
            out_shape=tuple(jax.ShapeDtypeStruct(o[0], o[1]) for o in outs),
            scratch_shapes=list(scratch) + [pltpu.SemaphoreType.DMA((96,))],
            compiler_params=pltpu.CompilerParams(vmem_limit_bytes=52 * 1024 * 1024),
            cost_estimate=pl.CostEstimate(flops=us * 10**9, bytes_accessed=us * 3 * 10**6, transcendentals=0),
        )(place, *[v.value if isinstance(v, Near) else v for v in values])

    return run


def near(width, dtype):
    return ((PIX, LINE, width), dtype, True)


def pm(width, dtype):
    return ((PIX, LINE, width), dtype)


def buf(width, dtype):
    return pltpu.VMEM((PIX, LINE, width), dtype)


def wbuf(width):
    return pltpu.VMEM((4, 2, 2, 2, 16, width), BF16)


STAT = ((8, 512), F32)
WIDE_STAT = ((8, 2048), F32)
PAIR = [(0, 1), (1, 0)]


class Links:
    def __init__(self, dp, core):
        self.dp, self.core = dp, core
        self.at = lax.axis_index("dp")

    def bit(self, k):
        return (self.at // k) % 2

    def place(self):
        y, x = (self.bit(2), self.bit(1)) if self.split else (0, 0)
        return jnp.stack([self.core, jnp.int32(y), jnp.int32(x)]).astype(jnp.int32)

    split = True

    def swap(self, v):
        return lax.ppermute(v, "pipe", PAIR)

    def across(self, v, k):
        return lax.ppermute(v, "dp", [(i, i ^ k) for i in range(self.dp)])

    def to_all(self, spread, *meanwhile):
        g = lax.all_to_all(spread, "dp", 0, 0)
        if meanwhile:
            g = after(g, *meanwhile)
        return g, self.swap(g)

    def by_core(self, own, other):
        first = self.core == 0
        return jnp.where(first, own, other), jnp.where(first, other, own)

    def in_order(self, which, own, other, axis):
        pair = jnp.where(which == 0, jnp.stack([own, other], axis), jnp.stack([other, own], axis))
        return pair

    def halves(self, piece):
        two = piece.reshape(2, 16, piece.shape[1])
        keep = lax.dynamic_index_in_dim(two, self.core, 0, keepdims=False)
        recv = self.swap(lax.dynamic_index_in_dim(two, 1 - self.core, 0, keepdims=False))
        return self.by_core(keep, recv)

    def gather_first(self, v, cut):
        p, q = v[..., :cut], v[..., cut:]
        p_other, q_other = self.across(p, 1), self.across(q, 2)
        return self.in_order(self.bit(1), p, p_other, 1), self.in_order(self.bit(2), q, q_other, 1)

    def gather_second(self, p, q):
        mine = (p, self.across(p, 2), q, self.across(q, 1))
        return mine + tuple(self.swap(v) for v in mine)

    def gather_whole(self, own):
        return lax.all_gather(own, "dp").reshape(4, 2, 2, 16, -1)

    def gather_blocks(self, gains, inner, rest, wide, permute, clips, cotangent):
        rows = jnp.concatenate([jnp.pad(v, ((0, 0), (0, 128 - v.shape[1]))) for v in gains], axis=0)
        tail = jnp.pad(rows, ((0, 32 - rows.shape[0]), (0, 0)))
        a = self.halves(jnp.concatenate([inner, tail], axis=1))
        b, c = self.halves(rest), self.halves(self.narrow_rows(wide))
        b0 = self.gather_whole(b[0])
        v = after(a[0], b[0])
        v = self.in_order(self.bit(8), v, self.across(v, 8), 0)
        x = permute(after(clips, v, b[0]))
        moved = after(self.across(v, 4), x)
        v = self.in_order(self.bit(4), v, moved, 1).reshape(4, 16, -1)
        ca = jnp.concatenate([c[0], a[1]], axis=1)
        ca = self.in_order(self.bit(8), ca, self.across(after(ca, v), 8), 0)
        dy = permute(after(cotangent, v))
        moved = after(self.across(ca, 4), dy)
        ca = self.in_order(self.bit(4), ca, moved, 1).reshape(4, 16, -1)
        a0 = self.gather_second(*self.gather_first(v, 1024))
        block_0 = {"A": (Weights("split", SPLIT_A), a0)}
        return (block_0, (ca, b0, jnp.concatenate([c[1], b[1]], axis=1))), x, dy

    def gather_middle(self, blocks, pieces, then):
        block_0, (_, b0, bc) = blocks
        ca = self.gather_second(*pieces)
        block_0["C"] = (Weights("split", SPLIT_C), ca)
        b0 = after(b0, then)
        block_0["B"] = (Weights("whole", middle_at(0)), (b0, self.swap(b0)))
        return block_0, (ca, self.gather_whole(after(bc, b0)))

    def gather_last(self, blocks, third):
        block_0, (ca, bc) = blocks
        bc = after(bc, third)
        bc = (bc, self.swap(bc))
        return block_0, {
            "A": (Weights("split", SPLIT_A1), ca),
            "B": (Weights("whole", middle_at(2048)), bc),
            "C": (Weights("whole", wide_at(0)), bc),
        }

    def gains_of(self, group, place):
        wt, refs = group
        return call(functools.partial(gains_kernel, wt), [STAT, WIDE_STAT], [wbuf(128)])(place, *refs)

    def add(self, a, b):
        return (a.astype(F32) + b.astype(F32)).astype(BF16)

    def halve(self, v, axis, k, then=None):
        which = self.bit(k)
        keep = lax.dynamic_index_in_dim(v, which, axis, keepdims=False)
        send = lax.dynamic_index_in_dim(v, 1 - which, axis, keepdims=False)
        moved = self.across(send, k)
        if then is not None:
            moved = after(moved, then)
        return self.add(keep, moved)

    def scatter_first(self, g):
        return [self.add(g[k], self.swap(g[k + 2])) for k in (1, 5)]

    def scatter_xy(self, g, sent, then=(None, None)):
        done = []
        for own, send_own, other, k in ((g[0], g[2], sent[0], 2), (g[4], g[6], sent[1], 1)):
            moved = self.across(other, k)
            if then[0] is not None:
                moved = after(moved, then[0])
            v = self.add(self.add(own, self.swap(send_own)), moved)
            done.append(self.halve(v, 1, 3 - k, then[1]))
        return jnp.concatenate(done, axis=-1)

    def scatter_z(self, v, then=(None, None)):
        half = self.halve(v.reshape(2, 2, 16, -1), 1, 4, then[0])
        return self.halve(half, 0, 8, then[1]), half

    def half_sums(self, keep, send):
        return self.add(keep, self.swap(send)).reshape(16, 16, -1)

    def scatter_whole(self, v):
        return lax.psum_scatter(v, "dp", scatter_dimension=0, tiled=True)[0]

    def scatter_at_once(self, v, *then):
        v = lax.all_to_all(v, "dp", 0, 0)
        if then:
            v = after(v, *then)
        return jnp.sum(v.astype(F32), axis=0)

    def handed(self, early, late):
        return lax.ppermute(early, "pipe", [(1, 0)]), lax.ppermute(late, "pipe", [(0, 1)])

    def to_owner(self, early, early_other, late, late_other):
        at_0 = jnp.concatenate([early, early_other], axis=0).astype(F32)
        at_1 = jnp.concatenate([late_other, late], axis=0).astype(F32)
        return jnp.where(self.core == 0, at_0, at_1)

    def wide_rows(self, v):
        return v.reshape(2, 16, 4, -1).transpose(0, 2, 1, 3).reshape(128, -1)

    def narrow_rows(self, v):
        return v.reshape(2, 4, 16, -1).transpose(0, 2, 1, 3).reshape(32, -1)


class AnyLinks(Links):
    split = False

    def gather_blocks(self, gains, inner, rest, wide, permute, clips, cotangent):
        full = [lax.all_gather(v, "dp", tiled=True) for v in (inner, wide, rest)]
        full[1] = jnp.stack([self.narrow_rows(f) for f in full[1].reshape(16, 128, -1)]).reshape(512, -1)
        own = jnp.concatenate(full, axis=1)
        vectors = [lax.all_gather(v, "dp", axis=1, tiled=True).astype(F32) for v in gains]
        mid = jnp.pad(jnp.concatenate(vectors[:4]), ((0, 4), (0, 0)))
        out = jnp.pad(jnp.concatenate(vectors[4:]), ((0, 6), (0, 0)))
        mids, outs = self.by_core(mid, self.swap(mid)), self.by_core(out, self.swap(out))
        blocks = []
        for s, full in enumerate(self.by_core(own, self.swap(own))):
            parts = full.reshape(16, 2, 16, -1)
            mine = lax.dynamic_index_in_dim(parts, self.core, 1, keepdims=False)
            theirs = lax.dynamic_index_in_dim(parts, 1 - self.core, 1, keepdims=False)
            refs = tuple(v.reshape(4, 2, 2, 16, -1) for v in (mine, theirs))
            groups = (("A", {"in": [("W", 0, 0, 2048)]}), ("B", middle_at(4096)), ("C", wide_at(2048)))
            blocks.append({k: (Weights("whole", v), refs) for k, v in groups})
            blocks[s]["gains"] = (mids[s], outs[s])
        return blocks, permute(clips), permute(cotangent)

    def gather_middle(self, blocks, pieces, then):
        return blocks

    def gather_last(self, blocks, third):
        return blocks

    def gains_of(self, group, place):
        return group

    def scatter_pairs(self, early, late, wide):
        full = []
        for keep, send in (early, late):
            half = self.add(keep, self.swap(send)).reshape(16, 16, -1)
            full.append(jnp.stack(self.by_core(half, self.swap(half)), axis=1))
        total = jnp.where(self.core == 0, full[0], full[1])
        if wide:
            total = jnp.stack([self.wide_rows(v.reshape(32, -1)) for v in total])
        total = total.reshape(-1, total.shape[-1])
        return lax.psum_scatter(total, "dp", scatter_dimension=0, tiled=True).astype(F32)


def after(v, *others):
    return lax.optimization_barrier((v, others))[0]


SPLIT_A = {"in": [("P", 0, 0, 1024), ("Q", 0, 1024, 1024)], "gain": [("Q", 1024, 0, 128)]}
SPLIT_C = {"out": [("P", 512 * g, (g,), 512) for g in range(4)]}
SPLIT_A1 = {"in": [("Q", 0, 0, 2048)], "gain": [("Q", 2048, 0, 128)]}


def middle_at(first):
    return {
        "sq": [("W", first, 0, 128)],
        "nf": [("W", first + 128, 0, 2304)],
        "mid": [("W", first + 2432, 0, 4608)],
    }


def wide_at(first):
    return {"out": [("W", first + 512 * g, (g,), 512) for g in range(4)]}


def local(
    clips_in, cotangent, segment_ids, w_in, w_squeeze, w_near, w_far, w_mid, w_out,
    gain_mid, bias_mid, gain_out, bias_out,
):
    dp = lax.axis_size("dp")
    core = lax.axis_index("pipe")
    links = (Links if dp == 16 else AnyLinks)(dp, core)
    place = links.place()
    rows_total = float(clips_in.shape[1] * dp)

    def low(v):
        return v[0].astype(BF16)

    n = w_in.shape[2]
    gain_rows = [low(gain_mid)[0:1], low(bias_mid)[0:1], low(gain_mid)[1:2], low(bias_mid)[1:2]]
    def permute(v):
        scratch = [pltpu.VMEM((3, SEG * PIX, 2048), BF16), buf(2048, BF16)]
        return call(permute_kernel, [pm(2048, BF16)], scratch)(place, v)[0]

    gathered, x0, dy = links.gather_blocks(
        gain_rows + [low(gain_out)[None], low(bias_out)[None]],
        low(w_in).T,
        jnp.concatenate([low(w_squeeze), low(w_near).T, low(w_far).T, low(w_mid).T], axis=1),
        low(w_out).T,
        permute, clips_in, cotangent,
    )

    def gains_of(s):
        return links.gains_of(gathered[s]["A" if links.split else "gains"], place)

    gains = [gains_of(0)]

    same = (segment_ids[:, 0, 1:] == segment_ids[:, 0, :-1]).astype(F32)
    same = jnp.concatenate([same, jnp.zeros((3, 1), F32)], axis=1)
    mine_seg = lax.dynamic_slice_in_dim(same, core * HALF, HALF, 1)
    msk = jnp.concatenate([mine_seg, jnp.zeros((3, 1), F32)], axis=1).reshape(15)
    msk = jnp.broadcast_to(jnp.concatenate([msk, jnp.zeros((1,), F32)])[:, None], (LINE, 128))


    wide_buf = pltpu.VMEM((4, 2, 2, 2, 4, 16, 512), BF16)

    stb = ((dp, 8, 384), F32)
    half_stat = ((8, 1024), F32)
    buffers = {"in": wbuf(2048), "sq": wbuf(128), "nf": wbuf(2304), "mid": wbuf(4608), "out": wide_buf}
    groups = {"A": ("in",), "B": ("sq", "nf", "mid"), "C": ("out",)}

    def kernel(body, group, values, outs, scratch, *static):
        wt, refs = group[1]
        names = groups[group[0]]
        refs = [Near2(v) if names == ("out",) and wt.kind == "split" else v for v in refs]
        return call(functools.partial(body, *static, wt), outs, [buffers[k] for k in names] + scratch)(
            place, *values, *refs
        )

    def group(s, k):
        return k, gathered[s][k]

    wide_sums = pltpu.VMEM((8, 2048), F32)
    lines = pltpu.VMEM((3, LINE, 2048), F32)
    padded = pltpu.VMEM((9, 9, LINE, 512), BF16)
    patch = pltpu.VMEM((SIDE, SIDE, LINE, 2304), BF16)

    def first(s, x):
        return kernel(first_kernel, group(s, "A"), [Near(x)], [near(512, F32), stb], [])

    def middle(s, a, other, *values):
        outs = [pm(512, F32), pm(512, BF16), pm(128, BF16), pm(512, BF16),
                ((9, 9, LINE, 512), BF16), near(512, F32), pm(512, F32), stb, STAT]
        scratch = [buf(512, F32), buf(512, BF16), buf(128, BF16), buf(512, BF16), padded, buf(512, F32), patch]
        return kernel(middle_kernel, group(s, "B"), [Near(a), Near(other), *values], outs, scratch)

    def widen(s, second, *values):
        outs = [pm(512, BF16), half_stat, half_stat, STAT]
        scratch = [buf(512, BF16), buf(512, F32), wide_sums]
        return kernel(wide_kernel, group(s, "C"), [Near(second), *values], outs, scratch)

    def turn(mid, *values):
        outs = [pm(2048, BF16)] * 3 + [near(512, F32), stb, WIDE_STAT]
        wide_wt, wide_refs = gathered[0]["C"]
        scratch = [buf(512, F32)] + [buf(2048, BF16)] * 4
        wt, refs = gathered[1]["A"]
        return call(
            functools.partial(turn_kernel, wide_wt, wt), outs, [wide_buf, buffers["in"]] + scratch
        )(place, Near(mid), *values, *[Near2(v) for v in wide_refs], *refs)

    def top(mid, *values):
        outs = [pm(2048, BF16)] * 2 + [near(2048, BF16), half_stat, half_stat, WIDE_STAT]
        wide_wt, wide_refs = gathered[1]["C"]
        scratch = [wide_buf, buf(512, F32)] + [buf(2048, BF16)] * 4 + [wide_sums]
        return call(functools.partial(top_kernel, wide_wt), outs, scratch)(
            place, Near(mid), *values, *wide_refs
        )

    def pairs(norm, keep, send, *meanwhile):
        recv = links.swap(send)
        v = pl.pallas_call(
            functools.partial(pair_kernel, norm), in_specs=[VM, VM], out_specs=VM,
            out_shape=jax.ShapeDtypeStruct((dp, 8, 768), F32),
            compiler_params=pltpu.CompilerParams(vmem_limit_bytes=8 * 1024 * 1024),
        )(keep, recv)
        return links.to_all(v, *meanwhile)

    def wide_back(s, dz, *values):
        outs = [near(512, F32), stb, pm(2048, BF16), WIDE_STAT]
        scratch = [buf(2048, BF16), buf(512, F32), buf(2048, BF16), lines]
        return kernel(wide_back_kernel, group(s, "C"), [Near(dz), *values], outs, scratch, rows_total)

    def second_back(sh, dn2, *values):
        outs = [near(512, BF16), STAT]
        scratch = [buf(512, F32)]
        if sh:
            outs, scratch = sh.outs() + outs, scratch + [padded] + sh.buffers()
        return call(functools.partial(second_back_kernel, rows_total, sh), outs, scratch)(
            place, Near(dn2), *values
        )

    def middle_back(s, d2, *values):
        outs = [near(512, F32), stb, near(512, BF16), near(128, BF16)]
        scratch = [padded, buf(512, F32), buf(512, BF16), buf(512, F32), pltpu.VMEM((SIDE, SIDE, LINE, 128), F32)]
        return kernel(middle_back_kernel, group(s, "B"), [Near(d2), *values], outs, scratch)

    def first_back(dn1, other, *values):
        outs = [pm(2048, BF16), near(512, BF16), STAT, near(2048, BF16), half_stat, half_stat]
        scratch = [buf(512, F32)] + [buf(2048, BF16)] * 4 + [wide_sums]
        return kernel(
            first_back_kernel, group(1, "A"), [Near(dn1), Near(other), *values], outs, scratch, rows_total
        )

    def last_grad(sh, dn1, other, *values):
        scratch = [buf(512, F32), buf(2048, BF16)] + sh.buffers()
        return call(
            functools.partial(last_grad_kernel, rows_total, sh), sh.outs() + [near(512, BF16), STAT], scratch
        )(place, Near(dn1), Near(other), *values)

    def last_back(d1, *values):
        scratch = [buf(2048, BF16), buf(2048, BF16)]
        return kernel(last_back_kernel, group(0, "A"), [Near(d1), *values], [pm(2048, BF16)], scratch)[0]

    def shares_of(kind, *parts):
        return Shares(kind if links.split else "whole", parts)

    def grad(body, sh, values, *scratch):
        bufs = [pltpu.VMEM(v.shape, v.dtype) for v in values if not isinstance(v, Near)]
        return call(
            functools.partial(body, sh), sh.outs(), bufs + list(scratch) + sh.buffers()
        )(place, *values)

    restore = call(
        restore_kernel, [((3, SEG * PIX, 2048), BF16)],
        [pltpu.VMEM((2, PIX, LINE, 2048), BF16), pltpu.VMEM((3, SEG * PIX, 2048), BF16)],
    )

    def crossed(early, late):
        return lax.ppermute(early, "pipe", [(1, 0)]), lax.ppermute(late, "pipe", [(0, 1)])

    kept = []
    x = x0
    if links.split:
        x = after(x, gathered[1][0])
    a, st = first(0, x)
    for s in range(2):
        gb, gbo = gains[s]
        if s == 0:
            pieces = links.gather_first(after(gathered[1][0], a), 2048) if links.split else ()
            sums = links.to_all(st, dy, *pieces, gb)
            gathered = links.gather_middle(gathered, pieces, sums[0])
        else:
            sums = links.to_all(st, gb)
        a, diff, sq, op, mix, second, second_far, st, mv1 = middle(s, a, links.swap(a), *sums, gb, msk)
        mid, keep, send, mv2 = widen(s, second, *links.to_all(st), gb)
        stats = pairs(True, keep, send)
        if s == 0:
            if links.split:
                gathered = (gathered[0], {"A": (Weights("split", SPLIT_A1), gathered[1][0])}, gathered[1])
                gains.append(gains_of(1))
            act0, xhat, slope0, a_next, st, mv3 = turn(mid, x, *stats, gbo)
            if links.split:
                gathered = links.gather_last((gathered[0], gathered[2]), a_next)
            else:
                gains.append(gains_of(1))
        else:
            act1, xhat, dz, keep, send, mv3 = top(mid, x, *stats, gbo, dy)
        kept.append((x, a, mv1, diff, sq, op, mix, second_far, mv2, mid, xhat, mv3))
        if s == 0:
            x, a = act0, a_next

    gb, gbo = gains[1]
    x, a, mv1, diff, sq, op, mix, second, mv2, mid, xhat, mv3 = kept[1]
    dn2, st, d3, s3 = wide_back(
        1, dz, xhat, mv3, *pairs(False, keep, send), gbo, second, mv2, gb
    )
    d2, s2 = second_back(None, dn2, second, mv2, *links.to_all(st), gb)
    dn1, st, dlog, dsq = middle_back(1, d2, a, mv1, gb, msk, op)
    g_rest = grad(
        all_grad_kernel, shares_of("whole", 2432, 4608, 2048),
        [Near(d2), Near(dlog), Near(dsq), d3, mid, mix, sq, diff], patch,
    )
    split = links.split
    sums = links.to_all(st, *g_rest)
    dn1_other = links.swap(dn1)
    dx1, d1_late, s1, dz, keep, send = first_back(
        dn1, dn1_other, a, mv1, *sums, gb, dz, slope0, kept[0][10]
    )
    meanwhile = []
    if split:
        recv = after(links.swap(after(g_rest[1], sums[1], dn1_other)), dx1)
        late = links.add(g_rest[0], recv).reshape(16, 16, -1)
        keep = after(keep, late)
        late = links.scatter_whole(late)
    norms_1 = (s1, s2, s3)
    x_late = x

    gb, gbo = gains[0]
    x, a, mv1, diff, sq, op, mix, second, mv2, mid, xhat, mv3 = kept[0]
    dn2, st, d3, s3 = wide_back(
        0, dz, xhat, mv3, *pairs(False, keep, send, *meanwhile), gbo, second, mv2, gb
    )
    g_mixed = grad(
        mixed_grad_kernel, shares_of("whole", 4096), [Near(d3), mid, Near(d1_late), x_late]
    )
    sums = links.to_all(st, *g_mixed)
    mixed_sums = sums
    *g_mid, d2, s2 = second_back(shares_of("split", 2048, 2560), dn2, second, mv2, *sums, gb, mix)
    dn1, st, dlog, dsq = middle_back(0, d2, a, mv1, gb, msk, op)
    if split:
        sent = links.scatter_first(g_mid)
        mixed = links.half_sums(g_mixed[0], after(g_mixed[1], mixed_sums[1]))
        dlog = after(dlog, mixed, *sent)
        mixed = links.scatter_whole(mixed)
    g_branch = grad(branch_grad_kernel, shares_of("whole", 2432), [Near(dlog), Near(dsq), sq, diff], patch)
    meanwhile = g_branch
    if split:
        rest_0 = [links.half_sums(*g_branch)]
    *g_in, d1, s1 = last_grad(
        shares_of("whole", 2048), dn1, links.swap(dn1), a, mv1, *links.to_all(st, *meanwhile), gb, x
    )
    norms_0 = (s1, s2, s3)
    if split:
        last = jnp.concatenate([links.half_sums(*g_in), *rest_0], axis=-1)
        dx0 = last_back(after(d1, last), dz)
        act0, act1, dx1 = after((act0, act1, dx1), last)
        early = links.scatter_xy(g_mid, sent, (d1, None))
        activations = restore(place, act0, act1, *crossed(act0, act1))[0]
        last = links.scatter_at_once(last, activations)
        input_grads = restore(place, after(dx0, last), dx1, *crossed(dx0, dx1))[0]
        mid_0, _ = links.scatter_z(early, (activations, input_grads))
        in_0, branch_0 = jnp.split(last, [2048], axis=-1)
        mixed = after(mixed, late, input_grads)
        out_0, in_1 = jnp.split(mixed, 2, axis=-1)
        branch_1, mid_1, out_1 = jnp.split(late, [2432, 7040], axis=-1)
        mid_other, late_other = links.handed(mid_0, late)
        branch_1o, mid_1o, out_1o = jnp.split(late_other, [2432, 7040], axis=-1)
        out_0o, in_1o = links.handed(out_0, in_1)
        in_0o, branch_0o = jnp.split(lax.ppermute(last, "pipe", [(1, 0)]), [2048], axis=-1)
        f_in = links.to_owner(in_0, in_0o, in_1, in_1o)
        f_branch = links.to_owner(branch_0, branch_0o, branch_1, branch_1o)
        f_mid = links.to_owner(mid_0, mid_other, mid_1, mid_1o)
        f_out = links.wide_rows(links.to_owner(out_0, out_0o, out_1, out_1o))
    else:
        activations = restore(place, act0, act1, *crossed(act0, act1))[0]
        dx0 = last_back(d1, dz)
        input_grads = restore(place, dx0, dx1, *crossed(dx0, dx1))[0]
        rest = [v[..., :2432] for v in g_rest], [v[..., 2432:7040] for v in g_rest], [v[..., 7040:] for v in g_rest]
        f_branch = links.scatter_pairs(g_branch, rest[0], False)
        f_mid = links.scatter_pairs(g_mid, rest[1], False)
        g_out, in_1 = [v[..., :2048] for v in g_mixed], [v[..., 2048:] for v in g_mixed]
        f_out = links.scatter_pairs(g_out, rest[2], True)
        f_in = links.scatter_pairs(g_in, in_1, False)

    grad_w_in = f_in.T[None]
    grad_w_squeeze = f_branch[:, :128][None]
    grad_w_near = f_branch[:, 128:1280].T[None]
    grad_w_far = f_branch[:, 1280:].T[None]
    grad_w_mid = f_mid.T[None]
    grad_w_out = f_out.T[None]

    s1, s2, s3 = [jnp.where(core == 0, e, l) for e, l in zip(norms_0, norms_1)]
    dp_index = lax.axis_index("dp")
    mid_sums = jnp.stack(
        [jnp.stack([s1[0:3].sum(0), s2[0:3].sum(0)]), jnp.stack([s1[4:7].sum(0), s2[4:7].sum(0)])]
    )
    mid_sums = lax.dynamic_slice_in_dim(mid_sums, dp_index * n, n, 2)
    out_sums = jnp.stack([s3[0:3].sum(0), s3[4:7].sum(0)])
    out_sums = lax.dynamic_slice_in_dim(out_sums, dp_index * 4 * n, 4 * n, 1)
    return (
        activations[None], input_grads[None], grad_w_in, grad_w_squeeze, grad_w_near, grad_w_far,
        grad_w_mid, grad_w_out, mid_sums[1][None], mid_sums[0][None], out_sums[1][None],
        out_sums[0][None],
    )


def solution(mesh):
    split = P("pipe", None, "dp")
    rows = P("pipe", "dp", None)
    vec = P("pipe", "dp")
    clips = P(None, "dp", None)
    weights = (split, rows, split, split, split, split, split, split, vec, vec)
    whole = P("pipe", None, "dp", None)
    return jax.shard_map(
        local,
        mesh=mesh,
        in_specs=(clips, clips, clips) + weights,
        out_specs=(whole, whole) + weights,
        check_vma=False,
    )
```

```python
import functools

import jax
import jax.numpy as jnp
from jax import lax
from jax.experimental import pallas as pl
from jax.experimental.pallas import tpu as pltpu
from jax.sharding import PartitionSpec as P

SEG = 8
SIDE = 7
PIX = SIDE * SIDE
HALF = SEG // 2
STRIDE = HALF + 1
LINE = 16
ROWS = PIX * LINE
EPS = 1e-05
F32 = jnp.float32
BF16 = jnp.bfloat16
VMEM_BYTES = 36 * 1024 * 1024


def dot(left, right):
    return lax.dot_general(left, right, (((1,), (0,)), ((), ())), preferred_element_type=F32)


def dot_nt(left, right):
    return lax.dot_general(left, right, (((1,), (1,)), ((), ())), preferred_element_type=F32)


def dot_tn(left, right):
    return lax.dot_general(left, right, (((0,), (0,)), ((), ())), preferred_element_type=F32)


def sigmoid(v):
    return 0.5 * jnp.tanh(0.5 * v) + 0.5


def line_of(width):
    return lax.broadcasted_iota(jnp.int32, (LINE, width), 0)


def own_lines(width):
    r = line_of(width)
    inside = (r < 4) | ((r >= 5) & (r < 9)) | ((r >= 10) & (r < 14))
    return inside.astype(F32)


def per_line(values):
    width = values.shape[1]
    r = line_of(width)
    return jnp.where(r < 5, values[0:1], jnp.where(r < 10, values[1:2], values[2:3]))


def per_batch(lines, count):
    r = line_of(lines.shape[1])
    pieces = []
    for b in range(3):
        keep = (r >= 5 * b) & (r < 5 * b + count)
        pieces.append(jnp.sum(jnp.where(keep, lines, 0.0), axis=0, keepdims=True))
    return pieces


def flat(v):
    return v.reshape(-1, v.shape[-1])


def chunks(body, init=0):
    return lax.fori_loop(0, SIDE, body, init)


def ref_stats(a_ref, first, width):
    lanes = pl.ds(first, width)

    def add(i, s):
        return s + jnp.sum(a_ref[pl.ds(i * SIDE, SIDE), :, lanes], axis=0)

    sums = per_batch(chunks(add, jnp.zeros((LINE, width), F32)), HALF)
    means = [s / (HALF * PIX) for s in sums]
    mean_lines = per_line(jnp.concatenate(means, axis=0))

    def add_sq(i, s):
        d = a_ref[pl.ds(i * SIDE, SIDE), :, lanes] - mean_lines[None]
        return s + jnp.sum(d * d, axis=0)

    sq = per_batch(chunks(add_sq, jnp.zeros((LINE, width), F32)), HALF)
    zero = jnp.zeros((1, width), F32)
    return jnp.concatenate(means + [zero] + sq + [zero], axis=0)


def pack(st):
    cut = st.shape[1] * 3 // 4
    rest = [
        jnp.concatenate([st[r : r + 1, cut:] for r in rows], axis=1)
        for rows in ((0, 1, 2), (4, 5, 6))
    ]
    return jnp.concatenate([st[0:3, :cut], st[4:7, :cut]] + rest, axis=0)


def unpack(p, group):
    third = p.shape[1] // 3
    row = p[6 + group : 7 + group]
    rest = jnp.concatenate([row[:, third * k : third * (k + 1)] for k in range(3)], axis=0)
    return jnp.concatenate([p[3 * group : 3 * group + 3], rest], axis=1)


def spread(st, out_ref):
    packed = pack(st)
    for k in range(out_ref.shape[0]):
        out_ref[k] = packed


def merge_norm(gs, rows_each):
    count = sum(g.shape[0] for g in gs)
    total = sum(jnp.sum(g[...], axis=0) for g in gs)
    mean = total / count
    off = 0.0
    for g in gs:
        d = g[...] - mean[None]
        off = off + jnp.sum(d * d, axis=0)
    var = (unpack(total, 1) + rows_each * unpack(off, 0)) / (rows_each * count)
    return eight(unpack(mean, 0), var)


def merge_sums(gs, rows_each):
    total = sum(jnp.sum(g[...], axis=0) for g in gs)
    return eight(unpack(total, 0), unpack(total, 1))


def eight(first, second):
    zero = jnp.zeros((1, first.shape[1]), F32)
    return jnp.concatenate([first, zero, second, zero], axis=0)


def merge_wide(merge, place, g, g_other, out_ref):
    core = place[0]
    rows_each = float(2 * HALF * PIX)
    half = out_ref.shape[1] // 2
    out_ref[:, pl.ds(pl.multiple_of(core * half, half), half)] = merge([g], rows_each)
    out_ref[:, pl.ds(pl.multiple_of((1 - core) * half, half), half)] = merge([g_other], rows_each)


def split_wide(place, st, keep_ref, send_ref):
    core = place[0]
    half = st.shape[1] // 2
    keep_ref[...] = st[:, pl.ds(pl.multiple_of(core * half, half), half)]
    send_ref[...] = st[:, pl.ds(pl.multiple_of((1 - core) * half, half), half)]


def pair_kernel(norm, keep, recv, out_ref):
    a, b = keep[...], recv[...]
    if norm:
        d = a[0:3] - b[0:3]
        mean = 0.5 * (a[0:3] + b[0:3])
        st = eight(mean, a[4:7] + b[4:7] + (HALF * PIX / 2.0) * d * d)
    else:
        st = a + b
    spread(st, out_ref)


OWN_ROWS = float(HALF * PIX)


def gains_kernel(wt, place, *rest):
    refs, (gb_ref, gbo_ref, buf, sems) = rest[: wt.count], rest[wt.count :]
    wait_all(wt.copies("gain", place, refs, buf, Moves(sems)))
    i = lax.broadcasted_iota(jnp.int32, (128, 512), 0)
    j = lax.broadcasted_iota(jnp.int32, (128, 512), 1)
    mid = jnp.zeros((16, 512), F32)
    for k in range(16):
        g = buf[k // 4, k // 2 % 2, k % 2, 0]
        hot = jnp.where((i < 32) & (j == 32 * k + i), 1.0, 0.0).astype(BF16)
        mid = mid + dot(g, hot)
        gbo_ref[:, 128 * k : 128 * k + 128] = g[4:12].astype(F32)
    gb_ref[...] = mid[0:8]


class Moves:
    def __init__(self, sems):
        self.sems, self.used, self.leaving = sems, 0, []

    def fetch(self, source, target):
        copy = pltpu.make_async_copy(source, target, self.sems.at[self.used])
        self.used += 1
        copy.start()
        return copy

    def store(self, source, target):
        self.leaving.append(self.fetch(source, target))

    def chunks_of(self, source, target):
        return [self.fetch(source.at[rows], target.at[rows]) for rows in CHUNKS]

    def tiles_of(self, source, target):
        return [self.fetch(source.at[:, :, lanes], target.at[:, :, lanes]) for lanes in TILES]

    def finish(self):
        wait_all(self.leaving)


CHUNKS = [pl.ds(SIDE * i, SIDE) for i in range(SIDE)]
TILES = [pl.ds(512 * j, 512) for j in range(4)]


def wait_all(copies):
    for c in copies:
        c.wait()


class Weights:
    def __init__(self, kind, segments):
        self.kind, self.segments = kind, segments

    @property
    def count(self):
        return 2 if self.kind == "whole" else 8

    def copies(self, name, place, refs, buf, moves):
        core, y, x = place[0], place[1], place[2]
        found = []
        for part, start, at, width in self.segments[name]:
            for side in range(2):
                c = core if side == 0 else 1 - core
                if self.kind == "whole":
                    pairs = [(refs[side], (ALL, ALL, ALL))]
                elif part == "P":
                    pairs = [(refs[4 * side], (ALL, y, ALL)), (refs[4 * side + 1], (ALL, 1 - y, ALL))]
                else:
                    pairs = [(refs[4 * side + 2], (ALL, ALL, x)), (refs[4 * side + 3], (ALL, ALL, 1 - x))]
                for ref, where in pairs:
                    source = ref.at[..., pl.ds(start, width)]
                    if isinstance(at, tuple):
                        target = buf.at[where + (c, at[0])]
                    else:
                        target = buf.at[where + (c, ALL, pl.ds(at, width))]
                    found.append(moves.fetch(source, target))
        return found


ALL = slice(None)


def first_matmul(x_buf, w_buf, a_ref, stb_ref):
    for j in range(2):
        w = w_buf[2 * j : 2 * j + 2].reshape(256, 2048)
        a_ref[:, :, pl.ds(256 * j, 256)] = dot_nt(flat(x_buf[...]), w).reshape(PIX, LINE, 256)
    spread(ref_stats(a_ref, 0, 512), stb_ref)


def permute_kernel(core_ref, x_ref, out_ref, x_buf, buf, sems):
    moves = Moves(sems)
    loads = moves.tiles_of(x_ref, x_buf)
    core = core_ref[0]
    i = lax.broadcasted_iota(jnp.int32, (ROWS, SEG * PIX), 0)
    j = lax.broadcasted_iota(jnp.int32, (ROWS, SEG * PIX), 1)
    pixel, line = i >> 4, i & 15
    hots = []
    for b in range(3):
        t = line - 5 * b
        target = (HALF * core + t) * PIX + pixel
        hots.append(jnp.where((t >= 0) & (t < HALF) & (j == target), 1.0, 0.0).astype(BF16))
    for load, lanes in zip(loads, TILES):
        load.wait()
        total = dot(hots[0], x_buf[0, :, lanes])
        total = total + dot(hots[1], x_buf[1, :, lanes])
        total = total + dot(hots[2], x_buf[2, :, lanes])
        buf[:, :, lanes] = total.astype(BF16).reshape(PIX, LINE, 512)
        moves.store(buf.at[:, :, lanes], out_ref.at[:, :, lanes])
    moves.finish()


def restore_kernel(place, early_ref, late_ref, early_in, late_in, out_ref, buf, out_buf, sems):
    core = place[0]

    def copies(mine, received):
        found = []
        for k, lanes in enumerate(TILES):
            for n, (v, side) in enumerate(((mine, core), (received, 1 - core))):
                found.append(
                    pltpu.make_async_copy(
                        v.at[:, :, lanes], buf.at[side, :, :, lanes], sems.at[2 * k + n]
                    )
                )
        return found

    @pl.when(core == 0)
    def _():
        for c in copies(early_ref, early_in):
            c.start()

    @pl.when(core == 1)
    def _():
        for c in copies(late_ref, late_in):
            c.start()

    def hot(first, count, side, b):
        j = lax.broadcasted_iota(jnp.int32, (count, ROWS), 0) + first
        i = lax.broadcasted_iota(jnp.int32, (count, ROWS), 1)
        seg = jnp.zeros_like(j)
        for k in range(1, SEG):
            seg = seg + jnp.where(j >= PIX * k, 1, 0)
        t = seg - HALF * side
        target = (j - PIX * seg) * LINE + 5 * b + t
        return jnp.where((t >= 0) & (t < HALF) & (i == target), 1.0, 0.0).astype(BF16)

    hots = [(hot(0, 208, 0, b), hot(192, 200, 1, b)) for b in range(3)]
    loads = copies(early_ref, early_in)
    leaving = []
    for k, lanes in enumerate(TILES):
        wait_all(loads[2 * k : 2 * k + 2])
        for b, (lower, upper) in enumerate(hots):
            low = dot(lower, flat(buf[0, :, :, lanes])).astype(BF16)
            high = dot(upper, flat(buf[1, :, :, lanes])).astype(BF16)
            out_buf[b, 0:192, lanes] = low[:192]
            out_buf[b, 192:208, lanes] = low[192:] + high[:16]
            out_buf[b, 208:392, lanes] = high[16:]
        copy = pltpu.make_async_copy(out_buf.at[:, :, lanes], out_ref.at[:, :, lanes], sems.at[8 + k])
        copy.start()
        leaving.append(copy)
    wait_all(leaving)


def first_kernel(wt, place, x_ref, *rest):
    refs, (a_ref, stb_ref, w_buf, sems) = rest[: wt.count], rest[wt.count :]
    wait_all(wt.copies("in", place, refs, w_buf, Moves(sems)))
    first_matmul(x_ref, w_buf, a_ref, stb_ref)


def tap_ranges(shift):
    return max(0, -shift), min(SIDE, SIDE - shift)


def build_patches(sq, patch):
    patch[...] = jnp.zeros(patch.shape, BF16)
    sq4 = sq.reshape(SIDE, SIDE, LINE, 128)
    for k in (1, 2):
        for tap in range(9):
            dy, dx = k * (tap // 3 - 1), k * (tap % 3 - 1)
            (y0, y1), (x0, x1) = tap_ranges(dy), tap_ranges(dx)
            col = ((k - 1) * 9 + tap) * 128
            patch[y0:y1, x0:x1, :, col : col + 128] = sq4[y0 + dy : y1 + dy, x0 + dx : x1 + dx]


def clear_border(pad):
    zero_row = jnp.zeros((9, LINE, 512), BF16)
    pad[0] = zero_row
    pad[8] = zero_row
    for y in range(1, 8):
        pad[y, 0] = jnp.zeros((LINE, 512), BF16)
        pad[y, 8] = jnp.zeros((LINE, 512), BF16)


def middle_kernel(wt, place, a_in, a_other, g, g_other, gb_ref, msk_ref, *rest):
    refs = rest[: wt.count]
    (
        a_ref, diff_ref, sq_ref, op_ref, mix_ref, second, second_ref, st_ref, mv_ref,
        sq_buf, nf_buf, mid_buf, a_buf, diff, sq_out, op, mixp, hid, patch, sems,
    ) = rest[wt.count :]
    core = place[0]
    moves = Moves(sems)
    sq_copies = wt.copies("sq", place, refs, sq_buf, moves)
    nf_copies = wt.copies("nf", place, refs, nf_buf, moves)
    mid_copies = wt.copies("mid", place, refs, mid_buf, moves)
    clear_border(mixp)
    mv_ref[...] = merge_norm([g, g_other], OWN_ROWS)
    r = line_of(512)
    halo = ((r == 4) | (r == 9) | (r == 14)) & (core == 0)
    mean = per_line(mv_ref[0:3])
    scale = lax.rsqrt(per_line(mv_ref[4:7]) + EPS) * gb_ref[0:1]
    shift = gb_ref[1:2]
    m = msk_ref[:, 0:1]
    for rows in CHUNKS:
        a = jnp.where(halo[None], pltpu.roll(a_other[rows], 4, 1), a_in[rows])
        a_buf[rows] = a
        n1 = (a - mean[None]) * scale[None] + shift[None]
        h = n1 * sigmoid(n1)
        hid[rows] = h
        diff[rows] = (m[None] * (pltpu.roll(h, LINE - 1, 1) - h)).astype(BF16)
    moves.store(a_buf, a_ref)
    moves.store(diff, diff_ref)
    wait_all(sq_copies)
    sq = dot(flat(diff[...]), sq_buf[...].reshape(512, 128)).astype(BF16)
    sq_out[...] = sq.reshape(PIX, LINE, 128)
    moves.store(sq_out, sq_ref)
    build_patches(sq, patch)
    wait_all(nf_copies)
    for j in range(2):
        lanes = pl.ds(256 * j, 256)
        w = nf_buf[2 * j : 2 * j + 2].reshape(256, 2304)
        logits = dot_nt(patch[...].reshape(ROWS, 2304), w).reshape(PIX, LINE, 256)
        opening = sigmoid(logits)
        op[:, :, lanes] = opening.astype(BF16)
        mixed = (hid[:, :, lanes] * (0.5 + opening)).astype(BF16)
        mixp[1:8, 1:8, :, lanes] = mixed.reshape(SIDE, SIDE, LINE, 256)
    moves.store(op, op_ref)
    moves.store(mixp, mix_ref)
    wait_all(mid_copies)

    total = 0.0
    for k in range(9):
        v = mixp[k // 3 : k // 3 + SIDE, k % 3 : k % 3 + SIDE].reshape(ROWS, 512)
        total = total + dot_nt(v, mid_buf[..., pl.ds(512 * k, 512)].reshape(512, 512))
    second[...] = total.reshape(PIX, LINE, 512)
    moves.store(second, second_ref)
    spread(ref_stats(second, 0, 512), st_ref)
    moves.finish()


def wide_kernel(wt, place, second, g, g_other, gb_ref, *rest):
    refs = rest[: wt.count]
    mid_ref, keep_ref, send_ref, mv_ref, buf, mid, third, st_ref, sems = rest[wt.count :]
    moves = Moves(sems)
    copies = wt.copies("out", place, refs, buf, moves)
    mv_ref[...] = merge_norm([g, g_other], OWN_ROWS)
    mean = per_line(mv_ref[0:3])
    scale = lax.rsqrt(per_line(mv_ref[4:7]) + EPS) * gb_ref[2:3]
    shift = gb_ref[3:4]
    for rows in CHUNKS:
        n2 = (second[rows] - mean[None]) * scale[None] + shift[None]
        mid[rows] = (n2 * sigmoid(n2)).astype(BF16)
    moves.store(mid, mid_ref)
    wait_all(copies)
    for j, lanes in enumerate(TILES):
        w = buf[j].reshape(512, 512)
        third[...] = dot_nt(flat(mid[...]), w).reshape(PIX, LINE, 512)
        st_ref[:, lanes] = ref_stats(third, 0, 512)
    split_wide(place, st_ref, keep_ref, send_ref)
    moves.finish()


def finish(mid, wide_buf, third, x_buf, loads, mv_ref, gb_ref, each, after_tile):
    for j, lanes in enumerate(TILES):
        third[...] = dot_nt(flat(mid[...]), wide_buf[j].reshape(512, 512)).reshape(PIX, LINE, 512)
        wait_all([load[j] for load in loads])
        mean = per_line(mv_ref[0:3, lanes])
        inv = lax.rsqrt(per_line(mv_ref[4:7, lanes]) + EPS)
        gain, bias = gb_ref[0:1, lanes], gb_ref[1:2, lanes]

        def chunk(i, carry):
            rows = pl.ds(i * SIDE, SIDE)
            xhat = (third[rows] - mean[None]) * inv[None]
            z = x_buf[rows, :, lanes].astype(F32) + xhat * gain[None] + bias[None]
            sg = sigmoid(z)
            return each(rows, lanes, xhat, z * sg, sg, carry)

        zero = jnp.zeros((LINE, 512), F32)
        after_tile(lanes, chunks(chunk, (zero, zero)))


def sums_of(dh, dg):
    zero = jnp.zeros((1, dh.shape[1]), F32)
    return jnp.concatenate(per_batch(dh, STRIDE) + [zero] + per_batch(dg, STRIDE) + [zero], axis=0)


def turn_kernel(wide_wt, wt, place, mid, x_ref, g, g_other, gb_ref, *rest):
    wide_refs, rest = rest[: wide_wt.count], rest[wide_wt.count :]
    refs = rest[: wt.count]
    (
        act_ref, xhat_ref, slope_ref, a_ref, st_ref, mv_ref,
        wide_buf, w_buf, third, x_buf, act, xhat_buf, slope, sems,
    ) = rest[wt.count :]
    moves = Moves(sems)
    wide_copies = wide_wt.copies("out", place, wide_refs, wide_buf, moves)
    loads = [moves.tiles_of(x_ref, x_buf)]
    copies = wt.copies("in", place, refs, w_buf, moves)
    merge_wide(merge_norm, place, g, g_other, mv_ref)

    def each(rows, lanes, xhat, y, sg, carry):
        act[rows, :, lanes] = y.astype(BF16)
        xhat_buf[rows, :, lanes] = xhat.astype(BF16)
        slope[rows, :, lanes] = (sg + y * (1.0 - sg)).astype(BF16)
        return carry

    def after_tile(lanes, _):
        for buf, ref in ((act, act_ref), (xhat_buf, xhat_ref), (slope, slope_ref)):
            moves.store(buf.at[:, :, lanes], ref.at[:, :, lanes])

    wait_all(wide_copies)
    finish(mid, wide_buf, third, x_buf, loads, mv_ref, gb_ref, each, after_tile)
    wait_all(copies)
    first_matmul(act, w_buf, a_ref, st_ref)
    moves.finish()


def top_kernel(
    wide_wt, place, mid, x_ref, g, g_other, gb_ref, dy_ref, *rest,
):
    wide_refs, rest = rest[: wide_wt.count], rest[wide_wt.count :]
    (
        act_ref, xhat_ref, dz, keep_ref, send_ref, mv_ref,
        wide_buf, third, x_buf, dy, act, xhat_buf, sums_ref, sems,
    ) = rest
    moves = Moves(sems)
    wide_copies = wide_wt.copies("out", place, wide_refs, wide_buf, moves)
    loads = [moves.tiles_of(r, b) for r, b in ((x_ref, x_buf), (dy_ref, dy))]
    merge_wide(merge_norm, place, g, g_other, mv_ref)

    def each(rows, lanes, xhat, y, sg, carry):
        act[rows, :, lanes] = y.astype(BF16)
        xhat_buf[rows, :, lanes] = xhat.astype(BF16)
        d = dy[rows, :, lanes].astype(F32) * (sg + y * (1.0 - sg))
        dz[rows, :, lanes] = d.astype(BF16)
        return carry[0] + jnp.sum(d, axis=0), carry[1] + jnp.sum(d * xhat, axis=0)

    def after_tile(lanes, carry):
        for buf, ref in ((act, act_ref), (xhat_buf, xhat_ref)):
            moves.store(buf.at[:, :, lanes], ref.at[:, :, lanes])
        sums_ref[:, lanes] = sums_of(*carry)

    wait_all(wide_copies)
    finish(mid, wide_buf, third, x_buf, loads, mv_ref, gb_ref, each, after_tile)
    split_wide(place, sums_ref, keep_ref, send_ref)
    moves.finish()


class Shares:
    def __init__(self, kind, parts):
        self.kind, self.parts = kind, parts

    @property
    def count(self):
        return 2 if self.kind == "whole" else 4 * sum(1 for width in self.parts if width)

    def outs(self):
        if self.kind == "whole":
            width = sum(self.parts)
            return [((4, 2, 2, 16, width), BF16)] * 2
        return [((4, 2, 16, width), BF16) for width in self.parts if width for _ in range(4)]

    def buffers(self):
        return [pltpu.VMEM(shape, dtype) for shape, dtype in self.outs()]

    def store(self, place, out, first, result, zs=ALL):
        refs, bufs, moves = out

        def put(ref, buf, v, lanes):
            buf[zs, ..., lanes] = v
            moves.store(buf.at[zs, ..., lanes], ref.at[zs, ..., lanes])

        core, y, x = place[0], place[1], place[2]
        width = result.shape[1]
        parts = result.astype(BF16).reshape(-1, 2, 2, 2, 16, width)
        lower, upper = parts[:, :, :, 0], parts[:, :, :, 1]
        sides = [jnp.where(core == 0, lower, upper), jnp.where(core == 0, upper, lower)]
        if self.kind == "whole":
            for ref, buf, v in zip(refs, bufs, sides):
                put(ref, buf, v, pl.ds(first, width))
            return
        is_p = first < self.parts[0]
        start = first if is_p else first - self.parts[0]
        lanes = pl.ds(start, width)
        refs = refs[:4] if is_p else refs[-4:]
        bufs = bufs[:4] if is_p else bufs[-4:]
        for k, v in enumerate(sides):
            if is_p:
                two, at = (v[:, 0], v[:, 1]), y
            else:
                two, at = (v[:, :, 0], v[:, :, 1]), x
            put(refs[2 * k], bufs[2 * k], jnp.where(at == 0, two[0], two[1]), lanes)
            put(refs[2 * k + 1], bufs[2 * k + 1], jnp.where(at == 0, two[1], two[0]), lanes)


def wide_back_kernel(
    rows_total, wt, place, dz, xhat_ref, mv3_ref, g, g_other, gbo_ref, second_ref, mv2_ref, gb_ref, *rest
):
    refs = rest[: wt.count]
    dn2, stb_ref, d3_ref, s3_ref, buf, xhat, second, d3, lines, sems = rest[wt.count :]
    moves = Moves(sems)
    loads = moves.chunks_of(xhat_ref, xhat)
    copies = wt.copies("out", place, refs, buf, moves)
    second_load = moves.fetch(second_ref, second)
    merge_wide(merge_sums, place, g, g_other, s3_ref)
    own = own_lines(512)
    for lanes in TILES:
        lines[0, :, lanes] = lax.rsqrt(per_line(mv3_ref[4:7, lanes]) + EPS) * gbo_ref[0:1, lanes] * own
        lines[1, :, lanes] = per_line(s3_ref[0:3, lanes]) / rows_total
        lines[2, :, lanes] = per_line(s3_ref[4:7, lanes]) / rows_total
    for load, rows in zip(loads, CHUNKS):
        load.wait()
        for lanes in TILES:
            v = dz[rows, :, lanes].astype(F32) - lines[1, :, lanes][None]
            v = v - xhat[rows, :, lanes].astype(F32) * lines[2, :, lanes][None]
            d3[rows, :, lanes] = (lines[0, :, lanes][None] * v).astype(BF16)
    moves.store(d3, d3_ref)
    wait_all(copies)
    for j, lanes in enumerate(TILES):
        part = dot(flat(d3[:, :, lanes]), buf[j].reshape(512, 512)).reshape(PIX, LINE, 512)
        dn2[...] = part if j == 0 else dn2[...] + part
    second_load.wait()
    mean = per_line(mv2_ref[0:3])
    inv = lax.rsqrt(per_line(mv2_ref[4:7]) + EPS)
    gain, bias = gb_ref[2:3], gb_ref[3:4]

    def chunk(i, carry):
        rows = pl.ds(i * SIDE, SIDE)
        xh = (second[rows] - mean[None]) * inv[None]
        n2 = xh * gain[None] + bias[None]
        sg = sigmoid(n2)
        dn = dn2[rows] * (sg * (1.0 + n2 * (1.0 - sg)))
        dn2[rows] = dn
        return carry[0] + jnp.sum(dn, axis=0), carry[1] + jnp.sum(dn * xh, axis=0)

    zero = jnp.zeros((LINE, 512), F32)
    spread(sums_of(*chunks(chunk, (zero, zero))), stb_ref)
    moves.finish()


def wide_grad(sh, place, refs, start, d3, mid):
    for j in range(4):
        v = flat(d3[:, :, pl.ds(512 * j, 512)])
        res = dot_tn(v, flat(mid[...])).reshape(2, 2, 2, 4, 16, 512)
        for g in range(4):
            sh.store(place, refs, start + 512 * g, res[:, :, :, g].reshape(128, 512), slice(j, j + 1))


def middle_grad(sh, place, refs, start, d2, mixp):
    for tap in range(9):
        mixed = mixp[tap // 3 : tap // 3 + SIDE, tap % 3 : tap % 3 + SIDE].reshape(ROWS, 512)
        sh.store(place, refs, start + 512 * tap, dot_tn(flat(d2[...]), mixed))


def branch_grad(sh, place, refs, start, dlog, sq_ref, diff, dsq, patch):
    build_patches(flat(sq_ref[...]), patch)
    for j in range(3):
        pv = patch[:, :, :, pl.ds(768 * j, 768)].reshape(ROWS, 768)
        sh.store(place, refs, start + 128 + 768 * j, dot_tn(flat(dlog[...]), pv))
    sh.store(place, refs, start, dot_tn(flat(diff[...]), flat(dsq[...])))


def fetch_all(moves, refs, bufs):
    return [moves.fetch(r, b) for r, b in zip(refs, bufs)]


def branch_grad_kernel(sh, place, dlog, dsq, sq_ref, diff_ref, *rest):
    refs, (sq, diff, patch), bufs = rest[: sh.count], rest[sh.count : -1 - sh.count], rest[-1 - sh.count : -1]
    moves = Moves(rest[-1])
    wait_all(fetch_all(moves, (sq_ref, diff_ref), (sq, diff)))
    branch_grad(sh, place, (refs, bufs, moves), 0, dlog, sq, diff, dsq, patch)
    moves.finish()


def all_grad_kernel(sh, place, d2, dlog, dsq, d3_ref, mid_ref, mix_ref, sq_ref, diff_ref, *rest):
    refs, (d3, mid, mixp, sq, diff, patch) = rest[: sh.count], rest[sh.count : -1 - sh.count]
    bufs, moves = rest[-1 - sh.count : -1], Moves(rest[-1])
    out = (refs, bufs, moves)
    mix_load = moves.fetch(mix_ref, mixp)
    loads = fetch_all(moves, (sq_ref, diff_ref, d3_ref, mid_ref), (sq, diff, d3, mid))
    mix_load.wait()
    middle_grad(sh, place, out, 2432, d2, mixp)
    wait_all(loads)
    wide_grad(sh, place, out, 7040, d3, mid)
    branch_grad(sh, place, out, 0, dlog, sq, diff, dsq, patch)
    moves.finish()


def mixed_grad_kernel(sh, place, d3, mid_ref, d1, x_ref, *rest):
    refs, (mid, x), bufs = rest[: sh.count], rest[sh.count : -1 - sh.count], rest[-1 - sh.count : -1]
    moves = Moves(rest[-1])
    wait_all(fetch_all(moves, (mid_ref, x_ref), (mid, x)))
    wide_grad(sh, place, (refs, bufs, moves), 0, d3, mid)
    first_grad(sh, place, (refs, bufs, moves), 2048, d1, x)
    moves.finish()


def second_back_kernel(rows_total, sh, place, dn2, second_ref, mv2_ref, g, g_other, gb_ref, *rest):
    if sh is not None:
        mix_ref, refs, rest = rest[0], rest[1 : 1 + sh.count], rest[1 + sh.count :]
        d2, s2_ref, second, mixp, *bufs, sems = rest
    else:
        d2, s2_ref, second, sems = rest
    moves = Moves(sems)
    second_loads = moves.chunks_of(second_ref, second)
    if sh is not None:
        mix_load = moves.fetch(mix_ref, mixp)
    s2_ref[...] = merge_sums([g, g_other], OWN_ROWS)
    own = own_lines(512)
    mean2 = per_line(mv2_ref[0:3])
    inv2 = lax.rsqrt(per_line(mv2_ref[4:7]) + EPS)
    k2 = inv2 * gb_ref[2:3] * own
    dh2 = per_line(s2_ref[0:3]) / rows_total
    dg2 = per_line(s2_ref[4:7]) / rows_total
    for i, rows in enumerate(CHUNKS):
        second_loads[i].wait()
        xh = (second[rows] - mean2[None]) * inv2[None]
        d2[rows] = (k2[None] * (dn2[rows] - dh2[None] - xh * dg2[None])).astype(BF16)
    if sh is not None:
        mix_load.wait()
        middle_grad(sh, place, (refs, bufs, moves), 0, d2, mixp)
    moves.finish()


def middle_back_kernel(wt, place, d2, a_ref, mv1_ref, gb_ref, msk_ref, op_ref, *rest):
    refs = rest[: wt.count]
    (
        dn1, stb_ref, dlog, dsq_out,
        sq_buf, nf_buf, mid_buf, d2p, a, op, dmix, dsq, sems,
    ) = rest[wt.count :]
    moves = Moves(sems)
    mid_copies = wt.copies("mid", place, refs, mid_buf, moves)
    late_loads = [moves.fetch(a_ref, a), moves.fetch(op_ref, op)]
    nf_copies = wt.copies("nf", place, refs, nf_buf, moves)
    sq_copies = wt.copies("sq", place, refs, sq_buf, moves)
    clear_border(d2p)
    for i, rows in enumerate(CHUNKS):
        d2p[i + 1, 1:8] = d2[rows]

    total = 0.0
    for k in range(9):
        wait_all(mid_copies[2 * k : 2 * k + 2])
        y, x = 2 - k // 3, 2 - k % 3
        v = d2p[y : y + SIDE, x : x + SIDE].reshape(ROWS, 512)
        total = total + dot(v, mid_buf[..., pl.ds(512 * k, 512)].reshape(512, 512))
    dmix[...] = total.reshape(PIX, LINE, 512)
    wait_all(late_loads)
    mean1 = per_line(mv1_ref[0:3])
    inv1 = lax.rsqrt(per_line(mv1_ref[4:7]) + EPS)
    gain1, bias1 = gb_ref[0:1], gb_ref[1:2]

    def log_chunk(i, c):
        rows = pl.ds(i * SIDE, SIDE)
        n1 = (a[rows] - mean1[None]) * inv1[None] * gain1[None] + bias1[None]
        h = n1 * sigmoid(n1)
        o = op[rows].astype(F32)
        dlog[rows] = (dmix[rows] * h * o * (1.0 - o)).astype(BF16)
        return c

    chunks(log_chunk)
    wait_all(nf_copies)
    dsq[...] = jnp.zeros(dsq.shape, F32)
    for k in (1, 2):
        for ty in range(3):
            w = nf_buf[..., pl.ds(((k - 1) * 9 + ty * 3) * 128, 384)].reshape(512, 384)
            res = dot(flat(dlog[...]), w).reshape(SIDE, SIDE, LINE, 384)
            for tx in range(3):
                dy, dx = k * (ty - 1), k * (tx - 1)
                (y0, y1), (x0, x1) = tap_ranges(dy), tap_ranges(dx)
                dsq[y0 + dy : y1 + dy, x0 + dx : x1 + dx] += res[
                    y0:y1, x0:x1, :, 128 * tx : 128 * tx + 128
                ]
    dsq_low = dsq[...].astype(BF16).reshape(ROWS, 128)
    dsq_out[...] = dsq_low.reshape(PIX, LINE, 128)
    wait_all(sq_copies)
    dn1[...] = dot_nt(dsq_low, sq_buf[...].reshape(512, 128)).reshape(PIX, LINE, 512)
    m = msk_ref[:, 0:1]

    def last_chunk(i, carry):
        rows = pl.ds(i * SIDE, SIDE)
        xh = (a[rows] - mean1[None]) * inv1[None]
        n1 = xh * gain1[None] + bias1[None]
        sg = sigmoid(n1)
        e = dn1[rows] * m[None]
        o = op[rows].astype(F32)
        dhid = dmix[rows] * (0.5 + o) - e + pltpu.roll(e, 1, 1)
        dn = dhid * (sg * (1.0 + n1 * (1.0 - sg)))
        dn1[rows] = dn
        return carry[0] + jnp.sum(dn, axis=0), carry[1] + jnp.sum(dn * xh, axis=0)

    zero = jnp.zeros((LINE, 512), F32)
    spread(sums_of(*chunks(last_chunk, (zero, zero))), stb_ref)


def first_d1(rows_total, place, loads, dn1, dn1_other, a, mv1_ref, s1_ref, gb_ref, d1):
    own = own_lines(512)
    r = line_of(512)
    first = ((r == 0) | (r == 5) | (r == 10)) & (place[0] == 1)
    mean = per_line(mv1_ref[0:3])
    inv = lax.rsqrt(per_line(mv1_ref[4:7]) + EPS)
    k = inv * gb_ref[0:1] * own
    dh = per_line(s1_ref[0:3]) / rows_total
    dg = per_line(s1_ref[4:7]) / rows_total
    for i, rows in enumerate(CHUNKS):
        loads[i].wait()
        xh = (a[rows] - mean[None]) * inv[None]
        dn = dn1[rows] + jnp.where(first[None], pltpu.roll(dn1_other[rows], LINE - 4, 1), 0.0)
        d1[rows] = (k[None] * (dn - dh[None] - xh * dg[None])).astype(BF16)


def first_back_kernel(
    rows_total, wt, place, dn1, other, a_ref, mv1_ref, g, g_other, gb_ref, dz_ref, slope_ref, xhat_ref, *rest
):
    refs = rest[: wt.count]
    (
        dx_ref, d1, s1_ref, below, keep_ref, send_ref,
        w_buf, a, dz, slope, xhat, dx, sums_ref, sems,
    ) = rest[wt.count :]
    moves = Moves(sems)
    loads = moves.chunks_of(a_ref, a)
    copies = wt.copies("in", place, refs, w_buf, moves)
    tiles = [moves.tiles_of(r, b) for r, b in ((dz_ref, dz), (slope_ref, slope), (xhat_ref, xhat))]
    s1_ref[...] = merge_sums([g, g_other], OWN_ROWS)
    first_d1(rows_total, place, loads, dn1, other, a, mv1_ref, s1_ref, gb_ref, d1)
    wait_all(copies)
    for j, lanes in enumerate(TILES):
        wait_all([load[j] for load in tiles])
        w = w_buf[..., lanes].reshape(512, 512)
        v = dot(flat(d1[...]), w).reshape(PIX, LINE, 512) + dz[:, :, lanes].astype(F32)
        low = v.astype(BF16)
        dx[:, :, lanes] = low
        d = low.astype(F32) * slope[:, :, lanes].astype(F32)
        below[:, :, lanes] = d.astype(BF16)
        moves.store(dx.at[:, :, lanes], dx_ref.at[:, :, lanes])
        sums_ref[:, lanes] = sums_of(
            jnp.sum(d, axis=0), jnp.sum(d * xhat[:, :, lanes].astype(F32), axis=0)
        )
    split_wide(place, sums_ref, keep_ref, send_ref)
    moves.finish()


def first_grad(sh, place, out, start, d1, x_ref):
    for j in range(4):
        x = flat(x_ref[:, :, pl.ds(512 * j, 512)])
        sh.store(place, out, start + 512 * j, dot_tn(flat(d1[...]), x))


def last_grad_kernel(rows_total, sh, place, dn1, other, a_ref, mv1_ref, g, g_other, gb_ref, x_ref, *rest):
    refs, rest = rest[: sh.count], rest[sh.count :]
    d1, s1_ref, a, x, *bufs, sems = rest
    moves = Moves(sems)
    loads = moves.chunks_of(a_ref, a)
    x_load = moves.fetch(x_ref, x)
    s1_ref[...] = merge_sums([g, g_other], OWN_ROWS)
    first_d1(rows_total, place, loads, dn1, other, a, mv1_ref, s1_ref, gb_ref, d1)
    x_load.wait()
    first_grad(sh, place, (refs, bufs, moves), 0, d1, x)
    moves.finish()


def last_back_kernel(wt, place, d1, dz_ref, *rest):
    refs, (dx_ref, w_buf, dz, dx, sems) = rest[: wt.count], rest[wt.count :]
    moves = Moves(sems)
    copies = wt.copies("in", place, refs, w_buf, moves)
    loads = moves.tiles_of(dz_ref, dz)
    wait_all(copies)
    for j, lanes in enumerate(TILES):
        loads[j].wait()
        w = w_buf[..., lanes].reshape(512, 512)
        v = dot(flat(d1[...]), w).reshape(PIX, LINE, 512) + dz[:, :, lanes].astype(F32)
        dx[:, :, lanes] = v.astype(BF16)
        moves.store(dx.at[:, :, lanes], dx_ref.at[:, :, lanes])
    moves.finish()


VM = pl.BlockSpec(memory_space=pltpu.VMEM)
HB = pl.BlockSpec(memory_space=pltpu.HBM)
SM = pl.BlockSpec(memory_space=pltpu.SMEM)
AN = pl.BlockSpec(memory_space=pl.ANY)


class Near:
    def __init__(self, value):
        self.value = value


class Near2(Near):
    pass


def is_big(shape):
    return len(shape) >= 4 or (len(shape) == 3 and shape[0] in (PIX, 3))


def size_of(shape, dtype):
    size = jnp.dtype(dtype).itemsize
    for k in shape:
        size *= k
    return size


def call(kernel, outs, scratch=(), us=5):
    def run(place, *values):
        specs = [SM]
        need = 6 * 1024 * 1024
        need += sum(size_of(v.shape, v.dtype) for v in scratch)
        need += sum(size_of(*o[:2]) for o in outs if not (is_big(o[0]) and len(o) == 2))
        for v in values:
            u = v.value if isinstance(v, Near) else v
            if not is_big(u.shape) or (isinstance(v, Near) and not isinstance(v, Near2)):
                need += size_of(u.shape, u.dtype)
        for v in values:
            if isinstance(v, Near):
                specs.append(AN if isinstance(v, Near2) else VM)
            else:
                specs.append(HB if is_big(v.shape) else VM)
        return pl.pallas_call(
            kernel,
            in_specs=specs,
            out_specs=tuple(HB if is_big(o[0]) and len(o) == 2 else VM for o in outs),
            out_shape=tuple(jax.ShapeDtypeStruct(o[0], o[1]) for o in outs),
            scratch_shapes=list(scratch) + [pltpu.SemaphoreType.DMA((96,))],
            compiler_params=pltpu.CompilerParams(vmem_limit_bytes=52 * 1024 * 1024),
            cost_estimate=pl.CostEstimate(flops=us * 10**9, bytes_accessed=us * 3 * 10**6, transcendentals=0),
        )(place, *[v.value if isinstance(v, Near) else v for v in values])

    return run


def near(width, dtype):
    return ((PIX, LINE, width), dtype, True)


def pm(width, dtype):
    return ((PIX, LINE, width), dtype)


def buf(width, dtype):
    return pltpu.VMEM((PIX, LINE, width), dtype)


def wbuf(width):
    return pltpu.VMEM((4, 2, 2, 2, 16, width), BF16)


STAT = ((8, 512), F32)
WIDE_STAT = ((8, 2048), F32)
PAIR = [(0, 1), (1, 0)]


class Links:
    def __init__(self, dp, core):
        self.dp, self.core = dp, core
        self.at = lax.axis_index("dp")

    def bit(self, k):
        return (self.at // k) % 2

    def place(self):
        y, x = (self.bit(2), self.bit(1)) if self.split else (0, 0)
        return jnp.stack([self.core, jnp.int32(y), jnp.int32(x)]).astype(jnp.int32)

    split = True

    def swap(self, v):
        return lax.ppermute(v, "pipe", PAIR)

    def across(self, v, k):
        return lax.ppermute(v, "dp", [(i, i ^ k) for i in range(self.dp)])

    def to_all(self, spread, *meanwhile):
        g = lax.all_to_all(spread, "dp", 0, 0)
        if meanwhile:
            g = after(g, *meanwhile)
        return g, self.swap(g)

    def by_core(self, own, other):
        first = self.core == 0
        return jnp.where(first, own, other), jnp.where(first, other, own)

    def in_order(self, which, own, other, axis):
        pair = jnp.where(which == 0, jnp.stack([own, other], axis), jnp.stack([other, own], axis))
        return pair

    def halves(self, piece):
        two = piece.reshape(2, 16, piece.shape[1])
        keep = lax.dynamic_index_in_dim(two, self.core, 0, keepdims=False)
        recv = self.swap(lax.dynamic_index_in_dim(two, 1 - self.core, 0, keepdims=False))
        return self.by_core(keep, recv)

    def gather_first(self, v, cut):
        p, q = v[..., :cut], v[..., cut:]
        p_other, q_other = self.across(p, 1), self.across(q, 2)
        return self.in_order(self.bit(1), p, p_other, 1), self.in_order(self.bit(2), q, q_other, 1)

    def gather_second(self, p, q):
        mine = (p, self.across(p, 2), q, self.across(q, 1))
        return mine + tuple(self.swap(v) for v in mine)

    def gather_whole(self, own):
        return lax.all_gather(own, "dp").reshape(4, 2, 2, 16, -1)

    def gather_blocks(self, gains, inner, rest, wide, permute, clips, cotangent):
        rows = jnp.concatenate([jnp.pad(v, ((0, 0), (0, 128 - v.shape[1]))) for v in gains], axis=0)
        tail = jnp.pad(rows, ((0, 32 - rows.shape[0]), (0, 0)))
        a = self.halves(jnp.concatenate([inner, tail], axis=1))
        b, c = self.halves(rest), self.halves(self.narrow_rows(wide))
        b0 = self.gather_whole(b[0])
        v = after(a[0], b[0])
        v = self.in_order(self.bit(8), v, self.across(v, 8), 0)
        x = permute(after(clips, v, b[0]))
        moved = after(self.across(v, 4), x)
        v = self.in_order(self.bit(4), v, moved, 1).reshape(4, 16, -1)
        ca = jnp.concatenate([c[0], a[1]], axis=1)
        ca = self.in_order(self.bit(8), ca, self.across(after(ca, v), 8), 0)
        dy = permute(after(cotangent, v))
        moved = after(self.across(ca, 4), dy)
        ca = self.in_order(self.bit(4), ca, moved, 1).reshape(4, 16, -1)
        a0 = self.gather_second(*self.gather_first(v, 1024))
        block_0 = {"A": (Weights("split", SPLIT_A), a0)}
        return (block_0, (ca, b0, jnp.concatenate([c[1], b[1]], axis=1))), x, dy

    def gather_middle(self, blocks, pieces, then):
        block_0, (_, b0, bc) = blocks
        ca = self.gather_second(*pieces)
        block_0["C"] = (Weights("split", SPLIT_C), ca)
        b0 = after(b0, then)
        block_0["B"] = (Weights("whole", middle_at(0)), (b0, self.swap(b0)))
        return block_0, (ca, self.gather_whole(after(bc, b0)))

    def gather_last(self, blocks, third):
        block_0, (ca, bc) = blocks
        bc = after(bc, third)
        bc = (bc, self.swap(bc))
        return block_0, {
            "A": (Weights("split", SPLIT_A1), ca),
            "B": (Weights("whole", middle_at(2048)), bc),
            "C": (Weights("whole", wide_at(0)), bc),
        }

    def gains_of(self, group, place):
        wt, refs = group
        return call(functools.partial(gains_kernel, wt), [STAT, WIDE_STAT], [wbuf(128)])(place, *refs)

    def add(self, a, b):
        return (a.astype(F32) + b.astype(F32)).astype(BF16)

    def halve(self, v, axis, k, then=None):
        which = self.bit(k)
        keep = lax.dynamic_index_in_dim(v, which, axis, keepdims=False)
        send = lax.dynamic_index_in_dim(v, 1 - which, axis, keepdims=False)
        moved = self.across(send, k)
        if then is not None:
            moved = after(moved, then)
        return self.add(keep, moved)

    def scatter_first(self, g):
        return [self.add(g[k], self.swap(g[k + 2])) for k in (1, 5)]

    def scatter_xy(self, g, sent, then=(None, None)):
        done = []
        for own, send_own, other, k in ((g[0], g[2], sent[0], 2), (g[4], g[6], sent[1], 1)):
            moved = self.across(other, k)
            if then[0] is not None:
                moved = after(moved, then[0])
            v = self.add(self.add(own, self.swap(send_own)), moved)
            done.append(self.halve(v, 1, 3 - k, then[1]))
        return jnp.concatenate(done, axis=-1)

    def scatter_z(self, v, then=(None, None)):
        half = self.halve(v.reshape(2, 2, 16, -1), 1, 4, then[0])
        return self.halve(half, 0, 8, then[1]), half

    def half_sums(self, keep, send):
        return self.add(keep, self.swap(send)).reshape(16, 16, -1)

    def scatter_whole(self, v):
        return lax.psum_scatter(v, "dp", scatter_dimension=0, tiled=True)[0]

    def scatter_at_once(self, v, *then):
        v = lax.all_to_all(v, "dp", 0, 0)
        if then:
            v = after(v, *then)
        return jnp.sum(v.astype(F32), axis=0)

    def handed(self, early, late):
        return lax.ppermute(early, "pipe", [(1, 0)]), lax.ppermute(late, "pipe", [(0, 1)])

    def to_owner(self, early, early_other, late, late_other):
        at_0 = jnp.concatenate([early, early_other], axis=0).astype(F32)
        at_1 = jnp.concatenate([late_other, late], axis=0).astype(F32)
        return jnp.where(self.core == 0, at_0, at_1)

    def wide_rows(self, v):
        return v.reshape(2, 16, 4, -1).transpose(0, 2, 1, 3).reshape(128, -1)

    def narrow_rows(self, v):
        return v.reshape(2, 4, 16, -1).transpose(0, 2, 1, 3).reshape(32, -1)


class AnyLinks(Links):
    split = False

    def gather_blocks(self, gains, inner, rest, wide, permute, clips, cotangent):
        full = [lax.all_gather(v, "dp", tiled=True) for v in (inner, wide, rest)]
        full[1] = jnp.stack([self.narrow_rows(f) for f in full[1].reshape(16, 128, -1)]).reshape(512, -1)
        own = jnp.concatenate(full, axis=1)
        vectors = [lax.all_gather(v, "dp", axis=1, tiled=True).astype(F32) for v in gains]
        mid = jnp.pad(jnp.concatenate(vectors[:4]), ((0, 4), (0, 0)))
        out = jnp.pad(jnp.concatenate(vectors[4:]), ((0, 6), (0, 0)))
        mids, outs = self.by_core(mid, self.swap(mid)), self.by_core(out, self.swap(out))
        blocks = []
        for s, full in enumerate(self.by_core(own, self.swap(own))):
            parts = full.reshape(16, 2, 16, -1)
            mine = lax.dynamic_index_in_dim(parts, self.core, 1, keepdims=False)
            theirs = lax.dynamic_index_in_dim(parts, 1 - self.core, 1, keepdims=False)
            refs = tuple(v.reshape(4, 2, 2, 16, -1) for v in (mine, theirs))
            groups = (("A", {"in": [("W", 0, 0, 2048)]}), ("B", middle_at(4096)), ("C", wide_at(2048)))
            blocks.append({k: (Weights("whole", v), refs) for k, v in groups})
            blocks[s]["gains"] = (mids[s], outs[s])
        return blocks, permute(clips), permute(cotangent)

    def gather_middle(self, blocks, pieces, then):
        return blocks

    def gather_last(self, blocks, third):
        return blocks

    def gains_of(self, group, place):
        return group

    def scatter_pairs(self, early, late, wide):
        full = []
        for keep, send in (early, late):
            half = self.add(keep, self.swap(send)).reshape(16, 16, -1)
            full.append(jnp.stack(self.by_core(half, self.swap(half)), axis=1))
        total = jnp.where(self.core == 0, full[0], full[1])
        if wide:
            total = jnp.stack([self.wide_rows(v.reshape(32, -1)) for v in total])
        total = total.reshape(-1, total.shape[-1])
        return lax.psum_scatter(total, "dp", scatter_dimension=0, tiled=True).astype(F32)


def after(v, *others):
    return lax.optimization_barrier((v, others))[0]


SPLIT_A = {"in": [("P", 0, 0, 1024), ("Q", 0, 1024, 1024)], "gain": [("Q", 1024, 0, 128)]}
SPLIT_C = {"out": [("P", 512 * g, (g,), 512) for g in range(4)]}
SPLIT_A1 = {"in": [("Q", 0, 0, 2048)], "gain": [("Q", 2048, 0, 128)]}


def middle_at(first):
    return {
        "sq": [("W", first, 0, 128)],
        "nf": [("W", first + 128, 0, 2304)],
        "mid": [("W", first + 2432 + 512 * k, 512 * k, 512) for k in range(9)],
    }


def wide_at(first):
    return {"out": [("W", first + 512 * g, (g,), 512) for g in range(4)]}


def local(
    clips_in, cotangent, segment_ids, w_in, w_squeeze, w_near, w_far, w_mid, w_out,
    gain_mid, bias_mid, gain_out, bias_out,
):
    dp = lax.axis_size("dp")
    core = lax.axis_index("pipe")
    links = (Links if dp == 16 else AnyLinks)(dp, core)
    place = links.place()
    rows_total = float(clips_in.shape[1] * dp)

    def low(v):
        return v[0].astype(BF16)

    n = w_in.shape[2]
    gain_rows = [low(gain_mid)[0:1], low(bias_mid)[0:1], low(gain_mid)[1:2], low(bias_mid)[1:2]]
    def permute(v):
        scratch = [pltpu.VMEM((3, SEG * PIX, 2048), BF16), buf(2048, BF16)]
        return call(permute_kernel, [pm(2048, BF16)], scratch)(place, v)[0]

    gathered, x0, dy = links.gather_blocks(
        gain_rows + [low(gain_out)[None], low(bias_out)[None]],
        low(w_in).T,
        jnp.concatenate([low(w_squeeze), low(w_near).T, low(w_far).T, low(w_mid).T], axis=1),
        low(w_out).T,
        permute, clips_in, cotangent,
    )

    def gains_of(s):
        return links.gains_of(gathered[s]["A" if links.split else "gains"], place)

    gains = [gains_of(0)]

    same = (segment_ids[:, 0, 1:] == segment_ids[:, 0, :-1]).astype(F32)
    same = jnp.concatenate([same, jnp.zeros((3, 1), F32)], axis=1)
    mine_seg = lax.dynamic_slice_in_dim(same, core * HALF, HALF, 1)
    msk = jnp.concatenate([mine_seg, jnp.zeros((3, 1), F32)], axis=1).reshape(15)
    msk = jnp.broadcast_to(jnp.concatenate([msk, jnp.zeros((1,), F32)])[:, None], (LINE, 128))


    wide_buf = pltpu.VMEM((4, 2, 2, 2, 4, 16, 512), BF16)

    stb = ((dp, 8, 384), F32)
    half_stat = ((8, 1024), F32)
    buffers = {"in": wbuf(2048), "sq": wbuf(128), "nf": wbuf(2304), "mid": wbuf(4608), "out": wide_buf}
    groups = {"A": ("in",), "B": ("sq", "nf", "mid"), "C": ("out",)}

    def kernel(body, group, values, outs, scratch, *static):
        wt, refs = group[1]
        names = groups[group[0]]
        refs = [Near2(v) if names == ("out",) and wt.kind == "split" else v for v in refs]
        return call(functools.partial(body, *static, wt), outs, [buffers[k] for k in names] + scratch)(
            place, *values, *refs
        )

    def group(s, k):
        return k, gathered[s][k]

    wide_sums = pltpu.VMEM((8, 2048), F32)
    lines = pltpu.VMEM((3, LINE, 2048), F32)
    padded = pltpu.VMEM((9, 9, LINE, 512), BF16)
    patch = pltpu.VMEM((SIDE, SIDE, LINE, 2304), BF16)

    def first(s, x):
        return kernel(first_kernel, group(s, "A"), [Near(x)], [near(512, F32), stb], [])

    def middle(s, a, other, *values):
        outs = [pm(512, F32), pm(512, BF16), pm(128, BF16), pm(512, BF16),
                ((9, 9, LINE, 512), BF16), near(512, F32), pm(512, F32), stb, STAT]
        scratch = [buf(512, F32), buf(512, BF16), buf(128, BF16), buf(512, BF16), padded, buf(512, F32), patch]
        return kernel(middle_kernel, group(s, "B"), [Near(a), Near(other), *values], outs, scratch)

    def widen(s, second, *values):
        outs = [pm(512, BF16), half_stat, half_stat, STAT]
        scratch = [buf(512, BF16), buf(512, F32), wide_sums]
        return kernel(wide_kernel, group(s, "C"), [Near(second), *values], outs, scratch)

    def turn(mid, *values):
        outs = [pm(2048, BF16)] * 3 + [near(512, F32), stb, WIDE_STAT]
        wide_wt, wide_refs = gathered[0]["C"]
        scratch = [buf(512, F32)] + [buf(2048, BF16)] * 4
        wt, refs = gathered[1]["A"]
        return call(
            functools.partial(turn_kernel, wide_wt, wt), outs, [wide_buf, buffers["in"]] + scratch
        )(place, Near(mid), *values, *[Near2(v) for v in wide_refs], *refs)

    def top(mid, *values):
        outs = [pm(2048, BF16)] * 2 + [near(2048, BF16), half_stat, half_stat, WIDE_STAT]
        wide_wt, wide_refs = gathered[1]["C"]
        scratch = [wide_buf, buf(512, F32)] + [buf(2048, BF16)] * 4 + [wide_sums]
        return call(functools.partial(top_kernel, wide_wt), outs, scratch)(
            place, Near(mid), *values, *wide_refs
        )

    def pairs(norm, keep, send, *meanwhile):
        recv = links.swap(send)
        v = pl.pallas_call(
            functools.partial(pair_kernel, norm), in_specs=[VM, VM], out_specs=VM,
            out_shape=jax.ShapeDtypeStruct((dp, 8, 768), F32),
            compiler_params=pltpu.CompilerParams(vmem_limit_bytes=8 * 1024 * 1024),
        )(keep, recv)
        return links.to_all(v, *meanwhile)

    def wide_back(s, dz, *values):
        outs = [near(512, F32), stb, pm(2048, BF16), WIDE_STAT]
        scratch = [buf(2048, BF16), buf(512, F32), buf(2048, BF16), lines]
        return kernel(wide_back_kernel, group(s, "C"), [Near(dz), *values], outs, scratch, rows_total)

    def second_back(sh, dn2, *values):
        outs = [near(512, BF16), STAT]
        scratch = [buf(512, F32)]
        if sh:
            outs, scratch = sh.outs() + outs, scratch + [padded] + sh.buffers()
        return call(functools.partial(second_back_kernel, rows_total, sh), outs, scratch)(
            place, Near(dn2), *values
        )

    def middle_back(s, d2, *values):
        outs = [near(512, F32), stb, near(512, BF16), near(128, BF16)]
        scratch = [padded, buf(512, F32), buf(512, BF16), buf(512, F32), pltpu.VMEM((SIDE, SIDE, LINE, 128), F32)]
        return kernel(middle_back_kernel, group(s, "B"), [Near(d2), *values], outs, scratch)

    def first_back(dn1, other, *values):
        outs = [pm(2048, BF16), near(512, BF16), STAT, near(2048, BF16), half_stat, half_stat]
        scratch = [buf(512, F32)] + [buf(2048, BF16)] * 4 + [wide_sums]
        return kernel(
            first_back_kernel, group(1, "A"), [Near(dn1), Near(other), *values], outs, scratch, rows_total
        )

    def last_grad(sh, dn1, other, *values):
        scratch = [buf(512, F32), buf(2048, BF16)] + sh.buffers()
        return call(
            functools.partial(last_grad_kernel, rows_total, sh), sh.outs() + [near(512, BF16), STAT], scratch
        )(place, Near(dn1), Near(other), *values)

    def last_back(d1, *values):
        scratch = [buf(2048, BF16), buf(2048, BF16)]
        return kernel(last_back_kernel, group(0, "A"), [Near(d1), *values], [pm(2048, BF16)], scratch)[0]

    def shares_of(kind, *parts):
        return Shares(kind if links.split else "whole", parts)

    def grad(body, sh, values, *scratch):
        bufs = [pltpu.VMEM(v.shape, v.dtype) for v in values if not isinstance(v, Near)]
        return call(
            functools.partial(body, sh), sh.outs(), bufs + list(scratch) + sh.buffers()
        )(place, *values)

    restore = call(
        restore_kernel, [((3, SEG * PIX, 2048), BF16)],
        [pltpu.VMEM((2, PIX, LINE, 2048), BF16), pltpu.VMEM((3, SEG * PIX, 2048), BF16)],
    )

    def crossed(early, late):
        return lax.ppermute(early, "pipe", [(1, 0)]), lax.ppermute(late, "pipe", [(0, 1)])

    kept = []
    x = x0
    if links.split:
        x = after(x, gathered[1][0])
    a, st = first(0, x)
    for s in range(2):
        gb, gbo = gains[s]
        if s == 0:
            pieces = links.gather_first(after(gathered[1][0], a), 2048) if links.split else ()
            sums = links.to_all(st, dy, *pieces, gb)
            gathered = links.gather_middle(gathered, pieces, sums[0])
        else:
            sums = links.to_all(st, gb)
        a, diff, sq, op, mix, second, second_far, st, mv1 = middle(s, a, links.swap(a), *sums, gb, msk)
        mid, keep, send, mv2 = widen(s, second, *links.to_all(st), gb)
        stats = pairs(True, keep, send)
        if s == 0:
            if links.split:
                gathered = (gathered[0], {"A": (Weights("split", SPLIT_A1), gathered[1][0])}, gathered[1])
                gains.append(gains_of(1))
            act0, xhat, slope0, a_next, st, mv3 = turn(mid, x, *stats, gbo)
            if links.split:
                gathered = links.gather_last((gathered[0], gathered[2]), a_next)
            else:
                gains.append(gains_of(1))
        else:
            act1, xhat, dz, keep, send, mv3 = top(mid, x, *stats, gbo, dy)
        kept.append((x, a, mv1, diff, sq, op, mix, second_far, mv2, mid, xhat, mv3))
        if s == 0:
            x, a = act0, a_next

    gb, gbo = gains[1]
    x, a, mv1, diff, sq, op, mix, second, mv2, mid, xhat, mv3 = kept[1]
    dn2, st, d3, s3 = wide_back(
        1, dz, xhat, mv3, *pairs(False, keep, send), gbo, second, mv2, gb
    )
    d2, s2 = second_back(None, dn2, second, mv2, *links.to_all(st), gb)
    dn1, st, dlog, dsq = middle_back(1, d2, a, mv1, gb, msk, op)
    g_rest = grad(
        all_grad_kernel, shares_of("whole", 2432, 4608, 2048),
        [Near(d2), Near(dlog), Near(dsq), d3, mid, mix, sq, diff], patch,
    )
    split = links.split
    sums = links.to_all(st, *g_rest)
    dn1_other = links.swap(dn1)
    dx1, d1_late, s1, dz, keep, send = first_back(
        dn1, dn1_other, a, mv1, *sums, gb, dz, slope0, kept[0][10]
    )
    meanwhile = []
    if split:
        recv = after(links.swap(after(g_rest[1], sums[1], dn1_other)), dx1)
        late = links.add(g_rest[0], recv).reshape(16, 16, -1)
        keep = after(keep, late)
        late = links.scatter_whole(late)
    norms_1 = (s1, s2, s3)
    x_late = x

    gb, gbo = gains[0]
    x, a, mv1, diff, sq, op, mix, second, mv2, mid, xhat, mv3 = kept[0]
    dn2, st, d3, s3 = wide_back(
        0, dz, xhat, mv3, *pairs(False, keep, send, *meanwhile), gbo, second, mv2, gb
    )
    g_mixed = grad(
        mixed_grad_kernel, shares_of("whole", 4096), [Near(d3), mid, Near(d1_late), x_late]
    )
    sums = links.to_all(st, *g_mixed)
    mixed_sums = sums
    *g_mid, d2, s2 = second_back(shares_of("split", 2048, 2560), dn2, second, mv2, *sums, gb, mix)
    dn1, st, dlog, dsq = middle_back(0, d2, a, mv1, gb, msk, op)
    if split:
        sent = links.scatter_first(g_mid)
        mixed = links.half_sums(g_mixed[0], after(g_mixed[1], mixed_sums[1]))
        dlog = after(dlog, mixed, *sent)
        mixed = links.scatter_whole(mixed)
    g_branch = grad(branch_grad_kernel, shares_of("whole", 2432), [Near(dlog), Near(dsq), sq, diff], patch)
    meanwhile = g_branch
    if split:
        rest_0 = [links.half_sums(*g_branch)]
    *g_in, d1, s1 = last_grad(
        shares_of("whole", 2048), dn1, links.swap(dn1), a, mv1, *links.to_all(st, *meanwhile), gb, x
    )
    norms_0 = (s1, s2, s3)
    if split:
        last = jnp.concatenate([links.half_sums(*g_in), *rest_0], axis=-1)
        dx0 = last_back(after(d1, last), dz)
        act0, act1, dx1 = after((act0, act1, dx1), last)
        early = links.scatter_xy(g_mid, sent, (d1, None))
        activations = restore(place, act0, act1, *crossed(act0, act1))[0]
        last = links.scatter_at_once(last, activations)
        input_grads = restore(place, after(dx0, last), dx1, *crossed(dx0, dx1))[0]
        mid_0, _ = links.scatter_z(early, (activations, input_grads))
        in_0, branch_0 = jnp.split(last, [2048], axis=-1)
        mixed = after(mixed, late, input_grads)
        out_0, in_1 = jnp.split(mixed, 2, axis=-1)
        branch_1, mid_1, out_1 = jnp.split(late, [2432, 7040], axis=-1)
        mid_other, late_other = links.handed(mid_0, late)
        branch_1o, mid_1o, out_1o = jnp.split(late_other, [2432, 7040], axis=-1)
        out_0o, in_1o = links.handed(out_0, in_1)
        in_0o, branch_0o = jnp.split(lax.ppermute(last, "pipe", [(1, 0)]), [2048], axis=-1)
        f_in = links.to_owner(in_0, in_0o, in_1, in_1o)
        f_branch = links.to_owner(branch_0, branch_0o, branch_1, branch_1o)
        f_mid = links.to_owner(mid_0, mid_other, mid_1, mid_1o)
        f_out = links.wide_rows(links.to_owner(out_0, out_0o, out_1, out_1o))
    else:
        activations = restore(place, act0, act1, *crossed(act0, act1))[0]
        dx0 = last_back(d1, dz)
        input_grads = restore(place, dx0, dx1, *crossed(dx0, dx1))[0]
        rest = [v[..., :2432] for v in g_rest], [v[..., 2432:7040] for v in g_rest], [v[..., 7040:] for v in g_rest]
        f_branch = links.scatter_pairs(g_branch, rest[0], False)
        f_mid = links.scatter_pairs(g_mid, rest[1], False)
        g_out, in_1 = [v[..., :2048] for v in g_mixed], [v[..., 2048:] for v in g_mixed]
        f_out = links.scatter_pairs(g_out, rest[2], True)
        f_in = links.scatter_pairs(g_in, in_1, False)

    grad_w_in = f_in.T[None]
    grad_w_squeeze = f_branch[:, :128][None]
    grad_w_near = f_branch[:, 128:1280].T[None]
    grad_w_far = f_branch[:, 1280:].T[None]
    grad_w_mid = f_mid.T[None]
    grad_w_out = f_out.T[None]

    s1, s2, s3 = [jnp.where(core == 0, e, l) for e, l in zip(norms_0, norms_1)]
    dp_index = lax.axis_index("dp")
    mid_sums = jnp.stack(
        [jnp.stack([s1[0:3].sum(0), s2[0:3].sum(0)]), jnp.stack([s1[4:7].sum(0), s2[4:7].sum(0)])]
    )
    mid_sums = lax.dynamic_slice_in_dim(mid_sums, dp_index * n, n, 2)
    out_sums = jnp.stack([s3[0:3].sum(0), s3[4:7].sum(0)])
    out_sums = lax.dynamic_slice_in_dim(out_sums, dp_index * 4 * n, 4 * n, 1)
    return (
        activations[None], input_grads[None], grad_w_in, grad_w_squeeze, grad_w_near, grad_w_far,
        grad_w_mid, grad_w_out, mid_sums[1][None], mid_sums[0][None], out_sums[1][None],
        out_sums[0][None],
    )


def solution(mesh):
    split = P("pipe", None, "dp")
    rows = P("pipe", "dp", None)
    vec = P("pipe", "dp")
    clips = P(None, "dp", None)
    weights = (split, rows, split, split, split, split, split, split, vec, vec)
    whole = P("pipe", None, "dp", None)
    return jax.shard_map(
        local,
        mesh=mesh,
        in_specs=(clips, clips, clips) + weights,
        out_specs=(whole, whole) + weights,
        check_vma=False,
    )
```
